32 devices in a mesh: dp: 4 (over z), feat: 8 (over y, x, core).
Axes of the slice: x: 2, y: 2, z: 4, core: 2. Of those that a mesh axis runs over, the one named last changes fastest.
Arguments:
- z_anchor: bfloat16 [2048, 8192], P('dp', 'feat'), may hold values from -54 to 54
- z_other: bfloat16 [2048, 8192], P('dp', 'feat'), may hold values from -54 to 54
Outputs:
- scaled_grad: float32 [2048, 8192], P('dp', 'feat')
The draws below stay inside these ranges and needn't reach their ends.
All inputs are finite; a program needn't handle non-finite values.
Results may differ from the reference program's by a relative error of at most 0.0035.
Values may be sent and summed in bfloat16 or wider, within the bound.
No kernel may reach another device: no remote copies, remote signals or barrier semaphores. Data moves between devices by JAX's collectives and lax.ppermute only.
A program may use at most 128 MiB of HBM per device.

```python
import math
import jax
import jax.numpy as jnp
from jax import lax

FEAT = 8192
TOK_DEV = 512
TOKENS = 2048
N_DP = 4


def common_part(key, strength):
    k_factor, k_load = jax.random.split(key)
    factor = jnp.clip(jax.random.normal(k_factor, (8, TOKENS), jnp.float32), -3.0, 3.0)
    loading = jnp.clip(jax.random.normal(k_load, (8, FEAT), jnp.float32), -2.0, 2.0)
    summed = jnp.zeros((TOKENS, FEAT), jnp.float32)
    for which in range(8):
        summed = summed + factor[which][:, None] * loading[which][None, :]
    return strength * summed


def column_scales(key):
    k_band, k_low, k_high = jax.random.split(key, 3)
    band = jax.random.randint(k_band, (FEAT,), 0, 2)
    low_log = jax.random.uniform(k_low, (FEAT,), jnp.float32, math.log(0.25), math.log(0.6))
    high_log = jax.random.uniform(k_high, (FEAT,), jnp.float32, math.log(1.6), math.log(4.0))
    return jnp.exp(jnp.where(band == 1, high_log, low_log))


def row_scales():
    position = jnp.arange(TOKENS).astype(jnp.float32) / TOKENS
    return jnp.exp(math.log(10.0) * position) / 4.6365


def normal_field(key, mean_scale):
    k_cols, k_base, k_mean, k_common = jax.random.split(key, 4)
    column = column_scales(k_cols)
    base = jnp.clip(jax.random.normal(k_base, (TOKENS, FEAT), jnp.float32), -5.5, 5.5)
    offset = mean_scale * jnp.clip(jax.random.normal(k_mean, (FEAT,), jnp.float32), -3.0, 3.0)
    spread = base * row_scales()[:, None] * column[None, :]
    return offset[None, :] + spread + common_part(k_common, 0.07)


def draw_z_anchor(key, part):
    key = jax.random.fold_in(key, 11)
    field = normal_field(key, 0.5)
    return field.astype(jnp.bfloat16)


def draw_z_other(key, part):
    key = jax.random.fold_in(key, 23)
    field = normal_field(key, 0.5)
    return field.astype(jnp.bfloat16)


def setup_inputs(seed: int = 0) -> dict:
    seeds = jax.random.split(jax.random.key(seed), 3)
    z_anchor = draw_z_anchor(jax.random.fold_in(seeds[2], 71), 0)
    z_other = draw_z_other(jax.random.fold_in(seeds[2], 71), 0)
    return {"z_anchor": z_anchor, "z_other": z_other}


def reference(z_anchor, z_other):
    anchor = z_anchor.astype(jnp.float32)
    mean = lax.optimization_barrier(jnp.sum(anchor, axis=0)) / TOKENS
    centered = anchor - mean
    variance = lax.optimization_barrier(jnp.sum(centered * centered, axis=0)) / (TOKENS - 1)
    deviation = jnp.sqrt(variance + 0.0001)
    rounded = centered.astype(jnp.bfloat16)
    widened = rounded.astype(jnp.float32)
    cov = jnp.zeros((FEAT, FEAT), jnp.float32)
    for group in range(N_DP):
        piece = widened[group * TOK_DEV:(group + 1) * TOK_DEV]
        partial_value = jnp.dot(piece.T, piece, precision=lax.Precision.HIGHEST, preferred_element_type=jnp.float32)
        partial_value = lax.optimization_barrier(partial_value.astype(jnp.bfloat16))
        cov = cov + partial_value.astype(jnp.float32)
    cov = cov / (TOKENS - 1)
    coef = 2.0 * TOKENS / (25.0 * (TOKENS - 1))
    index = jnp.arange(FEAT)
    weights = jnp.where(index[:, None] == index[None, :], 0.0, coef * cov).astype(jnp.bfloat16)
    update = jnp.dot(widened, weights.astype(jnp.float32), precision=lax.Precision.HIGHEST, preferred_element_type=jnp.float32)
    hinge = jnp.where(deviation < 1.0, centered / deviation, 0.0)
    factor = TOKENS / (4.0 * (TOKENS - 1))
    return anchor - z_other.astype(jnp.float32) - factor * hinge + update
```

```python
import jax
import jax.numpy as jnp
from jax import lax
from jax.sharding import PartitionSpec as P


def per_device(z_anchor, z_other):
    rows_here, width = z_anchor.shape
    groups = lax.axis_size("dp")
    total = rows_here * groups
    mine = lax.axis_index("dp") * rows_here
    column = lax.all_gather(z_anchor, "dp", axis=0, tiled=True).astype(jnp.float32)
    mean = jnp.sum(column, axis=0) / total
    centered_all = column - mean
    variance = jnp.sum(centered_all * centered_all, axis=0) / (total - 1)
    deviation = jnp.sqrt(variance + 0.0001)
    rounded_all = centered_all.astype(jnp.bfloat16)
    widened = rounded_all.astype(jnp.float32)
    own_square = jnp.sum(widened * widened, axis=0)
    rounded = lax.dynamic_slice_in_dim(rounded_all, mine, rows_here, 0)
    part = lax.dot_general(
        rounded, rounded_all, (((1,), (1,)), ((), ())), preferred_element_type=jnp.float32
    )
    inner = lax.psum(part.astype(jnp.bfloat16), "feat")
    product = jnp.dot(inner, rounded_all, preferred_element_type=jnp.float32)
    coef = 2.0 * total / (25.0 * (total - 1)) / (total - 1)
    update = coef * (product - rounded.astype(jnp.float32) * own_square)
    anchor = z_anchor.astype(jnp.float32)
    centered = anchor - mean
    hinge = jnp.where(deviation < 1.0, centered / deviation, 0.0)
    factor = total / (4.0 * (total - 1))
    return anchor - z_other.astype(jnp.float32) - factor * hinge + update


def solution(mesh):
    placed = (P("dp", "feat"), P("dp", "feat"))
    return jax.shard_map(
        per_device, mesh=mesh, in_specs=placed, out_specs=P("dp", "feat"), check_vma=False
    )
```

```python
import jax
import jax.numpy as jnp
from jax import lax
from jax.sharding import PartitionSpec as P

FLOOD = 4
SWAP = 4


def gram(left, right):
    return lax.dot_general(
        left, right, (((1,), (1,)), ((), ())), preferred_element_type=jnp.float32
    )


def dot_t(left, right):
    return lax.dot_general(
        left, right, (((0,), (0,)), ((), ())), preferred_element_type=jnp.float32
    )


def by_gather(z_anchor, z_other):
    rows_here, width = z_anchor.shape
    groups = lax.axis_size("dp")
    total = rows_here * groups
    mine = lax.axis_index("dp") * rows_here
    column = lax.all_gather(z_anchor, "dp", axis=0, tiled=True).astype(jnp.float32)
    mean = jnp.sum(column, axis=0) / total
    centered_all = column - mean
    variance = jnp.sum(centered_all * centered_all, axis=0) / (total - 1)
    rounded_all = centered_all.astype(jnp.bfloat16)
    widened = rounded_all.astype(jnp.float32)
    own_square = jnp.sum(widened * widened, axis=0)
    rounded = lax.dynamic_slice_in_dim(rounded_all, mine, rows_here, 0)
    inner = lax.psum(gram(rounded, rounded_all).astype(jnp.bfloat16), "feat")
    product = jnp.dot(inner, rounded_all, preferred_element_type=jnp.float32)
    product = product - rounded.astype(jnp.float32) * own_square
    return finish(z_anchor, z_other, mean, variance, total, product)


def finish(z_anchor, z_other, mean, variance, total, product):
    coef = 2.0 * total / (25.0 * (total - 1)) / (total - 1)
    anchor = z_anchor.astype(jnp.float32)
    centered = anchor - mean
    deviation = jnp.sqrt(variance + 0.0001)
    hinge = jnp.where(deviation < 1.0, centered / deviation, 0.0)
    factor = total / (4.0 * (total - 1))
    return anchor - z_other.astype(jnp.float32) - factor * hinge + coef * product


def over_dp(x):
    for step in (1, 3):
        x = x + lax.ppermute(x, "dp", [(i, i ^ step) for i in range(4)])
    return x


def over_feat(x):
    for step in (1, 2, 4):
        x = x + lax.ppermute(x, "feat", [(i, i ^ step) for i in range(8)])
    return x


def to_partner(x, step):
    return lax.ppermute(x, "feat", [(i, i ^ step) for i in range(8)])


def scatter_sum(x):
    here = lax.axis_index("feat")
    core, chip = here % 2, here // 2
    half = x.shape[0] // 2
    halves = x.reshape(2, half, x.shape[1])
    sent = lax.dynamic_index_in_dim(halves, 1 - core, 0, False).astype(jnp.bfloat16)
    kept = lax.dynamic_index_in_dim(halves, core, 0, False)
    kept = kept + to_partner(sent, 1).astype(jnp.float32)
    pieces = kept.reshape(4, half // 4, x.shape[1])
    result = lax.dynamic_index_in_dim(pieces, chip, 0, False)
    for step in (1, 2, 3):
        out = lax.dynamic_index_in_dim(pieces, chip ^ step, 0, False).astype(jnp.bfloat16)
        result = result + to_partner(out, 2 * step).astype(jnp.float32)
    return result.astype(jnp.bfloat16)


def gather_rows(x):
    here = lax.axis_index("feat")
    core, chip = here % 2, here // 2
    near = jnp.stack([x] + [to_partner(x, 2 * step) for step in (1, 2, 3)])
    near = jnp.where(chip % 2 == 1, near[jnp.array([1, 0, 3, 2])], near)
    near = jnp.where(chip // 2 == 1, near[jnp.array([2, 3, 0, 1])], near)
    near = near.reshape(4 * x.shape[0], x.shape[1])
    far = to_partner(near, 1)
    return jnp.where(
        core == 0, jnp.concatenate([near, far]), jnp.concatenate([far, near])
    )


def by_line(z_anchor, z_other):
    rows, width = z_anchor.shape
    total = rows * 4
    plane = lax.axis_index("dp")
    middle = (plane == 1) | (plane == 2)
    inward, across, outward = [(0, 1), (3, 2)], [(1, 2), (2, 1)], [(1, 0), (2, 3)]

    near, far = [], []
    for piece in jnp.split(z_anchor, FLOOD, axis=0):
        near.append(lax.ppermute(piece, "dp", inward))
        crossed = lax.ppermute(near[-1], "dp", across)
        at_end = lax.ppermute(crossed, "dp", outward)
        far.append(jnp.where(middle, crossed, at_end))
    swapped = [
        lax.ppermute(piece, "dp", across) for piece in jnp.split(z_anchor, SWAP, axis=1)
    ]

    anchor = z_anchor.astype(jnp.float32)
    mean = over_dp(jnp.sum(anchor, axis=0)) / total
    def center(block, shift):
        return (block.astype(jnp.float32) - shift).astype(jnp.bfloat16)

    centered = anchor - mean
    own = centered.astype(jnp.bfloat16)
    widened = own.astype(jnp.float32)
    squares = over_dp(
        jnp.stack([jnp.sum(centered * centered, axis=0), jnp.sum(widened * widened, axis=0)])
    )
    variance, own_square = squares[0] / (total - 1), squares[1]
    norms = over_feat(jnp.sum(widened * widened, axis=1))

    diagonal = jnp.arange(rows)[:, None] == jnp.arange(rows)[None, :]
    near = jnp.concatenate([center(x, mean) for x in near])
    far = jnp.concatenate([center(x, mean) for x in far])

    with_near = scatter_sum(gram(own, near))
    with_far = scatter_sum(gram(own, far))
    other_far = lax.ppermute(with_far, "dp", across)
    first = gather_rows(jnp.concatenate([with_near, other_far], axis=1))
    with_near, other_far = first[:, :rows], first[:, rows:]

    own_pieces = jnp.split(own, SWAP, axis=1)
    means = jnp.split(mean, SWAP)
    swapped = [center(x, m) for x, m in zip(swapped, means)]
    from_middle = [
        lax.ppermute(
            (dot_t(with_near, a) + dot_t(other_far, b)).astype(jnp.bfloat16), "dp", outward
        )
        for a, b in zip(own_pieces, swapped)
    ]
    swapped = jnp.concatenate(swapped, axis=1)

    with_own = gather_rows(scatter_sum(jnp.where(diagonal, 0.0, gram(own, own))))
    with_far = gather_rows(with_far)
    with_swapped = gather_rows(scatter_sum(gram(own, swapped)))
    zero = jnp.zeros((), jnp.bfloat16)
    with_near = jnp.where(middle, with_near, zero)
    with_swapped = jnp.where(middle, with_swapped, zero)

    def dot(a, b):
        return jnp.dot(a, b, preferred_element_type=jnp.float32)

    product = dot(with_own, own) + dot(with_far, far) + dot(with_near, near)
    product = product + dot(with_swapped, swapped)
    product = product + jnp.concatenate(from_middle, axis=1).astype(jnp.float32)
    product = product + widened * (norms[:, None] - own_square[None, :])
    return finish(z_anchor, z_other, mean, variance, total, product)


def solution(mesh):
    placed = (P("dp", "feat"), P("dp", "feat"))
    in_line = mesh.shape["dp"] == 4 and mesh.shape["feat"] == 8
    return jax.shard_map(
        by_line if in_line else by_gather,
        mesh=mesh, in_specs=placed, out_specs=P("dp", "feat"), check_vma=False,
    )
```

```python
import jax
import jax.numpy as jnp
from jax import lax
from jax.sharding import PartitionSpec as P

FLOOD = 4
SWAP = 4


def gram(left, right):
    return lax.dot_general(
        left, right, (((1,), (1,)), ((), ())), preferred_element_type=jnp.float32
    )


def dot_t(left, right):
    return lax.dot_general(
        left, right, (((0,), (0,)), ((), ())), preferred_element_type=jnp.float32
    )


def by_gather(z_anchor, z_other):
    rows_here, width = z_anchor.shape
    groups = lax.axis_size("dp")
    total = rows_here * groups
    mine = lax.axis_index("dp") * rows_here
    column = lax.all_gather(z_anchor, "dp", axis=0, tiled=True).astype(jnp.float32)
    mean = jnp.sum(column, axis=0) / total
    centered_all = column - mean
    variance = jnp.sum(centered_all * centered_all, axis=0) / (total - 1)
    rounded_all = centered_all.astype(jnp.bfloat16)
    widened = rounded_all.astype(jnp.float32)
    own_square = jnp.sum(widened * widened, axis=0)
    rounded = lax.dynamic_slice_in_dim(rounded_all, mine, rows_here, 0)
    inner = lax.psum(gram(rounded, rounded_all).astype(jnp.bfloat16), "feat")
    product = jnp.dot(inner, rounded_all, preferred_element_type=jnp.float32)
    product = product - rounded.astype(jnp.float32) * own_square
    return finish(z_anchor, z_other, mean, variance, total, product)


def finish(z_anchor, z_other, mean, variance, total, product):
    coef = 2.0 * total / (25.0 * (total - 1)) / (total - 1)
    anchor = z_anchor.astype(jnp.float32)
    centered = anchor - mean
    deviation = jnp.sqrt(variance + 0.0001)
    hinge = jnp.where(deviation < 1.0, centered / deviation, 0.0)
    factor = total / (4.0 * (total - 1))
    return anchor - z_other.astype(jnp.float32) - factor * hinge + coef * product


def over_dp(x):
    for step in (1, 3):
        x = x + lax.ppermute(x, "dp", [(i, i ^ step) for i in range(4)])
    return x


def over_feat(x):
    for step in (1, 2, 4):
        x = x + lax.ppermute(x, "feat", [(i, i ^ step) for i in range(8)])
    return x


def to_partner(x, step):
    return lax.ppermute(x, "feat", [(i, i ^ step) for i in range(8)])


def scatter_sum(x):
    here = lax.axis_index("feat")
    core, chip = here % 2, here // 2
    half = x.shape[0] // 2
    halves = x.reshape(2, half, x.shape[1])
    sent = lax.dynamic_index_in_dim(halves, 1 - core, 0, False).astype(jnp.bfloat16)
    kept = lax.dynamic_index_in_dim(halves, core, 0, False)
    kept = kept + to_partner(sent, 1).astype(jnp.float32)
    pieces = kept.reshape(4, half // 4, x.shape[1])
    result = lax.dynamic_index_in_dim(pieces, chip, 0, False)
    for step in (1, 2, 3):
        out = lax.dynamic_index_in_dim(pieces, chip ^ step, 0, False).astype(jnp.bfloat16)
        result = result + to_partner(out, 2 * step).astype(jnp.float32)
    return result.astype(jnp.bfloat16)


def gather_rows(x):
    here = lax.axis_index("feat")
    core, chip = here % 2, here // 2
    near = jnp.stack([x] + [to_partner(x, 2 * step) for step in (1, 2, 3)])
    near = jnp.where(chip % 2 == 1, near[jnp.array([1, 0, 3, 2])], near)
    near = jnp.where(chip // 2 == 1, near[jnp.array([2, 3, 0, 1])], near)
    near = near.reshape(4 * x.shape[0], x.shape[1])
    far = to_partner(near, 1)
    return jnp.where(
        core == 0, jnp.concatenate([near, far]), jnp.concatenate([far, near])
    )


def by_line(z_anchor, z_other):
    rows, width = z_anchor.shape
    total = rows * 4
    plane = lax.axis_index("dp")
    middle = (plane == 1) | (plane == 2)
    inward, across, outward = [(0, 1), (3, 2)], [(1, 2), (2, 1)], [(1, 0), (2, 3)]

    anchor = z_anchor.astype(jnp.float32)
    sums = jnp.sum(anchor, axis=0)
    pieces = jnp.split(z_anchor, FLOOD, axis=0)
    near = [lax.ppermute(pieces[0], "dp", inward)]
    others = [lax.ppermute(sums, "dp", [(i, (i + k) % 4) for i in range(4)]) for k in (1, 2, 3)]
    swaps = jnp.split(z_anchor, SWAP, axis=1)
    swapped = [lax.ppermute(after(swaps[0], sums), "dp", across)]
    for piece in pieces[1:]:
        near.append(lax.ppermute(after(piece, sums), "dp", inward))
    mean = (sums + others[0] + others[1] + others[2]) / total

    def center(block, shift):
        return (block.astype(jnp.float32) - shift).astype(jnp.bfloat16)

    centered = anchor - mean
    own = centered.astype(jnp.bfloat16)
    widened = own.astype(jnp.float32)
    squares = over_dp(
        jnp.stack([jnp.sum(centered * centered, axis=0), jnp.sum(widened * widened, axis=0)])
    )
    variance, own_square = squares[0] / (total - 1), squares[1]
    norms = over_feat(jnp.sum(widened * widened, axis=1))
    diagonal = jnp.arange(rows)[:, None] == jnp.arange(rows)[None, :]
    own_own = jnp.where(diagonal, 0.0, gram(own, own))

    crossed = [lax.ppermute(x, "dp", across) for x in near]
    at_end = [lax.ppermute(x, "dp", outward) for x in crossed]
    for piece in swaps[1:3]:
        swapped.append(lax.ppermute(after(piece, near[-1]), "dp", across))
    near = jnp.concatenate([center(x, mean) for x in near])
    crossed = jnp.concatenate([center(x, mean) for x in crossed])

    first = scatter_sum(
        jnp.concatenate([jnp.where(middle, gram(own, near), own_own), gram(own, crossed)], axis=1)
    )
    other_far = lax.ppermute(first[:, rows:], "dp", across)
    for piece in swaps[3:]:
        swapped.append(lax.ppermute(after(piece, first), "dp", across))
    first = gather_rows(jnp.concatenate([first, other_far], axis=1))
    with_near, with_crossed, other_far = (
        first[:, :rows], first[:, rows:2 * rows], first[:, 2 * rows:]
    )

    own_pieces = jnp.split(own, SWAP, axis=1)
    means = jnp.split(mean, SWAP)
    swapped = [center(x, m) for x, m in zip(swapped, means)]
    from_middle = [
        lax.ppermute(
            (dot_t(with_near, a) + dot_t(other_far, b)).astype(jnp.bfloat16), "dp", outward
        )
        for a, b in zip(own_pieces, swapped)
    ]
    swapped = jnp.concatenate(swapped, axis=1)
    at_end = jnp.concatenate([center(x, mean) for x in at_end])

    second = gather_rows(scatter_sum(jnp.concatenate(
        [jnp.where(middle, own_own, gram(own, at_end)), gram(own, swapped)], axis=1
    )))

    def dot(a, b):
        return jnp.dot(a, b, preferred_element_type=jnp.float32)

    zero = jnp.zeros((), jnp.bfloat16)
    one = jnp.where(middle, near, own)
    two = jnp.where(middle, own, at_end)
    product = dot(with_near, one) + dot(second[:, :rows], two)
    product = product + dot(jnp.where(middle, with_crossed, zero), crossed)
    product = product + dot(jnp.where(middle, second[:, rows:], zero), swapped)
    product = product + jnp.concatenate(from_middle, axis=1).astype(jnp.float32)
    product = product + widened * (norms[:, None] - own_square[None, :])
    return finish(z_anchor, z_other, mean, variance, total, product)


def after(x, *others):
    return lax.optimization_barrier((x, *others))[0]


def solution(mesh):
    placed = (P("dp", "feat"), P("dp", "feat"))
    in_line = mesh.shape["dp"] == 4 and mesh.shape["feat"] == 8
    return jax.shard_map(
        by_line if in_line else by_gather,
        mesh=mesh, in_specs=placed, out_specs=P("dp", "feat"), check_vma=False,
    )
```

```python
import functools
import math

import jax
import jax.numpy as jnp
from jax import lax
from jax.experimental import pallas as pl
from jax.experimental.pallas import tpu as pltpu
from jax.sharding import PartitionSpec as P

VMEM = pltpu.CompilerParams(vmem_limit_bytes=24 * 1024 * 1024)
NORM = 128


def kernel_call(body, outs, flops=0, smem=0):
    def call(*args):
        moved = sum(a.size * a.dtype.itemsize for a in args)
        moved += sum(math.prod(s) * jnp.dtype(t).itemsize for s, t in outs)
        space = [pltpu.SMEM] * smem + [pltpu.VMEM] * (len(args) - smem)
        return pl.pallas_call(
            body,
            out_shape=[jax.ShapeDtypeStruct(s, t) for s, t in outs],
            in_specs=[pl.BlockSpec(memory_space=m) for m in space],
            out_specs=[pl.BlockSpec(memory_space=pltpu.VMEM) for _ in outs],
            compiler_params=VMEM,
            cost_estimate=pl.CostEstimate(flops=0, bytes_accessed=0, transcendentals=0),
        )(*args)

    return call


def gram(left, right):
    return lax.dot_general(
        left, right, (((1,), (1,)), ((), ())), preferred_element_type=jnp.float32
    )


def dot_t(left, right):
    return lax.dot_general(
        left, right, (((0,), (0,)), ((), ())), preferred_element_type=jnp.float32
    )


def dot(left, right):
    return jnp.dot(left, right, preferred_element_type=jnp.float32)


def centered_into(out, at, piece, mean):
    block = (piece[...].astype(jnp.float32) - mean).astype(jnp.bfloat16)
    out[at:at + block.shape[0], :] = block
    wide = block.astype(jnp.float32)
    return jnp.sum(wide * wide, axis=0, keepdims=True)


def high_low(n, like):
    high = n.astype(jnp.bfloat16).astype(jnp.float32)
    lane = lax.broadcasted_iota(jnp.int32, like, 1)
    return jnp.where(lane == 0, high, jnp.where(lane == 1, n - high, 0.0))


def own_kernel(order, z, mean, own, turned, square, kept, sent):
    rows = z.shape[0]
    eighth, half = rows // 8, rows // 2
    square[...] = centered_into(own, 0, z, mean[...])
    for k in range(8):
        start = pl.multiple_of(order[k] * eighth, eighth)
        turned[k * eighth:(k + 1) * eighth, :] = own[pl.ds(start, eighth), :]
    inner = gram(turned[...], own[...])
    wide = turned[...].astype(jnp.float32)
    norm = jnp.sum(wide * wide, axis=1, keepdims=True)
    column = lax.broadcasted_iota(jnp.int32, (eighth, rows), 1)
    row = lax.broadcasted_iota(jnp.int32, (eighth, rows), 0)
    for k in range(8):
        here = slice(k * eighth, (k + 1) * eighth)
        off = jnp.where(column == row + order[k] * eighth, 0.0, inner[here])
        if k < 4:
            kept[here, :rows] = off
        else:
            sent[k * eighth - half:(k + 1) * eighth - half, :rows] = off.astype(jnp.bfloat16)
    lane = lax.broadcasted_iota(jnp.int32, (half, NORM), 1)
    kept[:, rows:] = jnp.where(lane == 0, norm[:half], 0.0)
    sent[:, rows:] = high_low(norm[half:], (half, NORM)).astype(jnp.bfloat16)


def first_kernel(turned, *refs):
    pieces = (len(refs) - 7) // 2
    near_in, far_in, mean = refs[:pieces], refs[pieces:2 * pieces], refs[2 * pieces]
    near, far, near_square, far_square, kept, sent = refs[2 * pieces + 1:]
    rows = near.shape[0]
    half = rows // 2
    for k, (pile, out, square) in enumerate(
        ((near_in, near, near_square), (far_in, far, far_square))
    ):
        at, total = 0, 0.0
        for piece in pile:
            total = total + centered_into(out, at, piece, mean[...])
            at += piece.shape[0]
        square[...] = total
        inner = gram(turned[...], out[...])
        kept[:, k * rows:(k + 1) * rows] = inner[:half]
        sent[:, k * rows:(k + 1) * rows] = inner[half:].astype(jnp.bfloat16)


def second_kernel(middle, turned, *refs):
    *ends, left, right, mean, own_kept, own_sent = refs[:-4]
    end, square, kept, sent = refs[-4:]
    rows, width = end.shape
    half = rows // 2
    for ref, own in ((kept, own_kept), (sent, own_sent)):
        ref[:, :rows] = own[:, :rows]
        ref[:, 2 * rows:] = own[:, rows:]

    def put(inner):
        kept[:, rows:2 * rows] = inner[:half]
        sent[:, rows:2 * rows] = inner[half:].astype(jnp.bfloat16)

    @pl.when(middle[0] == 1)
    def _():
        end[...] = jnp.zeros_like(end)
        square[...] = jnp.zeros_like(square)
        put(gram(turned[:, :width // 2], left[...]) + gram(turned[:, width // 2:], right[...]))

    @pl.when(middle[0] == 0)
    def _():
        at, total = 0, 0.0
        for piece in ends:
            total = total + centered_into(end, at, piece, mean[...])
            at += piece.shape[0]
        square[...] = total
        put(gram(turned[...], end[...]))


def with_norm(x, last):
    if not last:
        return x
    tail = x[:, last:]
    split = high_low(jnp.sum(tail, axis=1, keepdims=True), tail.shape)
    return jnp.concatenate([x[:, :last], split], axis=1)


def add_kernel(last, kept, got, mine, *out):
    total = with_norm(kept[...] + got[...].astype(jnp.float32), last)
    quarter = mine.shape[0]
    mine[...] = total[:quarter]
    for k, ref in enumerate(out, 1):
        ref[...] = total[k * quarter:(k + 1) * quarter].astype(jnp.bfloat16)


def total_kernel(last, mine, a, b, c, out):
    total = mine[...] + a[...].astype(jnp.float32)
    total = total + b[...].astype(jnp.float32) + c[...].astype(jnp.float32)
    out[...] = with_norm(total, last).astype(jnp.bfloat16)


def place_kernel(order, near, far, out):
    eighth = out.shape[0] // 8
    for k in range(4):
        here = slice(k * eighth, (k + 1) * eighth)
        out[pl.ds(pl.multiple_of(order[k] * eighth, eighth), eighth), :] = near[here, :]
        out[pl.ds(pl.multiple_of(order[4 + k] * eighth, eighth), eighth), :] = far[here, :]


def middle_kernel(inner, own, near, own_square, mean, *refs):
    *pieces, swapped, square, out = refs
    rows = own.shape[0]
    at = 0
    for piece in pieces:
        here = slice(at, at + piece.shape[1])
        block = (piece[...].astype(jnp.float32) - mean[:, here]).astype(jnp.bfloat16)
        swapped[:, here] = block
        wide = block.astype(jnp.float32)
        square[:, here] = jnp.sum(wide * wide, axis=0, keepdims=True)
        at += piece.shape[1]
    product = dot_t(inner[:, :rows], own[...]) + dot_t(inner[:, 2 * rows:], swapped[...])
    product = product - near[...].astype(jnp.float32) * (own_square[...] + square[...])
    out[...] = product.astype(jnp.bfloat16)


def last_kernel(
    total, middle, first, second, own, near, far, end, swapped, pushed, z, other,
    own_square, near_square, far_square, end_square, swapped_square, mean, spread, out,
):
    rows = own.shape[0]
    norm = jnp.sum(second[:, 2 * rows:].astype(jnp.float32), axis=1, keepdims=True)
    anchor = z[...].astype(jnp.float32)
    deviation = jnp.sqrt(spread[...] / (total - 1) + 0.0001)
    centered = anchor - mean[...]
    hinge = jnp.where(deviation < 1.0, centered / deviation, 0.0)
    plain = anchor - other[...].astype(jnp.float32) - total / (4.0 * (total - 1)) * hinge
    coef = 2.0 * total / (25.0 * (total - 1)) / (total - 1)
    both = dot(second[:, :rows], own[...])
    wide = own[...].astype(jnp.float32)

    @pl.when(middle[0] == 1)
    def _():
        product = both + dot(first[:, :rows], near[...])
        product = product + dot(first[:, rows:2 * rows], far[...])
        product = product + dot(second[:, rows:2 * rows], swapped[...])
        square = own_square[...] + near_square[...] + far_square[...] + swapped_square[...]
        out[...] = plain + coef * (product + wide * (norm - square))

    @pl.when(middle[0] == 0)
    def _():
        product = both + dot(second[:, rows:2 * rows], end[...])
        product = product + pushed[...].astype(jnp.float32)
        out[...] = plain + coef * (product + wide * (norm - own_square[...] - end_square[...]))


def to_partner(x, step):
    return lax.ppermute(x, "feat", [(i, i ^ step) for i in range(8)])


def scatter_sum(kept, sent, last=0):
    half, n = kept.shape
    eighth = (half // 4, n)
    mine, *out = kernel_call(
        functools.partial(add_kernel, last),
        [(eighth, jnp.float32)] + [(eighth, jnp.bfloat16)] * 3,
    )(kept, to_partner(sent, 1))
    got = [to_partner(x, 2 * k) for k, x in enumerate(out, 1)]
    return kernel_call(functools.partial(total_kernel, last), [(eighth, jnp.bfloat16)])(
        mine, *got
    )[0]


def gather_rows(x, order):
    near = jnp.concatenate([x] + [to_partner(x, 2 * k) for k in (1, 2, 3)])
    far = to_partner(near, 1)
    shape = (8 * x.shape[0], x.shape[1])
    return kernel_call(place_kernel, [(shape, jnp.bfloat16)], smem=1)(order, near, far)[0]


def after(x, *others):
    return lax.optimization_barrier((x, *others))[0]


def by_line(z_anchor, z_other):
    rows, width = z_anchor.shape
    total = rows * 4
    plane = lax.axis_index("dp")
    middle = ((plane == 1) | (plane == 2)).astype(jnp.int32).reshape(1)
    order = lax.axis_index("feat") ^ jnp.array([0, 2, 4, 6, 1, 3, 5, 7], jnp.int32)
    inward, across, outward = [(0, 1), (3, 2)], [(1, 2), (2, 1)], [(1, 0), (2, 3)]
    half = rows // 2
    flat, block = ((1, width), jnp.float32), ((rows, width), jnp.bfloat16)
    one_gram = 2 * rows * rows * width

    cuts = [0, 3 * rows // 8, 3 * rows // 4, rows]
    pieces = [z_anchor[a:b] for a, b in zip(cuts, cuts[1:])]
    cuts = [0, width // 4, width // 2, width]
    swaps = [z_anchor[:, a:b] for a, b in zip(cuts, cuts[1:])]

    near = [lax.ppermute(pieces[0], "dp", inward)]
    anchor = z_anchor.astype(jnp.float32)
    sums = jnp.sum(anchor, axis=0, keepdims=True)
    apart = anchor - sums / rows
    stats = jnp.concatenate([sums, jnp.sum(apart * apart, axis=0, keepdims=True)])
    all_stats = [stats] + [
        lax.ppermute(stats, "dp", [(i, (i + k) % 4) for i in range(4)]) for k in (1, 2, 3)
    ]
    swapped = [lax.ppermute(swaps[0], "dp", across)]
    for piece in pieces[1:]:
        near.append(lax.ppermute(after(piece, swapped[0], *all_stats[1:]), "dp", inward))
    mean = (all_stats[0][:1] + all_stats[1][:1] + all_stats[2][:1] + all_stats[3][:1]) / total
    spread = 0.0
    for one in all_stats:
        shift = one[:1] / rows - mean
        spread = spread + (one[1:] + rows * shift * shift)

    own, turned, own_square, own_kept, own_sent = kernel_call(
        own_kernel,
        [block, block, flat, ((half, rows + NORM), jnp.float32), ((half, rows + NORM), jnp.bfloat16)],
        flops=one_gram, smem=1,
    )(order, after(z_anchor, swapped[0]), mean)

    near[2] = after(near[2], near[1])
    crossed = [lax.ppermute(x, "dp", across) for x in near]
    at_end = [lax.ppermute(x, "dp", outward) for x in crossed]
    swapped.append(lax.ppermute(after(swaps[1], near[-1]), "dp", across))

    near, far, near_square, far_square, kept, sent = kernel_call(
        first_kernel,
        [block, block, flat, flat, ((half, 2 * rows), jnp.float32), ((half, 2 * rows), jnp.bfloat16)],
        flops=2 * one_gram,
    )(after(turned, at_end[0]), *near, *crossed, mean)
    first = scatter_sum(kept, sent)
    other_far = lax.ppermute(first[:, rows:], "dp", across)
    swapped.append(lax.ppermute(after(swaps[2], first), "dp", across))
    first = after(first, *at_end, swapped[1])
    first = gather_rows(jnp.concatenate([first, other_far], axis=1), order)

    pushed, kept_swapped, swapped_square = [], [], []
    for pile, here in (
        (swapped[:2], slice(0, width // 2)), (swapped[2:], slice(width // 2, width))
    ):
        a, b, c = kernel_call(
            middle_kernel,
            [((rows, width // 2), jnp.bfloat16), ((1, width // 2), jnp.float32),
             ((rows, width // 2), jnp.bfloat16)],
            flops=one_gram,
        )(first, own[:, here], near[:, here], own_square[:, here], mean[:, here], *pile)
        kept_swapped.append(a)
        swapped_square.append(b)
        pushed.append(lax.ppermute(c, "dp", outward))

    wide = 2 * rows + NORM
    end, end_square, kept, sent = kernel_call(
        second_kernel,
        [block, flat, ((half, wide), jnp.float32), ((half, wide), jnp.bfloat16)],
        flops=one_gram, smem=1,
    )(middle, turned, *at_end, *kept_swapped, mean, own_kept, own_sent)
    second = after(scatter_sum(kept, sent, 2 * rows), pushed[0])
    second = gather_rows(second, order)

    tile = width // 4
    whole = lambda n: pl.BlockSpec((rows, n), lambda j: (0, 0))
    strip = pl.BlockSpec((rows, tile), lambda j: (0, j))
    line = pl.BlockSpec((1, tile), lambda j: (0, j))
    return pl.pallas_call(
        functools.partial(last_kernel, total),
        grid=(4,),
        out_shape=jax.ShapeDtypeStruct((rows, width), jnp.float32),
        in_specs=[pl.BlockSpec(memory_space=pltpu.SMEM), whole(3 * rows), whole(wide)]
        + [strip] * 8 + [line] * 7,
        out_specs=strip,
        compiler_params=VMEM,
        cost_estimate=pl.CostEstimate(
            flops=4 * one_gram, bytes_accessed=14 * rows * width, transcendentals=0
        ),
    )(
        middle, first, second, own, near, far, end, jnp.concatenate(kept_swapped, axis=1),
        jnp.concatenate(pushed, axis=1), z_anchor, z_other, own_square, near_square, far_square,
        end_square, jnp.concatenate(swapped_square, axis=1), mean, spread,
    )


def by_gather(z_anchor, z_other):
    rows_here, width = z_anchor.shape
    groups = lax.axis_size("dp")
    total = rows_here * groups
    mine = lax.axis_index("dp") * rows_here
    column = lax.all_gather(z_anchor, "dp", axis=0, tiled=True).astype(jnp.float32)
    mean = jnp.sum(column, axis=0) / total
    centered_all = column - mean
    variance = jnp.sum(centered_all * centered_all, axis=0) / (total - 1)
    rounded_all = centered_all.astype(jnp.bfloat16)
    widened = rounded_all.astype(jnp.float32)
    own_square = jnp.sum(widened * widened, axis=0)
    rounded = lax.dynamic_slice_in_dim(rounded_all, mine, rows_here, 0)
    inner = lax.psum(gram(rounded, rounded_all).astype(jnp.bfloat16), "feat")
    product = jnp.dot(inner, rounded_all, preferred_element_type=jnp.float32)
    product = product - rounded.astype(jnp.float32) * own_square
    return finish(z_anchor, z_other, mean, variance, total, product)


def finish(z_anchor, z_other, mean, variance, total, product):
    coef = 2.0 * total / (25.0 * (total - 1)) / (total - 1)
    anchor = z_anchor.astype(jnp.float32)
    centered = anchor - mean
    deviation = jnp.sqrt(variance + 0.0001)
    hinge = jnp.where(deviation < 1.0, centered / deviation, 0.0)
    factor = total / (4.0 * (total - 1))
    return anchor - z_other.astype(jnp.float32) - factor * hinge + coef * product


def solution(mesh):
    placed = (P("dp", "feat"), P("dp", "feat"))
    in_line = mesh.shape["dp"] == 4 and mesh.shape["feat"] == 8
    return jax.shard_map(
        by_line if in_line else by_gather,
        mesh=mesh, in_specs=placed, out_specs=P("dp", "feat"), check_vma=False,
    )
```

```python
import functools
import math

import jax
import jax.numpy as jnp
from jax import lax
from jax.experimental import pallas as pl
from jax.experimental.pallas import tpu as pltpu
from jax.sharding import PartitionSpec as P

VMEM = pltpu.CompilerParams(vmem_limit_bytes=24 * 1024 * 1024)
NORM = 128


def kernel_call(body, outs, flops=0, smem=0):
    def call(*args):
        moved = sum(a.size * a.dtype.itemsize for a in args)
        moved += sum(math.prod(s) * jnp.dtype(t).itemsize for s, t in outs)
        space = [pltpu.SMEM] * smem + [pltpu.VMEM] * (len(args) - smem)
        return pl.pallas_call(
            body,
            out_shape=[jax.ShapeDtypeStruct(s, t) for s, t in outs],
            in_specs=[pl.BlockSpec(memory_space=m) for m in space],
            out_specs=[pl.BlockSpec(memory_space=pltpu.VMEM) for _ in outs],
            compiler_params=VMEM,
            cost_estimate=pl.CostEstimate(flops=0, bytes_accessed=0, transcendentals=0),
        )(*args)

    return call


def gram(left, right):
    return lax.dot_general(
        left, right, (((1,), (1,)), ((), ())), preferred_element_type=jnp.float32
    )


def dot_t(left, right):
    return lax.dot_general(
        left, right, (((0,), (0,)), ((), ())), preferred_element_type=jnp.float32
    )


def dot(left, right):
    return jnp.dot(left, right, preferred_element_type=jnp.float32)


def centered_into(out, block, mean, square):
    out[...] = (block[...].astype(jnp.float32) - mean).astype(jnp.bfloat16)
    wide = out[...].astype(jnp.float32)
    square[...] = jnp.sum(wide * wide, axis=0, keepdims=True)


def high_low(n, like):
    high = n.astype(jnp.bfloat16).astype(jnp.float32)
    lane = lax.broadcasted_iota(jnp.int32, like, 1)
    return jnp.where(lane == 0, high, jnp.where(lane == 1, n - high, 0.0))


def turn_into(turned, order, block):
    eighth = block.shape[0] // 8
    for k in range(8):
        start = pl.multiple_of(order[k] * eighth, eighth)
        turned[k * eighth:(k + 1) * eighth, :] = block[pl.ds(start, eighth), :]


def own_kernel(order, z, mean, own, turned, square):
    centered_into(own, z, mean[...], square)
    turn_into(turned, order, own)


def first_kernel(order, turned, near_in, swapped_in, mean, *refs):
    near, swapped, near_square, swapped_square, kept, sent, turned_near = refs
    rows = near.shape[0]
    half = rows // 2
    centered_into(near, near_in, mean[...], near_square)
    centered_into(swapped, swapped_in, mean[...], swapped_square)
    turn_into(turned_near, order, near)
    for k, (left, right) in enumerate(((turned, near), (turned_near, swapped))):
        inner = gram(left[...], right[...])
        kept[:, k * rows:(k + 1) * rows] = inner[:half]
        sent[:, k * rows:(k + 1) * rows] = inner[half:].astype(jnp.bfloat16)


def second_kernel(order, middle, turned, own, swapped, end_in, mean, end, square, kept, sent):
    rows = end.shape[0]
    eighth, half = rows // 8, rows // 2
    inner = gram(turned[...], own[...])
    wide = turned[...].astype(jnp.float32)
    norm = jnp.sum(wide * wide, axis=1, keepdims=True)
    column = lax.broadcasted_iota(jnp.int32, (eighth, rows), 1)
    row = lax.broadcasted_iota(jnp.int32, (eighth, rows), 0)
    for k in range(8):
        here = slice(k * eighth, (k + 1) * eighth)
        off = jnp.where(column == row + order[k] * eighth, 0.0, inner[here])
        if k < 4:
            kept[here, :rows] = off
        else:
            sent[k * eighth - half:(k + 1) * eighth - half, :rows] = off.astype(jnp.bfloat16)
    lane = lax.broadcasted_iota(jnp.int32, (half, NORM), 1)
    kept[:, 2 * rows:] = jnp.where(lane == 0, norm[:half], 0.0)
    sent[:, 2 * rows:] = high_low(norm[half:], (half, NORM)).astype(jnp.bfloat16)

    def put(inner):
        kept[:, rows:2 * rows] = inner[:half]
        sent[:, rows:2 * rows] = inner[half:].astype(jnp.bfloat16)

    @pl.when(middle[0] == 1)
    def _():
        end[...] = jnp.zeros_like(end)
        square[...] = jnp.zeros_like(square)
        put(gram(turned[...], swapped[...]))

    @pl.when(middle[0] == 0)
    def _():
        centered_into(end, end_in, mean[...], square)
        put(gram(turned[...], end[...]))


def with_norm(x, last):
    if not last:
        return x
    tail = x[:, last:]
    split = high_low(jnp.sum(tail, axis=1, keepdims=True), tail.shape)
    return jnp.concatenate([x[:, :last], split], axis=1)


def add_kernel(last, kept, got, mine, *out):
    total = with_norm(kept[...] + got[...].astype(jnp.float32), last)
    quarter = mine.shape[0]
    mine[...] = total[:quarter]
    for k, ref in enumerate(out, 1):
        ref[...] = total[k * quarter:(k + 1) * quarter].astype(jnp.bfloat16)


def total_kernel(last, mine, a, b, c, out):
    total = mine[...] + a[...].astype(jnp.float32)
    total = total + b[...].astype(jnp.float32) + c[...].astype(jnp.float32)
    out[...] = with_norm(total, last).astype(jnp.bfloat16)


def place_kernel(order, near, far, out):
    eighth = out.shape[0] // 8
    for k in range(4):
        here = slice(k * eighth, (k + 1) * eighth)
        out[pl.ds(pl.multiple_of(order[k] * eighth, eighth), eighth), :] = near[here, :]
        out[pl.ds(pl.multiple_of(order[4 + k] * eighth, eighth), eighth), :] = far[here, :]


def middle_kernel(inner, own, near, swapped, own_square, near_square, swapped_square, out, over):
    rows = own.shape[0]
    with_own, with_swapped = inner[:, :rows], inner[:, rows:]
    outward = dot_t(with_own, own[...]) + dot(with_swapped, swapped[...])
    square = own_square[...] + swapped_square[...]
    out[...] = (outward - near[...].astype(jnp.float32) * square).astype(jnp.bfloat16)
    across = dot_t(with_swapped, near[...])
    over[...] = (across - swapped[...].astype(jnp.float32) * near_square[...]).astype(jnp.bfloat16)


def coefficient(total):
    return 2.0 * total / (25.0 * (total - 1)) / (total - 1)


def last_kernel(
    total, middle, first, second, own, near, swapped, end, z, other,
    own_square, near_square, swapped_square, end_square, mean, spread, out,
):
    rows = own.shape[0]
    norm = jnp.sum(second[:, 2 * rows:].astype(jnp.float32), axis=1, keepdims=True)
    anchor = z[...].astype(jnp.float32)
    deviation = jnp.sqrt(spread[...] / (total - 1) + 0.0001)
    centered = anchor - mean[...]
    hinge = jnp.where(deviation < 1.0, centered / deviation, 0.0)
    plain = anchor - other[...].astype(jnp.float32) - total / (4.0 * (total - 1)) * hinge
    both = dot(second[:, :rows], own[...])
    wide = own[...].astype(jnp.float32)

    @pl.when(middle[0] == 1)
    def _():
        product = both + dot(first[:, :rows], near[...])
        product = product + dot(second[:, rows:2 * rows], swapped[...])
        square = own_square[...] + near_square[...] + swapped_square[...]
        out[...] = plain + coefficient(total) * (product + wide * (norm - square))

    @pl.when(middle[0] == 0)
    def _():
        product = both + dot(second[:, rows:2 * rows], end[...])
        square = own_square[...] + end_square[...]
        out[...] = plain + coefficient(total) * (product + wide * (norm - square))


def to_partner(x, step):
    return lax.ppermute(x, "feat", [(i, i ^ step) for i in range(8)])


def scatter_sum(kept, sent, last=0):
    half, n = kept.shape
    eighth = (half // 4, n)
    mine, *out = kernel_call(
        functools.partial(add_kernel, last),
        [(eighth, jnp.float32)] + [(eighth, jnp.bfloat16)] * 3,
    )(kept, to_partner(sent, 1))
    got = [to_partner(x, 2 * k) for k, x in enumerate(out, 1)]
    return kernel_call(functools.partial(total_kernel, last), [(eighth, jnp.bfloat16)])(
        mine, *got
    )[0]


def gather_rows(x, order):
    near = jnp.concatenate([x] + [to_partner(x, 2 * k) for k in (1, 2, 3)])
    far = to_partner(near, 1)
    shape = (8 * x.shape[0], x.shape[1])
    return kernel_call(place_kernel, [(shape, jnp.bfloat16)], smem=1)(order, near, far)[0]


def after(x, *others):
    return lax.optimization_barrier((x, *others))[0]


def by_line(z_anchor, z_other):
    rows, width = z_anchor.shape
    total = rows * 4
    plane = lax.axis_index("dp")
    middle = ((plane == 1) | (plane == 2)).astype(jnp.int32).reshape(1)
    order = lax.axis_index("feat") ^ jnp.array([0, 2, 4, 6, 1, 3, 5, 7], jnp.int32)
    inward, across, outward = [(0, 1), (3, 2)], [(1, 2), (2, 1)], [(1, 0), (2, 3)]
    half, wide = rows // 2, 2 * rows + NORM
    flat, block = ((1, width), jnp.float32), ((rows, width), jnp.bfloat16)

    near = lax.ppermute(z_anchor, "dp", inward)
    swapped = lax.ppermute(z_anchor, "dp", across)
    anchor = z_anchor.astype(jnp.float32)
    sums = jnp.sum(anchor, axis=0, keepdims=True)
    apart = anchor - sums / rows
    stats = jnp.concatenate([sums, jnp.sum(apart * apart, axis=0, keepdims=True)])
    all_stats = [stats] + [
        lax.ppermute(stats, "dp", [(i, (i + k) % 4) for i in range(4)]) for k in (1, 2, 3)
    ]
    mean = (all_stats[0][:1] + all_stats[1][:1] + all_stats[2][:1] + all_stats[3][:1]) / total
    spread = 0.0
    for one in all_stats:
        shift = one[:1] / rows - mean
        spread = spread + (one[1:] + rows * shift * shift)
    end = lax.ppermute(after(z_anchor, near, swapped), "dp", [(0, 3), (3, 0)])

    own, turned, own_square = kernel_call(own_kernel, [block, block, flat], smem=1)(
        order, z_anchor, mean
    )
    near, swapped, near_square, swapped_square, kept, sent, _ = kernel_call(
        first_kernel,
        [block, block, flat, flat, ((half, 2 * rows), jnp.float32),
         ((half, 2 * rows), jnp.bfloat16), block],
        smem=1,
    )(order, turned, near, swapped, mean)
    first = gather_rows(scatter_sum(kept, sent), order)

    pushed, ready = [], []
    for here in (slice(0, width // 2), slice(width // 2, width)):
        part = ((rows, width // 2), jnp.bfloat16)
        out, over = kernel_call(middle_kernel, [part, part])(
            first, own[:, here], near[:, here], swapped[:, here],
            own_square[:, here], near_square[:, here], swapped_square[:, here],
        )
        ready += [out, over]
        pushed.append((lax.ppermute(out, "dp", outward), lax.ppermute(over, "dp", across)))

    end, end_square, kept, sent = kernel_call(
        second_kernel,
        [block, flat, ((half, wide), jnp.float32), ((half, wide), jnp.bfloat16)],
        smem=2,
    )(order, middle, after(turned, *ready), own, swapped, end, mean)
    second = gather_rows(after(scatter_sum(kept, sent, 2 * rows), *pushed[0]), order)

    tile = width // 4
    whole = lambda n: pl.BlockSpec((rows, n), lambda j: (0, 0))
    strip = pl.BlockSpec((rows, tile), lambda j: (0, j))
    line = pl.BlockSpec((1, tile), lambda j: (0, j))
    held = pl.pallas_call(
        functools.partial(last_kernel, total),
        grid=(4,),
        out_shape=jax.ShapeDtypeStruct((rows, width), jnp.float32),
        in_specs=[pl.BlockSpec(memory_space=pltpu.SMEM), whole(2 * rows), whole(wide)]
        + [strip] * 6 + [line] * 6,
        out_specs=strip,
        compiler_params=VMEM,
        cost_estimate=pl.CostEstimate(
            flops=6 * rows * rows * width, bytes_accessed=20 * rows * width, transcendentals=0
        ),
    )(
        middle, first, second, own, near, swapped, end, z_anchor, z_other,
        own_square, near_square, swapped_square, end_square, mean, spread,
    )
    pushed = jnp.concatenate(
        [a.astype(jnp.float32) + b.astype(jnp.float32) for a, b in pushed], axis=1
    )
    return held + coefficient(total) * pushed


def by_gather(z_anchor, z_other):
    rows_here, width = z_anchor.shape
    groups = lax.axis_size("dp")
    total = rows_here * groups
    mine = lax.axis_index("dp") * rows_here
    column = lax.all_gather(z_anchor, "dp", axis=0, tiled=True).astype(jnp.float32)
    mean = jnp.sum(column, axis=0) / total
    centered_all = column - mean
    variance = jnp.sum(centered_all * centered_all, axis=0) / (total - 1)
    rounded_all = centered_all.astype(jnp.bfloat16)
    widened = rounded_all.astype(jnp.float32)
    own_square = jnp.sum(widened * widened, axis=0)
    rounded = lax.dynamic_slice_in_dim(rounded_all, mine, rows_here, 0)
    inner = lax.psum(gram(rounded, rounded_all).astype(jnp.bfloat16), "feat")
    product = jnp.dot(inner, rounded_all, preferred_element_type=jnp.float32)
    product = product - rounded.astype(jnp.float32) * own_square
    return finish(z_anchor, z_other, mean, variance, total, product)


def finish(z_anchor, z_other, mean, variance, total, product):
    coef = 2.0 * total / (25.0 * (total - 1)) / (total - 1)
    anchor = z_anchor.astype(jnp.float32)
    centered = anchor - mean
    deviation = jnp.sqrt(variance + 0.0001)
    hinge = jnp.where(deviation < 1.0, centered / deviation, 0.0)
    factor = total / (4.0 * (total - 1))
    return anchor - z_other.astype(jnp.float32) - factor * hinge + coef * product


def solution(mesh):
    placed = (P("dp", "feat"), P("dp", "feat"))
    in_line = mesh.shape["dp"] == 4 and mesh.shape["feat"] == 8
    return jax.shard_map(
        by_line if in_line else by_gather,
        mesh=mesh, in_specs=placed, out_specs=P("dp", "feat"), check_vma=False,
    )
```

```python
import functools
import math

import jax
import jax.numpy as jnp
from jax import lax
from jax.experimental import pallas as pl
from jax.experimental.pallas import tpu as pltpu
from jax.sharding import PartitionSpec as P

NORM = 128


def kernel_call(body, outs, smem=0, scratch=4):
    def call(*args):
        space = [pltpu.SMEM] * smem + [pltpu.VMEM] * (len(args) - smem)
        return pl.pallas_call(
            body,
            out_shape=[jax.ShapeDtypeStruct(s, t) for s, t in outs],
            in_specs=[pl.BlockSpec(memory_space=m) for m in space],
            out_specs=[pl.BlockSpec(memory_space=pltpu.VMEM) for _ in outs],
            compiler_params=pltpu.CompilerParams(vmem_limit_bytes=scratch * 1024 * 1024),
            cost_estimate=pl.CostEstimate(flops=0, bytes_accessed=0, transcendentals=0),
        )(*args)

    return call


def gram(left, right):
    return lax.dot_general(
        left, right, (((1,), (1,)), ((), ())), preferred_element_type=jnp.float32
    )


def dot_t(left, right):
    return lax.dot_general(
        left, right, (((0,), (0,)), ((), ())), preferred_element_type=jnp.float32
    )


def dot(left, right):
    return jnp.dot(left, right, preferred_element_type=jnp.float32)


def centered_into(out, pieces, mean, square):
    at, total = 0, 0.0
    for piece in pieces:
        block = (piece[...].astype(jnp.float32) - mean).astype(jnp.bfloat16)
        out[at:at + block.shape[0], :] = block
        wide = block.astype(jnp.float32)
        total = total + jnp.sum(wide * wide, axis=0, keepdims=True)
        at += block.shape[0]
    square[...] = total


def high_low(n, like):
    high = n.astype(jnp.bfloat16).astype(jnp.float32)
    lane = lax.broadcasted_iota(jnp.int32, like, 1)
    return jnp.where(lane == 0, high, jnp.where(lane == 1, n - high, 0.0))


def turn_into(turned, order, block):
    eighth = block.shape[0] // 8
    for k in range(8):
        start = pl.multiple_of(order[k] * eighth, eighth)
        turned[k * eighth:(k + 1) * eighth, :] = block[pl.ds(start, eighth), :]


def own_kernel(order, z, mean, own, turned, square, kept, sent):
    rows = z.shape[0]
    eighth, half = rows // 8, rows // 2
    centered_into(own, [z], mean[...], square)
    turn_into(turned, order, own)
    inner = gram(turned[...], own[...])
    wide = turned[...].astype(jnp.float32)
    norm = jnp.sum(wide * wide, axis=1, keepdims=True)
    column = lax.broadcasted_iota(jnp.int32, (eighth, rows), 1)
    row = lax.broadcasted_iota(jnp.int32, (eighth, rows), 0)
    for k in range(8):
        here = slice(k * eighth, (k + 1) * eighth)
        off = jnp.where(column == row + order[k] * eighth, 0.0, inner[here])
        if k < 4:
            kept[here, :rows] = off
        else:
            sent[k * eighth - half:(k + 1) * eighth - half, :rows] = off.astype(jnp.bfloat16)
    lane = lax.broadcasted_iota(jnp.int32, (half, NORM), 1)
    kept[:, rows:] = jnp.where(lane == 0, norm[:half], 0.0)
    sent[:, rows:] = high_low(norm[half:], (half, NORM)).astype(jnp.bfloat16)


def first_kernel(order, turned, near_a, near_b, swapped_a, swapped_b, mean, *refs):
    near, swapped, near_square, swapped_square, kept, sent, turned_near = refs
    rows = near.shape[0]
    half = rows // 2
    centered_into(near, [near_a, near_b], mean[...], near_square)
    centered_into(swapped, [swapped_a, swapped_b], mean[...], swapped_square)
    turn_into(turned_near, order, near)
    for k, (left, right) in enumerate(((turned, near), (turned_near, swapped))):
        inner = gram(left[...], right[...])
        kept[:, k * rows:(k + 1) * rows] = inner[:half]
        sent[:, k * rows:(k + 1) * rows] = inner[half:].astype(jnp.bfloat16)


def second_kernel(middle, turned, swapped, swapped_square, end, mean, third, square, kept, sent):
    half = third.shape[0] // 2

    @pl.when(middle[0] == 1)
    def _():
        third[...] = swapped[...]
        square[...] = swapped_square[...]

    @pl.when(middle[0] == 0)
    def _():
        centered_into(third, [end], mean[...], square)

    inner = gram(turned[...], third[...])
    kept[...] = inner[:half]
    sent[...] = inner[half:].astype(jnp.bfloat16)


def with_norm(x, last):
    if not last:
        return x
    tail = x[:, last:]
    split = high_low(jnp.sum(tail, axis=1, keepdims=True), tail.shape)
    return jnp.concatenate([x[:, :last], split], axis=1)


def add_kernel(last, kept, got, mine, *out):
    total = with_norm(kept[...] + got[...].astype(jnp.float32), last)
    quarter = mine.shape[0]
    mine[...] = total[:quarter]
    for k, ref in enumerate(out, 1):
        ref[...] = total[k * quarter:(k + 1) * quarter].astype(jnp.bfloat16)


def total_kernel(last, mine, a, b, c, out):
    total = mine[...] + a[...].astype(jnp.float32)
    total = total + b[...].astype(jnp.float32) + c[...].astype(jnp.float32)
    out[...] = with_norm(total, last).astype(jnp.bfloat16)


def place_kernel(order, near, far, out):
    eighth = out.shape[0] // 8
    for k in range(4):
        here = slice(k * eighth, (k + 1) * eighth)
        out[pl.ds(pl.multiple_of(order[k] * eighth, eighth), eighth), :] = near[here, :]
        out[pl.ds(pl.multiple_of(order[4 + k] * eighth, eighth), eighth), :] = far[here, :]


def middle_kernel(inner, own, near, swapped, own_square, near_square, swapped_square, *outs):
    rows, width = own.shape
    with_own, with_swapped = inner[:, :rows], inner[:, rows:2 * rows]
    for k, (out, over) in enumerate((outs[:2], outs[2:])):
        here = slice(k * width // 2, (k + 1) * width // 2)
        outward = dot_t(with_own, own[:, here]) + dot(with_swapped, swapped[:, here])
        square = own_square[:, here] + swapped_square[:, here]
        outward = outward - near[:, here].astype(jnp.float32) * square
        out[...] = outward.astype(jnp.bfloat16)
        across = dot_t(with_swapped, near[:, here])
        across = across - swapped[:, here].astype(jnp.float32) * near_square[:, here]
        over[...] = across.astype(jnp.bfloat16)


def coefficient(total):
    return 2.0 * total / (25.0 * (total - 1)) / (total - 1)


def held_kernel(
    total, middle, inner, own, near, z, other,
    own_square, near_square, third_square, mean, spread, held,
):
    rows, width = own.shape
    norm = jnp.sum(inner[:, 3 * rows:].astype(jnp.float32), axis=1, keepdims=True)
    for k in range(4):
        here = slice(k * width // 4, (k + 1) * width // 4)
        anchor = z[:, here].astype(jnp.float32)
        deviation = jnp.sqrt(spread[:, here] / (total - 1) + 0.0001)
        centered = anchor - mean[:, here]
        hinge = jnp.where(deviation < 1.0, centered / deviation, 0.0)
        plain = anchor - other[:, here].astype(jnp.float32) - total / (4.0 * (total - 1)) * hinge
        square = own_square[:, here] + third_square[:, here]
        product = dot(inner[:, 2 * rows:3 * rows], own[:, here])
        product = product + own[:, here].astype(jnp.float32) * (norm - square)
        held[:, here] = plain + coefficient(total) * product

    @pl.when(middle[0] == 1)
    def _():
        for k in range(4):
            here = slice(k * width // 4, (k + 1) * width // 4)
            product = dot(inner[:, :rows], near[:, here])
            product = product - own[:, here].astype(jnp.float32) * near_square[:, here]
            held[:, here] = held[:, here] + coefficient(total) * product


def last_kernel(total, middle, inner, third, held, out_a, over_a, out_b, over_b, result):
    width = third.shape[1]
    for here, out, over in (
        (slice(0, width // 2), out_a, over_a), (slice(width // 2, width), out_b, over_b)
    ):
        product = dot(inner[...], third[:, here])

        @pl.when(middle[0] == 1)
        def _():
            sums = product + over[...].astype(jnp.float32)
            result[:, here] = held[:, here] + coefficient(total) * sums

        @pl.when(middle[0] == 0)
        def _():
            sums = product + out[...].astype(jnp.float32)
            result[:, here] = held[:, here] + coefficient(total) * sums


def to_partner(x, step):
    return lax.ppermute(x, "feat", [(i, i ^ step) for i in range(8)])


def halve(kept, sent, last=0):
    half, n = kept.shape
    part = (half // 4, n)
    return kernel_call(
        functools.partial(add_kernel, last), [(part, jnp.float32)] + [(part, jnp.bfloat16)] * 3
    )(kept, to_partner(sent, 1))


def scatter(mine, *out, last=0):
    got = [to_partner(x, 2 * k) for k, x in enumerate(out, 1)]
    return kernel_call(functools.partial(total_kernel, last), [(mine.shape, jnp.bfloat16)])(
        mine, *got
    )[0]


def gather_rows(x, order, *others):
    near = after(jnp.concatenate([x] + [to_partner(x, 2 * k) for k in (1, 2, 3)]), *others)
    far = to_partner(near, 1)
    shape = (8 * x.shape[0], x.shape[1])
    return kernel_call(place_kernel, [(shape, jnp.bfloat16)], smem=1)(order, near, far)[0]


def after(x, *others):
    return lax.optimization_barrier((x, *others))[0]


def by_line(z_anchor, z_other):
    rows, width = z_anchor.shape
    total = rows * 4
    plane = lax.axis_index("dp")
    middle = ((plane == 1) | (plane == 2)).astype(jnp.int32).reshape(1)
    order = lax.axis_index("feat") ^ jnp.array([0, 2, 4, 6, 1, 3, 5, 7], jnp.int32)
    inward, across, outward = [(0, 1), (3, 2)], [(1, 2), (2, 1)], [(1, 0), (2, 3)]
    half = rows // 2
    flat, block = ((1, width), jnp.float32), ((rows, width), jnp.bfloat16)

    near = [lax.ppermute(z_anchor[:half], "dp", inward)]
    swapped = [lax.ppermute(z_anchor[:half], "dp", across)]
    anchor = z_anchor.astype(jnp.float32)
    sums = jnp.sum(anchor, axis=0, keepdims=True)
    apart = anchor - sums / rows
    stats = jnp.concatenate([sums, jnp.sum(apart * apart, axis=0, keepdims=True)])
    all_stats = [stats] + [
        lax.ppermute(stats, "dp", [(i, (i + k) % 4) for i in range(4)]) for k in (1, 2, 3)
    ]
    later = after(z_anchor[half:], *all_stats)
    end = lax.ppermute(after(z_anchor, *all_stats, near[0], swapped[0]), "dp", [(0, 3), (3, 0)])
    near.append(lax.ppermute(later, "dp", inward))
    swapped.append(lax.ppermute(later, "dp", across))
    mean = (all_stats[0][:1] + all_stats[1][:1] + all_stats[2][:1] + all_stats[3][:1]) / total
    spread = 0.0
    for one in all_stats:
        shift = one[:1] / rows - mean
        spread = spread + (one[1:] + rows * shift * shift)

    def summands(n):
        return [((half, n), jnp.float32), ((half, n), jnp.bfloat16)]

    own, turned, own_square, kept, sent = kernel_call(
        own_kernel, [block, block, flat, *summands(rows + NORM)], smem=1, scratch=12
    )(order, after(z_anchor, near[0], swapped[0]), mean)
    with_own = scatter(*halve(kept, sent, rows), last=rows)
    near, swapped, near_square, swapped_square, kept, sent, _ = kernel_call(
        first_kernel,
        [block, block, flat, flat, *summands(2 * rows), block],
        smem=1, scratch=12,
    )(order, after(turned, with_own), *near, *swapped, mean)
    first = scatter(*halve(kept, sent))
    first = gather_rows(jnp.concatenate([first, with_own], axis=1), order, end)

    part = ((rows, width // 2), jnp.bfloat16)
    ready = kernel_call(middle_kernel, [part] * 4, scratch=12)(
        first, own, near, swapped, own_square, near_square, swapped_square
    )
    pushed = [lax.ppermute(x, "dp", p) for x, p in zip(ready, (outward, across) * 2)]

    third, third_square, kept, sent = kernel_call(
        second_kernel, [block, flat, *summands(rows)], smem=1, scratch=12
    )(middle, after(turned, *ready), swapped, swapped_square, end, mean)
    halved = halve(kept, sent)
    result = ((rows, width), jnp.float32)
    held = kernel_call(functools.partial(held_kernel, total), [result], smem=1, scratch=12)(
        middle, first, own, near, z_anchor, z_other,
        own_square, near_square, after(third_square, halved[0]), mean, spread,
    )[0]
    second = gather_rows(after(scatter(*halved), *pushed[:2], held), order)
    return kernel_call(functools.partial(last_kernel, total), [result], smem=1, scratch=12)(
        middle, second, third, held, *pushed
    )[0]


def by_gather(z_anchor, z_other):
    rows_here, width = z_anchor.shape
    groups = lax.axis_size("dp")
    total = rows_here * groups
    mine = lax.axis_index("dp") * rows_here
    column = lax.all_gather(z_anchor, "dp", axis=0, tiled=True).astype(jnp.float32)
    mean = jnp.sum(column, axis=0) / total
    centered_all = column - mean
    variance = jnp.sum(centered_all * centered_all, axis=0) / (total - 1)
    rounded_all = centered_all.astype(jnp.bfloat16)
    widened = rounded_all.astype(jnp.float32)
    own_square = jnp.sum(widened * widened, axis=0)
    rounded = lax.dynamic_slice_in_dim(rounded_all, mine, rows_here, 0)
    inner = lax.psum(gram(rounded, rounded_all).astype(jnp.bfloat16), "feat")
    product = jnp.dot(inner, rounded_all, preferred_element_type=jnp.float32)
    product = product - rounded.astype(jnp.float32) * own_square
    return finish(z_anchor, z_other, mean, variance, total, product)


def finish(z_anchor, z_other, mean, variance, total, product):
    coef = 2.0 * total / (25.0 * (total - 1)) / (total - 1)
    anchor = z_anchor.astype(jnp.float32)
    centered = anchor - mean
    deviation = jnp.sqrt(variance + 0.0001)
    hinge = jnp.where(deviation < 1.0, centered / deviation, 0.0)
    factor = total / (4.0 * (total - 1))
    return anchor - z_other.astype(jnp.float32) - factor * hinge + coef * product


def solution(mesh):
    placed = (P("dp", "feat"), P("dp", "feat"))
    in_line = mesh.shape["dp"] == 4 and mesh.shape["feat"] == 8
    return jax.shard_map(
        by_line if in_line else by_gather,
        mesh=mesh, in_specs=placed, out_specs=P("dp", "feat"), check_vma=False,
    )
```

```python
import functools
import math

import jax
import jax.numpy as jnp
from jax import lax
from jax.experimental import pallas as pl
from jax.experimental.pallas import tpu as pltpu
from jax.sharding import PartitionSpec as P

NORM = 128


def kernel_call(body, outs, smem=0, scratch=4):
    def call(*args):
        space = [pltpu.SMEM] * smem + [pltpu.VMEM] * (len(args) - smem)
        return pl.pallas_call(
            body,
            out_shape=[jax.ShapeDtypeStruct(s, t) for s, t in outs],
            in_specs=[pl.BlockSpec(memory_space=m) for m in space],
            out_specs=[pl.BlockSpec(memory_space=pltpu.VMEM) for _ in outs],
            compiler_params=pltpu.CompilerParams(vmem_limit_bytes=scratch * 1024 * 1024),
            cost_estimate=pl.CostEstimate(flops=0, bytes_accessed=0, transcendentals=0),
        )(*args)

    return call


def gram(left, right):
    return lax.dot_general(
        left, right, (((1,), (1,)), ((), ())), preferred_element_type=jnp.float32
    )


def dot_t(left, right):
    return lax.dot_general(
        left, right, (((0,), (0,)), ((), ())), preferred_element_type=jnp.float32
    )


def dot(left, right):
    return jnp.dot(left, right, preferred_element_type=jnp.float32)


def centered_into(out, block, mean, square):
    out[...] = (block[...].astype(jnp.float32) - mean).astype(jnp.bfloat16)
    wide = out[...].astype(jnp.float32)
    square[...] = jnp.sum(wide * wide, axis=0, keepdims=True)


def high_low(n, like):
    high = n.astype(jnp.bfloat16).astype(jnp.float32)
    lane = lax.broadcasted_iota(jnp.int32, like, 1)
    return jnp.where(lane == 0, high, jnp.where(lane == 1, n - high, 0.0))


def turn_into(turned, order, block):
    eighth = block.shape[0] // 8
    for k in range(8):
        start = pl.multiple_of(order[k] * eighth, eighth)
        turned[k * eighth:(k + 1) * eighth, :] = block[pl.ds(start, eighth), :]


def own_kernel(order, z, mean, own, turned, square, kept, sent):
    rows = z.shape[0]
    eighth, half = rows // 8, rows // 2
    centered_into(own, z, mean[...], square)
    turn_into(turned, order, own)
    inner = gram(turned[...], own[...])
    wide = turned[...].astype(jnp.float32)
    norm = jnp.sum(wide * wide, axis=1, keepdims=True)
    column = lax.broadcasted_iota(jnp.int32, (eighth, rows), 1)
    row = lax.broadcasted_iota(jnp.int32, (eighth, rows), 0)
    for k in range(8):
        here = slice(k * eighth, (k + 1) * eighth)
        off = jnp.where(column == row + order[k] * eighth, 0.0, inner[here])
        if k < 4:
            kept[here, :rows] = off
        else:
            sent[k * eighth - half:(k + 1) * eighth - half, :rows] = off.astype(jnp.bfloat16)
    lane = lax.broadcasted_iota(jnp.int32, (half, NORM), 1)
    kept[:, rows:] = jnp.where(lane == 0, norm[:half], 0.0)
    sent[:, rows:] = high_low(norm[half:], (half, NORM)).astype(jnp.bfloat16)


def first_kernel(order, middle, turned, near_in, swapped_in, mean, *refs):
    near, swapped, near_square, swapped_square, kept, sent, turned_near = refs
    rows = near.shape[0]
    half = rows // 2

    @pl.when(middle[0] == 1)
    def _():
        centered_into(near, near_in, mean[...], near_square)
        centered_into(swapped, swapped_in, mean[...], swapped_square)
        turn_into(turned_near, order, near)
        for k, (left, right) in enumerate(((turned, near), (turned_near, swapped))):
            inner = gram(left[...], right[...])
            kept[:, k * rows:(k + 1) * rows] = inner[:half]
            sent[:, k * rows:(k + 1) * rows] = inner[half:].astype(jnp.bfloat16)

    @pl.when(middle[0] == 0)
    def _():
        for ref in refs[:-1]:
            ref[...] = jnp.zeros_like(ref)


def second_kernel(middle, turned, swapped, swapped_square, end, mean, third, square, kept, sent):
    half = third.shape[0] // 2

    @pl.when(middle[0] == 1)
    def _():
        third[...] = swapped[...]
        square[...] = swapped_square[...]

    @pl.when(middle[0] == 0)
    def _():
        centered_into(third, end, mean[...], square)

    inner = gram(turned[...], third[...])
    kept[...] = inner[:half]
    sent[...] = inner[half:].astype(jnp.bfloat16)


def with_norm(x, last):
    if not last:
        return x
    tail = x[:, last:]
    split = high_low(jnp.sum(tail, axis=1, keepdims=True), tail.shape)
    return jnp.concatenate([x[:, :last], split], axis=1)


def add_kernel(last, kept, got, mine, *out):
    total = with_norm(kept[...] + got[...].astype(jnp.float32), last)
    quarter = mine.shape[0]
    mine[...] = total[:quarter]
    for k, ref in enumerate(out, 1):
        ref[...] = total[k * quarter:(k + 1) * quarter].astype(jnp.bfloat16)


def total_kernel(last, mine, a, b, c, out):
    total = mine[...] + a[...].astype(jnp.float32)
    total = total + b[...].astype(jnp.float32) + c[...].astype(jnp.float32)
    out[...] = with_norm(total, last).astype(jnp.bfloat16)


def place_kernel(order, near, far, out):
    eighth = out.shape[0] // 8
    for k in range(4):
        here = slice(k * eighth, (k + 1) * eighth)
        out[pl.ds(pl.multiple_of(order[k] * eighth, eighth), eighth), :] = near[here, :]
        out[pl.ds(pl.multiple_of(order[4 + k] * eighth, eighth), eighth), :] = far[here, :]


def middle_kernel(
    middle, inner, own, near, swapped, own_square, near_square, swapped_square, out, over
):
    rows, width = own.shape

    @pl.when(middle[0] == 1)
    def _():
        with_own, with_swapped = inner[:, :rows], inner[:, rows:]
        for k in range(2):
            here = slice(k * width // 2, (k + 1) * width // 2)
            outward = dot_t(with_own, own[:, here]) + dot(with_swapped, swapped[:, here])
            square = own_square[:, here] + swapped_square[:, here]
            outward = outward - near[:, here].astype(jnp.float32) * square
            out[:, here] = outward.astype(jnp.bfloat16)
            across = dot_t(with_swapped, near[:, here])
            across = across - swapped[:, here].astype(jnp.float32) * near_square[:, here]
            over[:, here] = across.astype(jnp.bfloat16)

    @pl.when(middle[0] == 0)
    def _():
        out[...] = jnp.zeros_like(out)
        over[...] = jnp.zeros_like(over)


def coefficient(total):
    return 2.0 * total / (25.0 * (total - 1)) / (total - 1)


def held_kernel(
    total, middle, first, with_own, own, near, z, other,
    own_square, near_square, third_square, mean, spread, held,
):
    rows, width = own.shape
    norm = jnp.sum(with_own[:, rows:].astype(jnp.float32), axis=1, keepdims=True)
    for k in range(4):
        here = slice(k * width // 4, (k + 1) * width // 4)
        anchor = z[:, here].astype(jnp.float32)
        deviation = jnp.sqrt(spread[:, here] / (total - 1) + 0.0001)
        centered = anchor - mean[:, here]
        hinge = jnp.where(deviation < 1.0, centered / deviation, 0.0)
        plain = anchor - other[:, here].astype(jnp.float32) - total / (4.0 * (total - 1)) * hinge
        square = own_square[:, here] + third_square[:, here]
        product = dot(with_own[:, :rows], own[:, here])
        product = product + own[:, here].astype(jnp.float32) * (norm - square)
        held[:, here] = plain + coefficient(total) * product

    @pl.when(middle[0] == 1)
    def _():
        for k in range(4):
            here = slice(k * width // 4, (k + 1) * width // 4)
            product = dot(first[:, :rows], near[:, here])
            product = product - own[:, here].astype(jnp.float32) * near_square[:, here]
            held[:, here] = held[:, here] + coefficient(total) * product


def last_kernel(total, middle, inner, third, held, out, over, result):
    width = third.shape[1]

    def put(arrived):
        for k in range(4):
            here = slice(k * width // 4, (k + 1) * width // 4)
            product = dot(inner[...], third[:, here]) + arrived[:, here].astype(jnp.float32)
            result[:, here] = held[:, here] + coefficient(total) * product

    pl.when(middle[0] == 1)(lambda: put(over))
    pl.when(middle[0] == 0)(lambda: put(out))


def to_partner(x, step):
    return lax.ppermute(x, "feat", [(i, i ^ step) for i in range(8)])


def halve(kept, sent, last=0):
    half, n = kept.shape
    part = (half // 4, n)
    return kernel_call(
        functools.partial(add_kernel, last), [(part, jnp.float32)] + [(part, jnp.bfloat16)] * 3
    )(kept, to_partner(sent, 1))


def scatter(mine, *out, last=0):
    got = [to_partner(x, 2 * k) for k, x in enumerate(out, 1)]
    return kernel_call(functools.partial(total_kernel, last), [(mine.shape, jnp.bfloat16)])(
        mine, *got
    )[0]


def gather_chips(x):
    return jnp.concatenate([x] + [to_partner(x, 2 * k) for k in (1, 2, 3)])


def gather_cores(near, order, *others):
    far = after(to_partner(near, 1), *others)
    shape = (2 * near.shape[0], near.shape[1])
    return kernel_call(place_kernel, [(shape, jnp.bfloat16)], smem=1)(order, near, far)[0]


def after(x, *others):
    return lax.optimization_barrier((x, *others))[0]


def by_line(z_anchor, z_other):
    rows, width = z_anchor.shape
    total = rows * 4
    plane = lax.axis_index("dp")
    middle = ((plane == 1) | (plane == 2)).astype(jnp.int32).reshape(1)
    order = lax.axis_index("feat") ^ jnp.array([0, 2, 4, 6, 1, 3, 5, 7], jnp.int32)
    inward, across, outward = [(0, 1), (3, 2)], [(1, 2), (2, 1)], [(1, 0), (2, 3)]
    half = rows // 2
    flat, block = ((1, width), jnp.float32), ((rows, width), jnp.bfloat16)

    base = z_anchor[:1].astype(jnp.float32)
    apart = z_anchor.astype(jnp.float32) - base
    stats = jnp.concatenate(
        [jnp.sum(apart, axis=0, keepdims=True), jnp.sum(apart * apart, axis=0, keepdims=True)]
    )
    away = stats[:1] / rows
    stats = jnp.concatenate([base + away, stats[1:] - stats[:1] * away])
    all_stats = [stats] + [
        lax.ppermute(stats, "dp", [(i, (i + k) % 4) for i in range(4)]) for k in (1, 2, 3)
    ]
    ahead = after(z_anchor, stats)
    near = lax.ppermute(ahead, "dp", inward)
    swapped = lax.ppermute(ahead, "dp", across)
    end = lax.ppermute(ahead, "dp", [(0, 3), (3, 0)])
    mean = (all_stats[0][:1] + all_stats[1][:1] + all_stats[2][:1] + all_stats[3][:1]) / 4
    spread = 0.0
    for one in all_stats:
        shift = one[:1] - mean
        spread = spread + (one[1:] + rows * shift * shift)

    def summands(n):
        return [((half, n), jnp.float32), ((half, n), jnp.bfloat16)]

    own, turned, own_square, kept, sent = kernel_call(
        own_kernel, [block, block, flat, *summands(rows + NORM)], smem=1, scratch=12
    )(order, z_anchor, mean)
    with_own = gather_chips(scatter(*halve(kept, sent, rows), last=rows))
    near, swapped, near_square, swapped_square, kept, sent, _ = kernel_call(
        first_kernel,
        [block, block, flat, flat, *summands(2 * rows), block],
        smem=2, scratch=12,
    )(order, middle, after(turned, with_own), near, swapped, mean)
    with_own = gather_cores(with_own, order)
    first = gather_cores(gather_chips(scatter(*halve(kept, sent))), order, end)

    ready = kernel_call(middle_kernel, [block, block], smem=1, scratch=12)(
        middle, first, own, near, swapped, own_square, near_square, swapped_square
    )
    pushed = [lax.ppermute(x, "dp", p) for x, p in zip(ready, (outward, across))]

    third, third_square, kept, sent = kernel_call(
        second_kernel, [block, flat, *summands(rows)], smem=1, scratch=12
    )(middle, after(turned, *ready), swapped, swapped_square, end, mean)
    halved = halve(kept, sent)
    result = ((rows, width), jnp.float32)
    held = kernel_call(functools.partial(held_kernel, total), [result], smem=1, scratch=12)(
        middle, first, with_own, own, near, z_anchor, z_other,
        own_square, near_square, after(third_square, halved[0]), mean, spread,
    )[0]
    second = gather_chips(after(scatter(*halved), held))
    second = gather_cores(second, order, *pushed)
    return kernel_call(functools.partial(last_kernel, total), [result], smem=1, scratch=12)(
        middle, second, third, held, *pushed
    )[0]


def by_gather(z_anchor, z_other):
    rows_here, width = z_anchor.shape
    groups = lax.axis_size("dp")
    total = rows_here * groups
    mine = lax.axis_index("dp") * rows_here
    column = lax.all_gather(z_anchor, "dp", axis=0, tiled=True).astype(jnp.float32)
    mean = jnp.sum(column, axis=0) / total
    centered_all = column - mean
    variance = jnp.sum(centered_all * centered_all, axis=0) / (total - 1)
    rounded_all = centered_all.astype(jnp.bfloat16)
    widened = rounded_all.astype(jnp.float32)
    own_square = jnp.sum(widened * widened, axis=0)
    rounded = lax.dynamic_slice_in_dim(rounded_all, mine, rows_here, 0)
    inner = lax.psum(gram(rounded, rounded_all).astype(jnp.bfloat16), "feat")
    product = jnp.dot(inner, rounded_all, preferred_element_type=jnp.float32)
    product = product - rounded.astype(jnp.float32) * own_square
    return finish(z_anchor, z_other, mean, variance, total, product)


def finish(z_anchor, z_other, mean, variance, total, product):
    coef = 2.0 * total / (25.0 * (total - 1)) / (total - 1)
    anchor = z_anchor.astype(jnp.float32)
    centered = anchor - mean
    deviation = jnp.sqrt(variance + 0.0001)
    hinge = jnp.where(deviation < 1.0, centered / deviation, 0.0)
    factor = total / (4.0 * (total - 1))
    return anchor - z_other.astype(jnp.float32) - factor * hinge + coef * product


def solution(mesh):
    placed = (P("dp", "feat"), P("dp", "feat"))
    in_line = mesh.shape["dp"] == 4 and mesh.shape["feat"] == 8
    return jax.shard_map(
        by_line if in_line else by_gather,
        mesh=mesh, in_specs=placed, out_specs=P("dp", "feat"), check_vma=False,
    )
```

```python
import functools
import math

import jax
import jax.numpy as jnp
from jax import lax
from jax.experimental import pallas as pl
from jax.experimental.pallas import tpu as pltpu
from jax.sharding import PartitionSpec as P

NORM = 128


def kernel_call(body, outs, smem=0, scratch=4):
    def call(*args):
        space = [pltpu.SMEM] * smem + [pltpu.VMEM] * (len(args) - smem)
        return pl.pallas_call(
            body,
            out_shape=[jax.ShapeDtypeStruct(s, t) for s, t in outs],
            in_specs=[pl.BlockSpec(memory_space=m) for m in space],
            out_specs=[pl.BlockSpec(memory_space=pltpu.VMEM) for _ in outs],
            compiler_params=pltpu.CompilerParams(vmem_limit_bytes=scratch * 1024 * 1024),
            cost_estimate=pl.CostEstimate(flops=0, bytes_accessed=0, transcendentals=0),
        )(*args)

    return call


def gram(left, right):
    return lax.dot_general(
        left, right, (((1,), (1,)), ((), ())), preferred_element_type=jnp.float32
    )


def dot_t(left, right):
    return lax.dot_general(
        left, right, (((0,), (0,)), ((), ())), preferred_element_type=jnp.float32
    )


def dot(left, right):
    return jnp.dot(left, right, preferred_element_type=jnp.float32)


def centered_into(out, block, mean, square):
    out[...] = (block[...].astype(jnp.float32) - mean).astype(jnp.bfloat16)
    wide = out[...].astype(jnp.float32)
    square[...] = jnp.sum(wide * wide, axis=0, keepdims=True)


def high_low(n, like):
    high = n.astype(jnp.bfloat16).astype(jnp.float32)
    lane = lax.broadcasted_iota(jnp.int32, like, 1)
    return jnp.where(lane == 0, high, jnp.where(lane == 1, n - high, 0.0))


def turn_into(turned, order, block):
    eighth = block.shape[0] // 8
    for k in range(8):
        start = pl.multiple_of(order[k] * eighth, eighth)
        turned[k * eighth:(k + 1) * eighth, :] = block[pl.ds(start, eighth), :]


def own_kernel(order, z, mean, own, turned, square, kept, sent):
    rows = z.shape[0]
    eighth, half = rows // 8, rows // 2
    centered_into(own, z, mean[...], square)
    turn_into(turned, order, own)
    inner = gram(turned[...], own[...])
    wide = turned[...].astype(jnp.float32)
    norm = jnp.sum(wide * wide, axis=1, keepdims=True)
    column = lax.broadcasted_iota(jnp.int32, (eighth, rows), 1)
    row = lax.broadcasted_iota(jnp.int32, (eighth, rows), 0)
    for k in range(8):
        here = slice(k * eighth, (k + 1) * eighth)
        off = jnp.where(column == row + order[k] * eighth, 0.0, inner[here])
        if k < 4:
            kept[here, :rows] = off
        else:
            sent[k * eighth - half:(k + 1) * eighth - half, :rows] = off.astype(jnp.bfloat16)
    lane = lax.broadcasted_iota(jnp.int32, (half, NORM), 1)
    kept[:, rows:] = jnp.where(lane == 0, norm[:half], 0.0)
    sent[:, rows:] = high_low(norm[half:], (half, NORM)).astype(jnp.bfloat16)


def first_kernel(order, turned, beside_in, opposite_in, mean, *refs):
    beside, beside_square, kept, sent, opposite, turned_beside, unused = refs
    rows = beside.shape[0]
    half = rows // 2

    def put(left, right, k):
        inner = gram(left[...], right[...])
        kept[:, k * rows:(k + 1) * rows] = inner[:half]
        sent[:, k * rows:(k + 1) * rows] = inner[half:].astype(jnp.bfloat16)

    centered_into(beside, beside_in, mean[...], beside_square)
    put(turned, beside, 0)
    centered_into(opposite, opposite_in, mean[...], unused)
    turn_into(turned_beside, order, beside)
    put(turned_beside, opposite, 1)


def first_end_kernel(turned, beside_in, mean, beside, beside_square, kept, sent):
    half = beside.shape[0] // 2
    centered_into(beside, beside_in, mean[...], beside_square)
    inner = gram(turned[...], beside[...])
    kept[...] = inner[:half]
    sent[...] = inner[half:].astype(jnp.bfloat16)


def second_kernel(middle, turned, swapped, end, mean, opposite, square, kept, sent):
    half = opposite.shape[0] // 2

    @pl.when(middle[0] == 1)
    def _():
        centered_into(opposite, swapped, mean[...], square)

    @pl.when(middle[0] == 0)
    def _():
        centered_into(opposite, end, mean[...], square)

    inner = gram(turned[...], opposite[...])
    kept[...] = inner[:half]
    sent[...] = inner[half:].astype(jnp.bfloat16)


def with_norm(x, last):
    if not last:
        return x
    tail = x[:, last:]
    split = high_low(jnp.sum(tail, axis=1, keepdims=True), tail.shape)
    return jnp.concatenate([x[:, :last], split], axis=1)


def add_kernel(last, kept, got, mine, *out):
    total = with_norm(kept[...] + got[...].astype(jnp.float32), last)
    quarter = mine.shape[0]
    mine[...] = total[:quarter]
    for k, ref in enumerate(out, 1):
        ref[...] = total[k * quarter:(k + 1) * quarter].astype(jnp.bfloat16)


def total_kernel(last, mine, a, b, c, out):
    total = mine[...] + a[...].astype(jnp.float32)
    total = total + b[...].astype(jnp.float32) + c[...].astype(jnp.float32)
    out[...] = with_norm(total, last).astype(jnp.bfloat16)


def place_kernel(order, near, far, out):
    eighth = out.shape[0] // 8
    for k in range(4):
        here = slice(k * eighth, (k + 1) * eighth)
        out[pl.ds(pl.multiple_of(order[k] * eighth, eighth), eighth), :] = near[here, :]
        out[pl.ds(pl.multiple_of(order[4 + k] * eighth, eighth), eighth), :] = far[here, :]


def coefficient(total):
    return 2.0 * total / (25.0 * (total - 1)) / (total - 1)


def held_kernel(
    total, first, with_own, own, beside, z, other,
    own_square, beside_square, opposite_square, mean, spread, held,
):
    rows, width = own.shape
    norm = jnp.sum(with_own[:, rows:].astype(jnp.float32), axis=1, keepdims=True)
    for k in range(4):
        here = slice(k * width // 4, (k + 1) * width // 4)
        anchor = z[:, here].astype(jnp.float32)
        deviation = jnp.sqrt(spread[:, here] / (total - 1) + 0.0001)
        centered = anchor - mean[:, here]
        hinge = jnp.where(deviation < 1.0, centered / deviation, 0.0)
        plain = anchor - other[:, here].astype(jnp.float32) - total / (4.0 * (total - 1)) * hinge
        square = own_square[:, here] + beside_square[:, here] + opposite_square[:, here]
        product = dot(with_own[:, :rows], own[:, here])
        product = product + dot(first[:, :rows], beside[:, here])
        product = product + own[:, here].astype(jnp.float32) * (norm - square)
        held[:, here] = plain + coefficient(total) * product


def last_kernel(total, middle, first, second, opposite, own, held, mean, out, over, result):
    rows, width = own.shape

    def put(arrived, product_of):
        for k in range(4):
            here = slice(k * width // 4, (k + 1) * width // 4)
            block = (arrived[:, here].astype(jnp.float32) - mean[:, here]).astype(jnp.bfloat16)
            wide = block.astype(jnp.float32)
            square = jnp.sum(wide * wide, axis=0, keepdims=True)
            product = dot(second[...], opposite[:, here]) + product_of(first[:, rows:], block)
            product = product - own[:, here].astype(jnp.float32) * square
            result[:, here] = held[:, here] + coefficient(total) * product

    pl.when(middle[0] == 1)(lambda: put(over, dot_t))
    pl.when(middle[0] == 0)(lambda: put(out, dot))


def to_partner(x, step):
    return lax.ppermute(x, "feat", [(i, i ^ step) for i in range(8)])


def halve(kept, sent, last=0):
    half, n = kept.shape
    part = (half // 4, n)
    return kernel_call(
        functools.partial(add_kernel, last), [(part, jnp.float32)] + [(part, jnp.bfloat16)] * 3
    )(kept, to_partner(sent, 1))


def scatter(mine, *out, last=0):
    got = [to_partner(x, 2 * k) for k, x in enumerate(out, 1)]
    return kernel_call(functools.partial(total_kernel, last), [(mine.shape, jnp.bfloat16)])(
        mine, *got
    )[0]


def gather_chips(x):
    return jnp.concatenate([x] + [to_partner(x, 2 * k) for k in (1, 2, 3)])


def gather_cores(near, order, *others):
    far = after(to_partner(near, 1), *others)
    shape = (2 * near.shape[0], near.shape[1])
    return kernel_call(place_kernel, [(shape, jnp.bfloat16)], smem=1)(order, near, far)[0]


def after(x, *others):
    return lax.optimization_barrier((x, *others))[0]


def by_line(z_anchor, z_other):
    rows, width = z_anchor.shape
    total = rows * 4
    plane = lax.axis_index("dp")
    middle = ((plane == 1) | (plane == 2)).astype(jnp.int32).reshape(1)
    order = lax.axis_index("feat") ^ jnp.array([0, 2, 4, 6, 1, 3, 5, 7], jnp.int32)
    across, outward = [(1, 2), (2, 1)], [(1, 0), (2, 3)]
    half = rows // 2
    flat, block = ((1, width), jnp.float32), ((rows, width), jnp.bfloat16)

    base = z_anchor[:1].astype(jnp.float32)
    apart = z_anchor.astype(jnp.float32) - base
    stats = jnp.concatenate(
        [jnp.sum(apart, axis=0, keepdims=True), jnp.sum(apart * apart, axis=0, keepdims=True)]
    )
    away = stats[:1] / rows
    stats = jnp.concatenate([base + away, stats[1:] - stats[:1] * away])
    all_stats = [stats] + [
        lax.ppermute(stats, "dp", [(i, (i + k) % 4) for i in range(4)]) for k in (1, 2, 3)
    ]
    ahead = after(z_anchor, stats)
    beside_in = lax.ppermute(ahead, "dp", [(i, i ^ 1) for i in range(4)])
    swapped = lax.ppermute(ahead, "dp", across)
    end = lax.ppermute(ahead, "dp", [(0, 3), (3, 0)])
    mean = (all_stats[0][:1] + all_stats[1][:1] + all_stats[2][:1] + all_stats[3][:1]) / 4
    spread = 0.0
    for one in all_stats:
        shift = one[:1] - mean
        spread = spread + (one[1:] + rows * shift * shift)

    def summands(n):
        return [((half, n), jnp.float32), ((half, n), jnp.bfloat16)]

    own, turned, own_square, kept, sent = kernel_call(
        own_kernel, [block, block, flat, *summands(rows + NORM)], smem=1, scratch=12
    )(order, z_anchor, mean)
    with_own = gather_chips(scatter(*halve(kept, sent, rows), last=rows))

    def on_middle(order, turned, beside_in, swapped, mean):
        beside, square, kept, sent, *_ = kernel_call(
            first_kernel,
            [block, flat, *summands(2 * rows), block, block, flat], smem=1, scratch=12,
        )(order, turned, beside_in, swapped, mean)
        return beside, square, scatter(*halve(kept, sent))

    def on_end(order, turned, beside_in, swapped, mean):
        beside, square, kept, sent = kernel_call(
            first_end_kernel, [block, flat, *summands(rows)], scratch=12
        )(turned, beside_in, mean)
        first = scatter(*halve(kept, sent))
        return beside, square, jnp.concatenate([first, jnp.zeros_like(first)], axis=1)

    beside, beside_square, first = lax.cond(
        middle[0] == 1, on_middle, on_end,
        order, after(turned, with_own), beside_in, swapped, mean,
    )
    with_own = gather_cores(with_own, order)
    handed = [lax.ppermute(first[:, rows:], "dp", p) for p in (outward, across)]
    out = lax.ppermute(after(swapped, first), "dp", outward)
    over = lax.ppermute(after(beside_in, first), "dp", across)
    first = jnp.concatenate([first[:, :rows], handed[0] + handed[1]], axis=1)
    first = gather_chips(first)

    opposite, opposite_square, kept, sent = kernel_call(
        second_kernel, [block, flat, *summands(rows)], smem=1, scratch=12
    )(middle, after(turned, first), swapped, end, mean)
    first = gather_cores(first, order)
    halved = halve(kept, sent)
    result = ((rows, width), jnp.float32)
    held = kernel_call(functools.partial(held_kernel, total), [result], scratch=12)(
        first, with_own, own, beside, z_anchor, z_other,
        own_square, beside_square, after(opposite_square, halved[0]), mean, spread,
    )[0]
    second = after(gather_chips(after(scatter(*halved), held)), out, over)
    second = gather_cores(second, order)
    return kernel_call(functools.partial(last_kernel, total), [result], smem=1, scratch=12)(
        middle, first, second, opposite, own, held, mean, out, over
    )[0]


def by_gather(z_anchor, z_other):
    rows_here, width = z_anchor.shape
    groups = lax.axis_size("dp")
    total = rows_here * groups
    mine = lax.axis_index("dp") * rows_here
    column = lax.all_gather(z_anchor, "dp", axis=0, tiled=True).astype(jnp.float32)
    mean = jnp.sum(column, axis=0) / total
    centered_all = column - mean
    variance = jnp.sum(centered_all * centered_all, axis=0) / (total - 1)
    rounded_all = centered_all.astype(jnp.bfloat16)
    widened = rounded_all.astype(jnp.float32)
    own_square = jnp.sum(widened * widened, axis=0)
    rounded = lax.dynamic_slice_in_dim(rounded_all, mine, rows_here, 0)
    inner = lax.psum(gram(rounded, rounded_all).astype(jnp.bfloat16), "feat")
    product = jnp.dot(inner, rounded_all, preferred_element_type=jnp.float32)
    product = product - rounded.astype(jnp.float32) * own_square
    return finish(z_anchor, z_other, mean, variance, total, product)


def finish(z_anchor, z_other, mean, variance, total, product):
    coef = 2.0 * total / (25.0 * (total - 1)) / (total - 1)
    anchor = z_anchor.astype(jnp.float32)
    centered = anchor - mean
    deviation = jnp.sqrt(variance + 0.0001)
    hinge = jnp.where(deviation < 1.0, centered / deviation, 0.0)
    factor = total / (4.0 * (total - 1))
    return anchor - z_other.astype(jnp.float32) - factor * hinge + coef * product


def solution(mesh):
    placed = (P("dp", "feat"), P("dp", "feat"))
    in_line = mesh.shape["dp"] == 4 and mesh.shape["feat"] == 8
    return jax.shard_map(
        by_line if in_line else by_gather,
        mesh=mesh, in_specs=placed, out_specs=P("dp", "feat"), check_vma=False,
    )
```

```python
import functools
import math

import jax
import jax.numpy as jnp
from jax import lax
from jax.experimental import pallas as pl
from jax.experimental.pallas import tpu as pltpu
from jax.sharding import PartitionSpec as P

NORM = 128


def kernel_call(body, outs, smem=0, scratch=4):
    def call(*args):
        space = [pltpu.SMEM] * smem + [pltpu.VMEM] * (len(args) - smem)
        return pl.pallas_call(
            body,
            out_shape=[jax.ShapeDtypeStruct(s, t) for s, t in outs],
            in_specs=[pl.BlockSpec(memory_space=m) for m in space],
            out_specs=[pl.BlockSpec(memory_space=pltpu.VMEM) for _ in outs],
            compiler_params=pltpu.CompilerParams(vmem_limit_bytes=scratch * 1024 * 1024),
            cost_estimate=pl.CostEstimate(flops=0, bytes_accessed=0, transcendentals=0),
        )(*args)

    return call


def gram(left, right):
    return lax.dot_general(
        left, right, (((1,), (1,)), ((), ())), preferred_element_type=jnp.float32
    )


def dot_t(left, right):
    return lax.dot_general(
        left, right, (((0,), (0,)), ((), ())), preferred_element_type=jnp.float32
    )


def dot(left, right):
    return jnp.dot(left, right, preferred_element_type=jnp.float32)


def centered_into(out, block, mean, square):
    out[...] = (block[...].astype(jnp.float32) - mean).astype(jnp.bfloat16)
    wide = out[...].astype(jnp.float32)
    square[...] = jnp.sum(wide * wide, axis=0, keepdims=True)


def high_low(n, like):
    high = n.astype(jnp.bfloat16).astype(jnp.float32)
    lane = lax.broadcasted_iota(jnp.int32, like, 1)
    return jnp.where(lane == 0, high, jnp.where(lane == 1, n - high, 0.0))


def turn_into(turned, order, block):
    eighth = block.shape[0] // 8
    for k in range(8):
        start = pl.multiple_of(order[k] * eighth, eighth)
        turned[k * eighth:(k + 1) * eighth, :] = block[pl.ds(start, eighth), :]


def own_kernel(order, z, mean, own, turned, square, kept, sent):
    rows = z.shape[0]
    eighth, half = rows // 8, rows // 2
    centered_into(own, z, mean[...], square)
    turn_into(turned, order, own)
    inner = gram(turned[...], own[...])
    wide = turned[...].astype(jnp.float32)
    norm = jnp.sum(wide * wide, axis=1, keepdims=True)
    column = lax.broadcasted_iota(jnp.int32, (eighth, rows), 1)
    row = lax.broadcasted_iota(jnp.int32, (eighth, rows), 0)
    for k in range(8):
        here = slice(k * eighth, (k + 1) * eighth)
        off = jnp.where(column == row + order[k] * eighth, 0.0, inner[here])
        if k < 4:
            kept[here, :rows] = off
        else:
            sent[k * eighth - half:(k + 1) * eighth - half, :rows] = off.astype(jnp.bfloat16)
    lane = lax.broadcasted_iota(jnp.int32, (half, NORM), 1)
    kept[:, rows:] = jnp.where(lane == 0, norm[:half], 0.0)
    sent[:, rows:] = high_low(norm[half:], (half, NORM)).astype(jnp.bfloat16)


def split_sum(inner, kept, sent, here):
    half = kept.shape[0]
    kept[:, here] = inner[:half]
    sent[:, here] = inner[half:].astype(jnp.bfloat16)


def middle_kernel(
    order, turned, beside_in, opposite_in, mean,
    beside, beside_square, opposite, opposite_square, kept, sent, turned_beside,
):
    rows = beside.shape[0]
    centered_into(beside, beside_in, mean[...], beside_square)
    split_sum(gram(turned[...], beside[...]), kept, sent, slice(0, rows))
    centered_into(opposite, opposite_in, mean[...], opposite_square)
    split_sum(gram(turned[...], opposite[...]), kept, sent, slice(rows, 2 * rows))
    turn_into(turned_beside, order, beside)
    split_sum(gram(turned_beside[...], opposite[...]), kept, sent, slice(2 * rows, 3 * rows))


def block_kernel(turned, block_in, mean, block, square, kept, sent):
    centered_into(block, block_in, mean[...], square)
    split_sum(gram(turned[...], block[...]), kept, sent, slice(None))


def stats_kernel(z, out):
    rows = z.shape[0]
    base = z[:16, :].astype(jnp.float32)[:1]
    apart = z[...].astype(jnp.float32) - base
    total = jnp.sum(apart, axis=0, keepdims=True)
    away = total / rows
    out[:1, :] = base + away
    out[1:, :] = jnp.sum(apart * apart, axis=0, keepdims=True) - total * away


def with_norm(x, last):
    if not last:
        return x
    tail = x[:, last:]
    split = high_low(jnp.sum(tail, axis=1, keepdims=True), tail.shape)
    return jnp.concatenate([x[:, :last], split], axis=1)


def add_kernel(last, kept, got, mine, *out):
    total = with_norm(kept[...] + got[...].astype(jnp.float32), last)
    quarter = mine.shape[0]
    mine[...] = total[:quarter]
    for k, ref in enumerate(out, 1):
        ref[...] = total[k * quarter:(k + 1) * quarter].astype(jnp.bfloat16)


def total_kernel(last, mine, a, b, c, out):
    total = mine[...] + a[...].astype(jnp.float32)
    total = total + b[...].astype(jnp.float32) + c[...].astype(jnp.float32)
    out[...] = with_norm(total, last).astype(jnp.bfloat16)


def place_kernel(order, near, far, out):
    eighth = out.shape[0] // 8
    for k in range(4):
        here = slice(k * eighth, (k + 1) * eighth)
        out[pl.ds(pl.multiple_of(order[k] * eighth, eighth), eighth), :] = near[here, :]
        out[pl.ds(pl.multiple_of(order[4 + k] * eighth, eighth), eighth), :] = far[here, :]


def coefficient(total):
    return 2.0 * total / (25.0 * (total - 1)) / (total - 1)


def held_kernel(
    total, with_own, own, z, other,
    own_square, beside_square, opposite_square, mean, spread, held,
):
    rows, width = own.shape
    norm = jnp.sum(with_own[:, rows:].astype(jnp.float32), axis=1, keepdims=True)
    for k in range(4):
        here = slice(k * width // 4, (k + 1) * width // 4)
        anchor = z[:, here].astype(jnp.float32)
        deviation = jnp.sqrt(spread[:, here] / (total - 1) + 0.0001)
        centered = anchor - mean[:, here]
        hinge = jnp.where(deviation < 1.0, centered / deviation, 0.0)
        plain = anchor - other[:, here].astype(jnp.float32) - total / (4.0 * (total - 1)) * hinge
        square = own_square[:, here] + beside_square[:, here] + opposite_square[:, here]
        product = dot(with_own[:, :rows], own[:, here])
        product = product + own[:, here].astype(jnp.float32) * (norm - square)
        held[:, here] = plain + coefficient(total) * product


def last_kernel(total, middle, inner, beside, opposite, own, held, mean, out, over, result):
    rows, width = own.shape

    def put(arrived, product_of):
        for k in range(4):
            here = slice(k * width // 4, (k + 1) * width // 4)
            block = (arrived[:, here].astype(jnp.float32) - mean[:, here]).astype(jnp.bfloat16)
            wide = block.astype(jnp.float32)
            square = jnp.sum(wide * wide, axis=0, keepdims=True)
            product = dot(inner[:, :rows], beside[:, here])
            product = product + dot(inner[:, rows:2 * rows], opposite[:, here])
            product = product + product_of(inner[:, 2 * rows:], block)
            product = product - own[:, here].astype(jnp.float32) * square
            result[:, here] = held[:, here] + coefficient(total) * product

    pl.when(middle[0] == 1)(lambda: put(over, dot_t))
    pl.when(middle[0] == 0)(lambda: put(out, dot))


def to_partner(x, step):
    return lax.ppermute(x, "feat", [(i, i ^ step) for i in range(8)])


def halve(kept, sent, last=0):
    half, n = kept.shape
    part = (half // 4, n)
    return kernel_call(
        functools.partial(add_kernel, last), [(part, jnp.float32)] + [(part, jnp.bfloat16)] * 3
    )(kept, to_partner(sent, 1))


def scatter(mine, *out, last=0):
    got = [to_partner(x, 2 * k) for k, x in enumerate(out, 1)]
    return kernel_call(functools.partial(total_kernel, last), [(mine.shape, jnp.bfloat16)])(
        mine, *got
    )[0]


def gather_chips(x):
    return jnp.concatenate([x] + [to_partner(x, 2 * k) for k in (1, 2, 3)])


def gather_cores(near, order, *others):
    far = after(to_partner(near, 1), *others)
    shape = (2 * near.shape[0], near.shape[1])
    return kernel_call(place_kernel, [(shape, jnp.bfloat16)], smem=1)(order, near, far)[0]


def after(x, *others):
    return lax.optimization_barrier((x, *others))[0]


def by_line(z_anchor, z_other):
    rows, width = z_anchor.shape
    total = rows * 4
    plane = lax.axis_index("dp")
    middle = ((plane == 1) | (plane == 2)).astype(jnp.int32).reshape(1)
    order = lax.axis_index("feat") ^ jnp.array([0, 2, 4, 6, 1, 3, 5, 7], jnp.int32)
    across, outward = [(1, 2), (2, 1)], [(1, 0), (2, 3)]
    half = rows // 2
    flat, block = ((1, width), jnp.float32), ((rows, width), jnp.bfloat16)

    stats = kernel_call(stats_kernel, [((2, width), jnp.float32)], scratch=12)(z_anchor)[0]
    all_stats = [stats] + [
        lax.ppermute(stats, "dp", [(i, (i + k) % 4) for i in range(4)]) for k in (1, 2, 3)
    ]
    ahead = after(z_anchor, *all_stats)
    beside_in = lax.ppermute(ahead, "dp", [(i, i ^ 1) for i in range(4)])
    swapped = lax.ppermute(ahead, "dp", across)
    mean = (all_stats[0][:1] + all_stats[1][:1] + all_stats[2][:1] + all_stats[3][:1]) / 4
    spread = 0.0
    for one in all_stats:
        shift = one[:1] - mean
        spread = spread + (one[1:] + rows * shift * shift)

    def summands(n):
        return [((half, n), jnp.float32), ((half, n), jnp.bfloat16)]

    own, turned, own_square, kept, sent = kernel_call(
        own_kernel, [block, block, flat, *summands(rows + NORM)], smem=1, scratch=12
    )(order, z_anchor, mean)
    with_own = gather_cores(gather_chips(scatter(*halve(kept, sent, rows), last=rows)), order)

    end = lax.ppermute(after(z_anchor, beside_in, swapped, with_own), "dp", [(0, 3), (3, 0)])

    def first_of_middle(order, turned, beside_in, swapped, mean):
        *blocks, kept, sent, _ = kernel_call(
            middle_kernel, [block, flat, block, flat, *summands(3 * rows), block],
            smem=1, scratch=12,
        )(order, turned, beside_in, swapped, mean)
        return *blocks, scatter(*halve(kept, sent))

    def first_of_end(order, turned, beside_in, swapped, mean):
        beside, square, kept, sent = kernel_call(
            block_kernel, [block, flat, *summands(rows)], scratch=12
        )(turned, beside_in, mean)
        first = scatter(*halve(kept, sent))
        first = jnp.concatenate([first, jnp.zeros((rows // 8, 2 * rows), first.dtype)], axis=1)
        return beside, square, swapped, jnp.zeros_like(square), first

    beside, beside_square, opposite, opposite_square, first = lax.cond(
        middle[0] == 1, first_of_middle, first_of_end,
        order, after(turned, with_own), beside_in, swapped, mean,
    )
    handed = [lax.ppermute(first[:, 2 * rows:], "dp", p) for p in (outward, across)]
    out = lax.ppermute(after(swapped, *handed), "dp", outward)
    over = lax.ppermute(after(beside_in, *handed), "dp", across)
    handed = handed[0] + handed[1]
    result = ((rows, width), jnp.float32)

    def hold(opposite_square):
        return kernel_call(functools.partial(held_kernel, total), [result], scratch=12)(
            with_own, own, z_anchor, z_other,
            own_square, beside_square, opposite_square, mean, spread,
        )[0]

    def second_of_middle(turned, end, opposite, opposite_square, first, handed):
        inner = jnp.concatenate([first[:, :2 * rows], handed], axis=1)
        return opposite, gather_chips(inner), hold(opposite_square)

    def second_of_end(turned, end, opposite, opposite_square, first, handed):
        opposite, opposite_square, kept, sent = kernel_call(
            block_kernel, [block, flat, *summands(rows)], scratch=12
        )(turned, end, mean)
        inner = scatter(*halve(kept, sent))
        inner = jnp.concatenate([first[:, :rows], inner, handed], axis=1)
        return opposite, gather_chips(inner), hold(opposite_square)

    opposite, inner, held = lax.cond(
        middle[0] == 1, second_of_middle, second_of_end,
        turned, end, opposite, opposite_square, first, handed,
    )
    inner = gather_cores(inner, order, out, over)
    return kernel_call(functools.partial(last_kernel, total), [result], smem=1, scratch=12)(
        middle, inner, beside, opposite, own, held, mean, out, over
    )[0]


def by_gather(z_anchor, z_other):
    rows_here, width = z_anchor.shape
    groups = lax.axis_size("dp")
    total = rows_here * groups
    mine = lax.axis_index("dp") * rows_here
    column = lax.all_gather(z_anchor, "dp", axis=0, tiled=True).astype(jnp.float32)
    mean = jnp.sum(column, axis=0) / total
    centered_all = column - mean
    variance = jnp.sum(centered_all * centered_all, axis=0) / (total - 1)
    rounded_all = centered_all.astype(jnp.bfloat16)
    widened = rounded_all.astype(jnp.float32)
    own_square = jnp.sum(widened * widened, axis=0)
    rounded = lax.dynamic_slice_in_dim(rounded_all, mine, rows_here, 0)
    inner = lax.psum(gram(rounded, rounded_all).astype(jnp.bfloat16), "feat")
    product = jnp.dot(inner, rounded_all, preferred_element_type=jnp.float32)
    product = product - rounded.astype(jnp.float32) * own_square
    return finish(z_anchor, z_other, mean, variance, total, product)


def finish(z_anchor, z_other, mean, variance, total, product):
    coef = 2.0 * total / (25.0 * (total - 1)) / (total - 1)
    anchor = z_anchor.astype(jnp.float32)
    centered = anchor - mean
    deviation = jnp.sqrt(variance + 0.0001)
    hinge = jnp.where(deviation < 1.0, centered / deviation, 0.0)
    factor = total / (4.0 * (total - 1))
    return anchor - z_other.astype(jnp.float32) - factor * hinge + coef * product


def solution(mesh):
    placed = (P("dp", "feat"), P("dp", "feat"))
    in_line = mesh.shape["dp"] == 4 and mesh.shape["feat"] == 8
    return jax.shard_map(
        by_line if in_line else by_gather,
        mesh=mesh, in_specs=placed, out_specs=P("dp", "feat"), check_vma=False,
    )
```

```python
import functools
import math

import jax
import jax.numpy as jnp
from jax import lax
from jax.experimental import pallas as pl
from jax.experimental.pallas import tpu as pltpu
from jax.sharding import PartitionSpec as P

NORM = 128


def kernel_call(body, outs, smem=0, scratch=4):
    def call(*args):
        space = [pltpu.SMEM] * smem + [pltpu.VMEM] * (len(args) - smem)
        return pl.pallas_call(
            body,
            out_shape=[jax.ShapeDtypeStruct(s, t) for s, t in outs],
            in_specs=[pl.BlockSpec(memory_space=m) for m in space],
            out_specs=[pl.BlockSpec(memory_space=pltpu.VMEM) for _ in outs],
            compiler_params=pltpu.CompilerParams(vmem_limit_bytes=scratch * 1024 * 1024),
            cost_estimate=pl.CostEstimate(flops=0, bytes_accessed=0, transcendentals=0),
        )(*args)

    return call


def gram(left, right):
    return lax.dot_general(
        left, right, (((1,), (1,)), ((), ())), preferred_element_type=jnp.float32
    )


def dot_t(left, right):
    return lax.dot_general(
        left, right, (((0,), (0,)), ((), ())), preferred_element_type=jnp.float32
    )


def dot(left, right):
    return jnp.dot(left, right, preferred_element_type=jnp.float32)


def centered_into(out, block, mean, square):
    out[...] = (block[...].astype(jnp.float32) - mean).astype(jnp.bfloat16)
    wide = out[...].astype(jnp.float32)
    square[...] = jnp.sum(wide * wide, axis=0, keepdims=True)


def high_low(n, like):
    high = n.astype(jnp.bfloat16).astype(jnp.float32)
    lane = lax.broadcasted_iota(jnp.int32, like, 1)
    return jnp.where(lane == 0, high, jnp.where(lane == 1, n - high, 0.0))


def turn_into(turned, order, block):
    eighth = block.shape[0] // 8
    for k in range(8):
        start = pl.multiple_of(order[k] * eighth, eighth)
        turned[k * eighth:(k + 1) * eighth, :] = block[pl.ds(start, eighth), :]


def own_kernel(order, z, mean, own, turned, square, kept, sent):
    rows = z.shape[0]
    eighth, half = rows // 8, rows // 2
    centered_into(own, z, mean[...], square)
    turn_into(turned, order, own)
    inner = gram(turned[...], own[...])
    wide = turned[...].astype(jnp.float32)
    norm = jnp.sum(wide * wide, axis=1, keepdims=True)
    column = lax.broadcasted_iota(jnp.int32, (eighth, rows), 1)
    row = lax.broadcasted_iota(jnp.int32, (eighth, rows), 0)
    for k in range(8):
        here = slice(k * eighth, (k + 1) * eighth)
        off = jnp.where(column == row + order[k] * eighth, 0.0, inner[here])
        if k < 4:
            kept[here, :rows] = off
        else:
            sent[k * eighth - half:(k + 1) * eighth - half, :rows] = off.astype(jnp.bfloat16)
    lane = lax.broadcasted_iota(jnp.int32, (half, NORM), 1)
    kept[:, rows:] = jnp.where(lane == 0, norm[:half], 0.0)
    sent[:, rows:] = high_low(norm[half:], (half, NORM)).astype(jnp.bfloat16)


def split_sum(inner, kept, sent, here):
    half = kept.shape[0]
    kept[:, here] = inner[:half]
    sent[:, here] = inner[half:].astype(jnp.bfloat16)


def middle_kernel(
    order, beside_in, opposite_in, mean,
    beside, beside_square, opposite, opposite_square, kept, sent, turned_beside,
):
    centered_into(beside, beside_in, mean[...], beside_square)
    centered_into(opposite, opposite_in, mean[...], opposite_square)
    turn_into(turned_beside, order, beside)
    split_sum(gram(turned_beside[...], opposite[...]), kept, sent, slice(None))


def both_kernel(turned, beside, opposite, kept, sent):
    rows = beside.shape[0]
    split_sum(gram(turned[...], beside[...]), kept, sent, slice(0, rows))
    split_sum(gram(turned[...], opposite[...]), kept, sent, slice(rows, 2 * rows))


def block_kernel(turned, block_in, mean, block, square, kept, sent):
    centered_into(block, block_in, mean[...], square)
    split_sum(gram(turned[...], block[...]), kept, sent, slice(None))


def stats_kernel(z, out):
    rows = z.shape[0]
    base = z[:16, :].astype(jnp.float32)[:1]
    apart = z[...].astype(jnp.float32) - base
    total = jnp.sum(apart, axis=0, keepdims=True)
    away = total / rows
    out[:1, :] = base + away
    out[1:, :] = jnp.sum(apart * apart, axis=0, keepdims=True) - total * away


def with_norm(x, last):
    if not last:
        return x
    tail = x[:, last:]
    split = high_low(jnp.sum(tail, axis=1, keepdims=True), tail.shape)
    return jnp.concatenate([x[:, :last], split], axis=1)


def add_kernel(last, kept, got, out):
    total = with_norm(kept[...] + got[...].astype(jnp.float32), last).astype(jnp.bfloat16)
    quarter = out.shape[1]
    for k in range(4):
        out[k] = total[k * quarter:(k + 1) * quarter]


def total_kernel(last, got, out):
    total = got[0].astype(jnp.float32)
    for k in range(1, 4):
        total = total + got[k].astype(jnp.float32)
    out[...] = with_norm(total, last).astype(jnp.bfloat16)


def place_kernel(order, near, far, out):
    eighth = out.shape[0] // 8
    for k in range(4):
        here = slice(k * eighth, (k + 1) * eighth)
        out[pl.ds(pl.multiple_of(order[k] * eighth, eighth), eighth), :] = near[here, :]
        out[pl.ds(pl.multiple_of(order[4 + k] * eighth, eighth), eighth), :] = far[here, :]


def coefficient(total):
    return 2.0 * total / (25.0 * (total - 1)) / (total - 1)


def held_kernel(
    total, with_own, own, z, other,
    own_square, beside_square, opposite_square, mean, spread, held,
):
    rows, width = own.shape
    norm = jnp.sum(with_own[:, rows:].astype(jnp.float32), axis=1, keepdims=True)
    for k in range(4):
        here = slice(k * width // 4, (k + 1) * width // 4)
        anchor = z[:, here].astype(jnp.float32)
        deviation = jnp.sqrt(spread[:, here] / (total - 1) + 0.0001)
        centered = anchor - mean[:, here]
        hinge = jnp.where(deviation < 1.0, centered / deviation, 0.0)
        plain = anchor - other[:, here].astype(jnp.float32) - total / (4.0 * (total - 1)) * hinge
        square = own_square[:, here] + beside_square[:, here] + opposite_square[:, here]
        product = dot(with_own[:, :rows], own[:, here])
        product = product + own[:, here].astype(jnp.float32) * (norm - square)
        held[:, here] = plain + coefficient(total) * product


def last_kernel(total, middle, inner, beside, opposite, own, held, mean, out, over, result):
    rows, width = own.shape

    def put(arrived, product_of):
        for k in range(4):
            here = slice(k * width // 4, (k + 1) * width // 4)
            block = (arrived[:, here].astype(jnp.float32) - mean[:, here]).astype(jnp.bfloat16)
            wide = block.astype(jnp.float32)
            square = jnp.sum(wide * wide, axis=0, keepdims=True)
            product = dot(inner[:, :rows], beside[:, here])
            product = product + dot(inner[:, rows:2 * rows], opposite[:, here])
            product = product + product_of(inner[:, 2 * rows:], block)
            product = product - own[:, here].astype(jnp.float32) * square
            result[:, here] = held[:, here] + coefficient(total) * product

    pl.when(middle[0] == 1)(lambda: put(over, dot_t))
    pl.when(middle[0] == 0)(lambda: put(out, dot))


def to_other_core(x):
    return lax.ppermute(x, "feat", [(i, i ^ 1) for i in range(8)])


def over_chips(x):
    return lax.all_to_all(
        x, "feat", 0, 0, axis_index_groups=[[0, 2, 4, 6], [1, 3, 5, 7]], tiled=True
    )


def scatter_sum(kept, sent, last=0):
    half, n = kept.shape
    part = (half // 4, n)
    out = kernel_call(functools.partial(add_kernel, last), [((4, *part), jnp.bfloat16)])(
        kept, to_other_core(sent)
    )[0]
    return kernel_call(functools.partial(total_kernel, last), [(part, jnp.bfloat16)])(
        over_chips(out)
    )[0]


def gather_chips(x):
    out = over_chips(jnp.broadcast_to(x[None], (4, *x.shape)))
    return out.reshape(4 * x.shape[0], x.shape[1])


def gather_cores(near, order, *others):
    far = after(to_other_core(near), *others)
    shape = (2 * near.shape[0], near.shape[1])
    return kernel_call(place_kernel, [(shape, jnp.bfloat16)], smem=1)(order, near, far)[0]


def after(x, *others):
    return lax.optimization_barrier((x, *others))[0]


def by_line(z_anchor, z_other):
    rows, width = z_anchor.shape
    total = rows * 4
    plane = lax.axis_index("dp")
    middle = ((plane == 1) | (plane == 2)).astype(jnp.int32).reshape(1)
    core, chips = lax.axis_index("feat") % 2, jnp.array([0, 2, 4, 6], jnp.int32)
    order = jnp.concatenate([chips + core, chips + 1 - core])
    across, outward = [(1, 2), (2, 1)], [(1, 0), (2, 3)]
    half = rows // 2
    flat, block = ((1, width), jnp.float32), ((rows, width), jnp.bfloat16)

    stats = kernel_call(stats_kernel, [((2, width), jnp.float32)], scratch=12)(z_anchor)[0]
    all_stats = [stats] + [
        lax.ppermute(stats, "dp", [(i, (i + k) % 4) for i in range(4)]) for k in (1, 2, 3)
    ]
    ahead = after(z_anchor, stats)
    beside_in = lax.ppermute(ahead, "dp", [(i, i ^ 1) for i in range(4)])
    swapped = lax.ppermute(ahead, "dp", across)
    mean = (all_stats[0][:1] + all_stats[1][:1] + all_stats[2][:1] + all_stats[3][:1]) / 4
    spread = 0.0
    for one in all_stats:
        shift = one[:1] - mean
        spread = spread + (one[1:] + rows * shift * shift)

    def summands(n):
        return [((half, n), jnp.float32), ((half, n), jnp.bfloat16)]

    own, turned, own_square, kept, sent = kernel_call(
        own_kernel, [block, block, flat, *summands(rows + NORM)], smem=1, scratch=12
    )(order, z_anchor, mean)
    near_own = gather_chips(scatter_sum(kept, sent, rows))

    end = lax.ppermute(after(z_anchor, beside_in, swapped, near_own), "dp", [(0, 3), (3, 0)])
    with_own = gather_cores(after(near_own, beside_in, swapped), order)

    def first_of_middle(turned, beside_in, swapped, mean):
        *blocks, kept, sent, _ = kernel_call(
            middle_kernel, [block, flat, block, flat, *summands(rows), block],
            smem=1, scratch=12,
        )(order, beside_in, swapped, mean)
        return *blocks, scatter_sum(kept, sent)

    def first_of_end(turned, beside_in, swapped, mean):
        beside, square, kept, sent = kernel_call(
            block_kernel, [block, flat, *summands(rows)], scratch=12
        )(turned, beside_in, mean)
        return beside, square, swapped, jnp.zeros_like(square), scatter_sum(kept, sent)

    beside, beside_square, opposite, opposite_square, first = lax.cond(
        middle[0] == 1, first_of_middle, first_of_end,
        after(turned, near_own), beside_in, swapped, mean,
    )
    handed = [lax.ppermute(first, "dp", p) for p in (outward, across)]
    out = lax.ppermute(after(swapped, *handed), "dp", outward)
    over = lax.ppermute(after(beside_in, *handed), "dp", across)
    handed = handed[0] + handed[1]
    result = ((rows, width), jnp.float32)

    def hold(opposite_square):
        return kernel_call(functools.partial(held_kernel, total), [result], scratch=12)(
            with_own, own, z_anchor, z_other,
            own_square, beside_square, opposite_square, mean, spread,
        )[0]

    def second_of_middle(turned, end, opposite, opposite_square, first, handed):
        kept, sent = kernel_call(both_kernel, summands(2 * rows), scratch=12)(
            turned, beside, opposite
        )
        inner = jnp.concatenate([scatter_sum(kept, sent), handed], axis=1)
        return opposite, gather_chips(inner), hold(opposite_square)

    def second_of_end(turned, end, opposite, opposite_square, first, handed):
        opposite, opposite_square, kept, sent = kernel_call(
            block_kernel, [block, flat, *summands(rows)], scratch=12
        )(turned, end, mean)
        inner = jnp.concatenate([first, scatter_sum(kept, sent), handed], axis=1)
        return opposite, gather_chips(inner), hold(opposite_square)

    opposite, inner, held = lax.cond(
        middle[0] == 1, second_of_middle, second_of_end,
        turned, end, opposite, opposite_square, first, handed,
    )
    inner = gather_cores(inner, order, out, over)
    return kernel_call(functools.partial(last_kernel, total), [result], smem=1, scratch=12)(
        middle, inner, beside, opposite, own, held, mean, out, over
    )[0]


def by_gather(z_anchor, z_other):
    rows_here, width = z_anchor.shape
    groups = lax.axis_size("dp")
    total = rows_here * groups
    mine = lax.axis_index("dp") * rows_here
    column = lax.all_gather(z_anchor, "dp", axis=0, tiled=True).astype(jnp.float32)
    mean = jnp.sum(column, axis=0) / total
    centered_all = column - mean
    variance = jnp.sum(centered_all * centered_all, axis=0) / (total - 1)
    rounded_all = centered_all.astype(jnp.bfloat16)
    widened = rounded_all.astype(jnp.float32)
    own_square = jnp.sum(widened * widened, axis=0)
    rounded = lax.dynamic_slice_in_dim(rounded_all, mine, rows_here, 0)
    inner = lax.psum(gram(rounded, rounded_all).astype(jnp.bfloat16), "feat")
    product = jnp.dot(inner, rounded_all, preferred_element_type=jnp.float32)
    product = product - rounded.astype(jnp.float32) * own_square
    return finish(z_anchor, z_other, mean, variance, total, product)


def finish(z_anchor, z_other, mean, variance, total, product):
    coef = 2.0 * total / (25.0 * (total - 1)) / (total - 1)
    anchor = z_anchor.astype(jnp.float32)
    centered = anchor - mean
    deviation = jnp.sqrt(variance + 0.0001)
    hinge = jnp.where(deviation < 1.0, centered / deviation, 0.0)
    factor = total / (4.0 * (total - 1))
    return anchor - z_other.astype(jnp.float32) - factor * hinge + coef * product


def solution(mesh):
    placed = (P("dp", "feat"), P("dp", "feat"))
    in_line = mesh.shape["dp"] == 4 and mesh.shape["feat"] == 8
    return jax.shard_map(
        by_line if in_line else by_gather,
        mesh=mesh, in_specs=placed, out_specs=P("dp", "feat"), check_vma=False,
    )
```

```python
import functools
import math

import jax
import jax.numpy as jnp
from jax import lax
from jax.experimental import pallas as pl
from jax.experimental.pallas import tpu as pltpu
from jax.sharding import PartitionSpec as P

NORM = 128


def kernel_call(body, outs, smem=0, scratch=4):
    def call(*args):
        space = [pltpu.SMEM] * smem + [pltpu.VMEM] * (len(args) - smem)
        return pl.pallas_call(
            body,
            out_shape=[jax.ShapeDtypeStruct(s, t) for s, t in outs],
            in_specs=[pl.BlockSpec(memory_space=m) for m in space],
            out_specs=[pl.BlockSpec(memory_space=pltpu.VMEM) for _ in outs],
            compiler_params=pltpu.CompilerParams(vmem_limit_bytes=scratch * 1024 * 1024),
            cost_estimate=pl.CostEstimate(flops=0, bytes_accessed=0, transcendentals=0),
        )(*args)

    return call


def gram(left, right):
    return lax.dot_general(
        left, right, (((1,), (1,)), ((), ())), preferred_element_type=jnp.float32
    )


def dot_t(left, right):
    return lax.dot_general(
        left, right, (((0,), (0,)), ((), ())), preferred_element_type=jnp.float32
    )


def dot(left, right):
    return jnp.dot(left, right, preferred_element_type=jnp.float32)


def centered_into(out, block, mean, square):
    out[...] = (block[...].astype(jnp.float32) - mean).astype(jnp.bfloat16)
    wide = out[...].astype(jnp.float32)
    square[...] = jnp.sum(wide * wide, axis=0, keepdims=True)


def high_low(n, like):
    high = n.astype(jnp.bfloat16).astype(jnp.float32)
    lane = lax.broadcasted_iota(jnp.int32, like, 1)
    return jnp.where(lane == 0, high, jnp.where(lane == 1, n - high, 0.0))


def turn_into(turned, order, block):
    eighth = block.shape[0] // 8
    for k in range(8):
        start = pl.multiple_of(order[k] * eighth, eighth)
        turned[k * eighth:(k + 1) * eighth, :] = block[pl.ds(start, eighth), :]


def own_kernel(order, z, mean, own, turned, square, kept, sent):
    rows = z.shape[0]
    eighth, half = rows // 8, rows // 2
    centered_into(own, z, mean[...], square)
    turn_into(turned, order, own)
    inner = gram(turned[...], own[...])
    wide = turned[...].astype(jnp.float32)
    norm = jnp.sum(wide * wide, axis=1, keepdims=True)
    column = lax.broadcasted_iota(jnp.int32, (eighth, rows), 1)
    row = lax.broadcasted_iota(jnp.int32, (eighth, rows), 0)
    for k in range(8):
        here = slice(k * eighth, (k + 1) * eighth)
        off = jnp.where(column == row + order[k] * eighth, 0.0, inner[here])
        if k < 4:
            kept[here, :rows] = off
        else:
            sent[k * eighth - half:(k + 1) * eighth - half, :rows] = off.astype(jnp.bfloat16)
    lane = lax.broadcasted_iota(jnp.int32, (half, NORM), 1)
    kept[:, rows:] = jnp.where(lane == 0, norm[:half], 0.0)
    sent[:, rows:] = high_low(norm[half:], (half, NORM)).astype(jnp.bfloat16)


def split_sum(inner, kept, sent, here):
    half = kept.shape[0]
    kept[:, here] = inner[:half]
    sent[:, here] = inner[half:].astype(jnp.bfloat16)


def middle_kernel(
    order, beside_in, opposite_in, mean,
    beside, beside_square, opposite, opposite_square, kept, sent, turned_beside,
):
    centered_into(beside, beside_in, mean[...], beside_square)
    centered_into(opposite, opposite_in, mean[...], opposite_square)
    turn_into(turned_beside, order, beside)
    split_sum(gram(turned_beside[...], opposite[...]), kept, sent, slice(None))


def both_kernel(turned, beside, opposite, kept, sent):
    rows = beside.shape[0]
    split_sum(gram(turned[...], beside[...]), kept, sent, slice(0, rows))
    split_sum(gram(turned[...], opposite[...]), kept, sent, slice(rows, 2 * rows))


def block_kernel(turned, block_in, mean, block, square, kept, sent):
    centered_into(block, block_in, mean[...], square)
    split_sum(gram(turned[...], block[...]), kept, sent, slice(None))


def stats_kernel(z, out):
    rows = z.shape[0]
    base = z[:16, :].astype(jnp.float32)[:1]
    apart = z[...].astype(jnp.float32) - base
    total = jnp.sum(apart, axis=0, keepdims=True)
    away = total / rows
    out[:1, :] = base + away
    out[1:, :] = jnp.sum(apart * apart, axis=0, keepdims=True) - total * away


def with_norm(x, last):
    if not last:
        return x
    tail = x[:, last:]
    split = high_low(jnp.sum(tail, axis=1, keepdims=True), tail.shape)
    return jnp.concatenate([x[:, :last], split], axis=1)


def add_kernel(last, kept, got, mine, *out):
    total = with_norm(kept[...] + got[...].astype(jnp.float32), last)
    quarter = mine.shape[0]
    mine[...] = total[:quarter]
    for k, ref in enumerate(out, 1):
        ref[...] = total[k * quarter:(k + 1) * quarter].astype(jnp.bfloat16)


def total_kernel(last, mine, a, b, c, out):
    total = mine[...] + a[...].astype(jnp.float32)
    total = total + b[...].astype(jnp.float32) + c[...].astype(jnp.float32)
    out[...] = with_norm(total, last).astype(jnp.bfloat16)


def place_kernel(order, near, far, *outs):
    rows, width = outs[0].shape
    eighth = rows // 8
    for n, out in enumerate(outs):
        columns = slice(n * width, (n + 1) * width)
        for k in range(4):
            here = slice(k * eighth, (k + 1) * eighth)
            start = pl.multiple_of(order[k] * eighth, eighth)
            out[pl.ds(start, eighth), :] = near[here, columns]
            start = pl.multiple_of(order[4 + k] * eighth, eighth)
            out[pl.ds(start, eighth), :] = far[here, columns]


def push_kernel(inner, beside, opposite, beside_square, opposite_square, out, over):
    width = beside.shape[1]
    for k in range(2):
        here = slice(k * width // 2, (k + 1) * width // 2)
        outward = dot(inner[...], opposite[:, here])
        outward = outward - beside[:, here].astype(jnp.float32) * opposite_square[:, here]
        out[:, here] = outward.astype(jnp.bfloat16)
        across = dot_t(inner[...], beside[:, here])
        across = across - opposite[:, here].astype(jnp.float32) * beside_square[:, here]
        over[:, here] = across.astype(jnp.bfloat16)


def coefficient(total):
    return 2.0 * total / (25.0 * (total - 1)) / (total - 1)


def held_kernel(
    total, with_own, own, z, other,
    own_square, beside_square, opposite_square, mean, spread, held,
):
    rows, width = own.shape
    norm = jnp.sum(with_own[:, rows:].astype(jnp.float32), axis=1, keepdims=True)
    for k in range(4):
        here = slice(k * width // 4, (k + 1) * width // 4)
        anchor = z[:, here].astype(jnp.float32)
        deviation = jnp.sqrt(spread[:, here] / (total - 1) + 0.0001)
        centered = anchor - mean[:, here]
        hinge = jnp.where(deviation < 1.0, centered / deviation, 0.0)
        plain = anchor - other[:, here].astype(jnp.float32) - total / (4.0 * (total - 1)) * hinge
        square = own_square[:, here] + beside_square[:, here] + opposite_square[:, here]
        product = dot(with_own[:, :rows], own[:, here])
        product = product + own[:, here].astype(jnp.float32) * (norm - square)
        held[:, here] = plain + coefficient(total) * product


def last_kernel(
    total, middle, with_beside, with_opposite, beside, opposite, held, out, over, result
):
    width = beside.shape[1]

    def put(arrived):
        for k in range(4):
            here = slice(k * width // 4, (k + 1) * width // 4)
            product = dot(with_beside[...], beside[:, here])
            product = product + dot(with_opposite[...], opposite[:, here])
            product = product + arrived[:, here].astype(jnp.float32)
            result[:, here] = held[:, here] + coefficient(total) * product

    pl.when(middle[0] == 1)(lambda: put(over))
    pl.when(middle[0] == 0)(lambda: put(out))


def to_partner(x, step):
    return lax.ppermute(x, "feat", [(i, i ^ step) for i in range(8)])


def scatter_sum(kept, sent, last=0):
    half, n = kept.shape
    part = (half // 4, n)
    mine, *out = kernel_call(
        functools.partial(add_kernel, last), [(part, jnp.float32)] + [(part, jnp.bfloat16)] * 3
    )(kept, to_partner(sent, 1))
    got = [to_partner(x, 2 * k) for k, x in enumerate(out, 1)]
    return kernel_call(functools.partial(total_kernel, last), [(part, jnp.bfloat16)])(
        mine, *got
    )[0]


def gather_chips(x):
    return jnp.concatenate([x] + [to_partner(x, 2 * k) for k in (1, 2, 3)])


def gather_cores(near, order, parts=1):
    shape = (2 * near.shape[0], near.shape[1] // parts)
    return kernel_call(place_kernel, [(shape, jnp.bfloat16)] * parts, smem=1)(
        order, near, to_partner(near, 1)
    )


def after(x, *others):
    return lax.optimization_barrier((x, *others))[0]


def by_line(z_anchor, z_other):
    rows, width = z_anchor.shape
    total = rows * 4
    plane = lax.axis_index("dp")
    middle = ((plane == 1) | (plane == 2)).astype(jnp.int32).reshape(1)
    order = lax.axis_index("feat") ^ jnp.array([0, 2, 4, 6, 1, 3, 5, 7], jnp.int32)
    across, outward = [(1, 2), (2, 1)], [(1, 0), (2, 3)]
    half = rows // 2
    flat, block = ((1, width), jnp.float32), ((rows, width), jnp.bfloat16)

    stats = kernel_call(stats_kernel, [((2, width), jnp.float32)], scratch=12)(z_anchor)[0]
    all_stats = [stats] + [
        lax.ppermute(stats, "dp", [(i, (i + k) % 4) for i in range(4)]) for k in (1, 2, 3)
    ]
    ahead = after(z_anchor, stats)
    beside_in = lax.ppermute(ahead, "dp", [(i, i ^ 1) for i in range(4)])
    swapped = lax.ppermute(ahead, "dp", across)
    mean = (all_stats[0][:1] + all_stats[1][:1] + all_stats[2][:1] + all_stats[3][:1]) / 4
    spread = 0.0
    for one in all_stats:
        shift = one[:1] - mean
        spread = spread + (one[1:] + rows * shift * shift)

    def summands(n):
        return [((half, n), jnp.float32), ((half, n), jnp.bfloat16)]

    own, turned, own_square, kept, sent = kernel_call(
        own_kernel, [block, block, flat, *summands(rows + NORM)], smem=1, scratch=12
    )(order, z_anchor, mean)
    near_own = gather_chips(scatter_sum(kept, sent, rows))

    end = lax.ppermute(after(z_anchor, beside_in, swapped, near_own), "dp", [(0, 3), (3, 0)])
    with_own = gather_cores(after(near_own, beside_in, swapped), order)[0]

    def first_of_middle(turned, beside_in, swapped):
        *blocks, kept, sent, _ = kernel_call(
            middle_kernel, [block, flat, block, flat, *summands(rows), block],
            smem=1, scratch=12,
        )(order, beside_in, swapped, mean)
        inner = gather_cores(gather_chips(scatter_sum(kept, sent)), order)[0]
        beside, beside_square, opposite, opposite_square = blocks
        out, over = kernel_call(push_kernel, [block, block], scratch=12)(
            inner, beside, opposite, beside_square, opposite_square
        )
        return *blocks, inner, out, over

    def first_of_end(turned, beside_in, swapped):
        beside, square, kept, sent = kernel_call(
            block_kernel, [block, flat, *summands(rows)], scratch=12
        )(turned, beside_in, mean)
        inner = gather_cores(gather_chips(scatter_sum(kept, sent)), order)[0]
        return beside, square, swapped, jnp.zeros_like(square), inner, swapped, swapped

    beside, beside_square, opposite, opposite_square, first, *ready = lax.cond(
        middle[0] == 1, first_of_middle, first_of_end,
        after(turned, near_own), beside_in, swapped,
    )
    out, over = (lax.ppermute(x, "dp", p) for x, p in zip(ready, (outward, across)))
    result = ((rows, width), jnp.float32)

    def hold(opposite_square):
        return kernel_call(functools.partial(held_kernel, total), [result], scratch=12)(
            with_own, own, z_anchor, z_other,
            own_square, beside_square, opposite_square, mean, spread,
        )[0]

    def second_of_middle(turned, end, opposite, opposite_square, first):
        kept, sent = kernel_call(both_kernel, summands(2 * rows), scratch=12)(
            turned, beside, opposite
        )
        inner = gather_cores(gather_chips(scatter_sum(kept, sent)), order, 2)
        return opposite, *inner, hold(opposite_square)

    def second_of_end(turned, end, opposite, opposite_square, first):
        opposite, opposite_square, kept, sent = kernel_call(
            block_kernel, [block, flat, *summands(rows)], scratch=12
        )(turned, end, mean)
        inner = gather_cores(gather_chips(scatter_sum(kept, sent)), order)
        return opposite, first, *inner, hold(opposite_square)

    opposite, with_beside, with_opposite, held = lax.cond(
        middle[0] == 1, second_of_middle, second_of_end,
        after(turned, *ready), end, opposite, opposite_square, first,
    )
    return kernel_call(functools.partial(last_kernel, total), [result], smem=1, scratch=12)(
        middle, with_beside, with_opposite, beside, opposite, held, out, over
    )[0]


def by_gather(z_anchor, z_other):
    rows_here, width = z_anchor.shape
    groups = lax.axis_size("dp")
    total = rows_here * groups
    mine = lax.axis_index("dp") * rows_here
    column = lax.all_gather(z_anchor, "dp", axis=0, tiled=True).astype(jnp.float32)
    mean = jnp.sum(column, axis=0) / total
    centered_all = column - mean
    variance = jnp.sum(centered_all * centered_all, axis=0) / (total - 1)
    rounded_all = centered_all.astype(jnp.bfloat16)
    widened = rounded_all.astype(jnp.float32)
    own_square = jnp.sum(widened * widened, axis=0)
    rounded = lax.dynamic_slice_in_dim(rounded_all, mine, rows_here, 0)
    inner = lax.psum(gram(rounded, rounded_all).astype(jnp.bfloat16), "feat")
    product = jnp.dot(inner, rounded_all, preferred_element_type=jnp.float32)
    product = product - rounded.astype(jnp.float32) * own_square
    return finish(z_anchor, z_other, mean, variance, total, product)


def finish(z_anchor, z_other, mean, variance, total, product):
    coef = 2.0 * total / (25.0 * (total - 1)) / (total - 1)
    anchor = z_anchor.astype(jnp.float32)
    centered = anchor - mean
    deviation = jnp.sqrt(variance + 0.0001)
    hinge = jnp.where(deviation < 1.0, centered / deviation, 0.0)
    factor = total / (4.0 * (total - 1))
    return anchor - z_other.astype(jnp.float32) - factor * hinge + coef * product


def solution(mesh):
    placed = (P("dp", "feat"), P("dp", "feat"))
    in_line = mesh.shape["dp"] == 4 and mesh.shape["feat"] == 8
    return jax.shard_map(
        by_line if in_line else by_gather,
        mesh=mesh, in_specs=placed, out_specs=P("dp", "feat"), check_vma=False,
    )
```

```python
import functools
import math

import jax
import jax.numpy as jnp
from jax import lax
from jax.experimental import pallas as pl
from jax.experimental.pallas import tpu as pltpu
from jax.sharding import PartitionSpec as P

NORM = 128


def kernel_call(body, outs, smem=0, scratch=4):
    def call(*args):
        space = [pltpu.SMEM] * smem + [pltpu.VMEM] * (len(args) - smem)
        return pl.pallas_call(
            body,
            out_shape=[jax.ShapeDtypeStruct(s, t) for s, t in outs],
            in_specs=[pl.BlockSpec(memory_space=m) for m in space],
            out_specs=[pl.BlockSpec(memory_space=pltpu.VMEM) for _ in outs],
            compiler_params=pltpu.CompilerParams(vmem_limit_bytes=scratch * 1024 * 1024),
            cost_estimate=pl.CostEstimate(flops=0, bytes_accessed=0, transcendentals=0),
        )(*args)

    return call


def gram(left, right):
    return lax.dot_general(
        left, right, (((1,), (1,)), ((), ())), preferred_element_type=jnp.float32
    )


def dot_t(left, right):
    return lax.dot_general(
        left, right, (((0,), (0,)), ((), ())), preferred_element_type=jnp.float32
    )


def dot(left, right):
    return jnp.dot(left, right, preferred_element_type=jnp.float32)


def centered_into(out, block, mean, square):
    out[...] = (block[...].astype(jnp.float32) - mean).astype(jnp.bfloat16)
    wide = out[...].astype(jnp.float32)
    square[...] = jnp.sum(wide * wide, axis=0, keepdims=True)


def high_low(n, like):
    high = n.astype(jnp.bfloat16).astype(jnp.float32)
    lane = lax.broadcasted_iota(jnp.int32, like, 1)
    return jnp.where(lane == 0, high, jnp.where(lane == 1, n - high, 0.0))


def turn_into(turned, order, block):
    eighth = block.shape[0] // 8
    for k in range(8):
        start = pl.multiple_of(order[k] * eighth, eighth)
        turned[k * eighth:(k + 1) * eighth, :] = block[pl.ds(start, eighth), :]


def own_kernel(order, z, mean, own, turned, square, kept, sent):
    rows = z.shape[0]
    eighth, half = rows // 8, rows // 2
    centered_into(own, z, mean[...], square)
    turn_into(turned, order, own)
    inner = gram(turned[...], own[...])
    wide = turned[...].astype(jnp.float32)
    norm = jnp.sum(wide * wide, axis=1, keepdims=True)
    column = lax.broadcasted_iota(jnp.int32, (eighth, rows), 1)
    row = lax.broadcasted_iota(jnp.int32, (eighth, rows), 0)
    for k in range(8):
        here = slice(k * eighth, (k + 1) * eighth)
        off = jnp.where(column == row + order[k] * eighth, 0.0, inner[here])
        if k < 4:
            kept[here, :rows] = off
        else:
            sent[k * eighth - half:(k + 1) * eighth - half, :rows] = off.astype(jnp.bfloat16)
    lane = lax.broadcasted_iota(jnp.int32, (half, NORM), 1)
    kept[:, rows:] = jnp.where(lane == 0, norm[:half], 0.0)
    sent[:, rows:] = high_low(norm[half:], (half, NORM)).astype(jnp.bfloat16)


def split_sum(inner, kept, sent, here):
    half = kept.shape[0]
    kept[:, here] = inner[:half]
    sent[:, here] = inner[half:].astype(jnp.bfloat16)


def first_kernel(
    order, middle, turned, beside_in, opposite_in, mean,
    beside, beside_square, opposite, opposite_square, kept, sent, turned_beside,
):
    centered_into(beside, beside_in, mean[...], beside_square)

    @pl.when(middle[0] == 1)
    def _():
        centered_into(opposite, opposite_in, mean[...], opposite_square)
        turn_into(turned_beside, order, beside)
        split_sum(gram(turned_beside[...], opposite[...]), kept, sent, slice(None))

    @pl.when(middle[0] == 0)
    def _():
        split_sum(gram(turned[...], beside[...]), kept, sent, slice(None))


def second_kernel(
    middle, turned, beside, swapped, swapped_square, end, mean, opposite, square, kept, sent
):
    rows = opposite.shape[0]

    @pl.when(middle[0] == 1)
    def _():
        opposite[...] = swapped[...]
        square[...] = swapped_square[...]
        split_sum(gram(turned[...], beside[...]), kept, sent, slice(rows, 2 * rows))

    @pl.when(middle[0] == 0)
    def _():
        centered_into(opposite, end, mean[...], square)
        kept[:, rows:] = jnp.zeros_like(kept[:, rows:])
        sent[:, rows:] = jnp.zeros_like(sent[:, rows:])

    split_sum(gram(turned[...], opposite[...]), kept, sent, slice(0, rows))


def stats_kernel(z, out):
    rows = z.shape[0]
    base = z[:16, :].astype(jnp.float32)[:1]
    apart = z[...].astype(jnp.float32) - base
    total = jnp.sum(apart, axis=0, keepdims=True)
    away = total / rows
    out[:1, :] = base + away
    out[1:, :] = jnp.sum(apart * apart, axis=0, keepdims=True) - total * away


def with_norm(x, last):
    if not last:
        return x
    tail = x[:, last:]
    split = high_low(jnp.sum(tail, axis=1, keepdims=True), tail.shape)
    return jnp.concatenate([x[:, :last], split], axis=1)


def add_kernel(last, kept, got, mine, *out):
    total = with_norm(kept[...] + got[...].astype(jnp.float32), last)
    quarter = mine.shape[0]
    mine[...] = total[:quarter]
    for k, ref in enumerate(out, 1):
        ref[...] = total[k * quarter:(k + 1) * quarter].astype(jnp.bfloat16)


def total_kernel(last, mine, a, b, c, out):
    total = mine[...] + a[...].astype(jnp.float32)
    total = total + b[...].astype(jnp.float32) + c[...].astype(jnp.float32)
    out[...] = with_norm(total, last).astype(jnp.bfloat16)


def place_kernel(order, near, far, out):
    eighth = out.shape[0] // 8
    for k in range(4):
        here = slice(k * eighth, (k + 1) * eighth)
        out[pl.ds(pl.multiple_of(order[k] * eighth, eighth), eighth), :] = near[here, :]
        out[pl.ds(pl.multiple_of(order[4 + k] * eighth, eighth), eighth), :] = far[here, :]


def push_kernel(middle, inner, beside, opposite, beside_square, opposite_square, out, over):
    width = beside.shape[1]

    @pl.when(middle[0] == 1)
    def _():
        for k in range(2):
            here = slice(k * width // 2, (k + 1) * width // 2)
            outward = dot(inner[...], opposite[:, here])
            outward = outward - beside[:, here].astype(jnp.float32) * opposite_square[:, here]
            out[:, here] = outward.astype(jnp.bfloat16)
            across = dot_t(inner[...], beside[:, here])
            across = across - opposite[:, here].astype(jnp.float32) * beside_square[:, here]
            over[:, here] = across.astype(jnp.bfloat16)


def coefficient(total):
    return 2.0 * total / (25.0 * (total - 1)) / (total - 1)


def held_kernel(
    total, with_own, own, z, other,
    own_square, beside_square, opposite_square, mean, spread, held,
):
    rows, width = own.shape
    norm = jnp.sum(with_own[:, rows:].astype(jnp.float32), axis=1, keepdims=True)
    for k in range(4):
        here = slice(k * width // 4, (k + 1) * width // 4)
        anchor = z[:, here].astype(jnp.float32)
        deviation = jnp.sqrt(spread[:, here] / (total - 1) + 0.0001)
        centered = anchor - mean[:, here]
        hinge = jnp.where(deviation < 1.0, centered / deviation, 0.0)
        plain = anchor - other[:, here].astype(jnp.float32) - total / (4.0 * (total - 1)) * hinge
        square = own_square[:, here] + beside_square[:, here] + opposite_square[:, here]
        product = dot(with_own[:, :rows], own[:, here])
        product = product + own[:, here].astype(jnp.float32) * (norm - square)
        held[:, here] = plain + coefficient(total) * product


def last_kernel(total, middle, first, second, beside, opposite, held, out, over, result):
    rows, width = beside.shape

    def put(with_beside, arrived):
        for k in range(4):
            here = slice(k * width // 4, (k + 1) * width // 4)
            product = dot(with_beside, beside[:, here])
            product = product + dot(second[:, :rows], opposite[:, here])
            product = product + arrived[:, here].astype(jnp.float32)
            result[:, here] = held[:, here] + coefficient(total) * product

    pl.when(middle[0] == 1)(lambda: put(second[:, rows:], over))
    pl.when(middle[0] == 0)(lambda: put(first[...], out))


def to_partner(x, step):
    return lax.ppermute(x, "feat", [(i, i ^ step) for i in range(8)])


def halve(kept, sent, last=0):
    half, n = kept.shape
    part = (half // 4, n)
    return kernel_call(
        functools.partial(add_kernel, last), [(part, jnp.float32)] + [(part, jnp.bfloat16)] * 3
    )(kept, to_partner(sent, 1))


def scatter(mine, *out, last=0):
    got = [to_partner(x, 2 * k) for k, x in enumerate(out, 1)]
    return kernel_call(functools.partial(total_kernel, last), [(mine.shape, jnp.bfloat16)])(
        mine, *got
    )[0]


def gather_chips(x):
    return jnp.concatenate([x] + [to_partner(x, 2 * k) for k in (1, 2, 3)])


def gather_cores(near, order, *others):
    far = after(to_partner(near, 1), *others)
    shape = (2 * near.shape[0], near.shape[1])
    return kernel_call(place_kernel, [(shape, jnp.bfloat16)], smem=1)(order, near, far)[0]


def after(x, *others):
    return lax.optimization_barrier((x, *others))[0]


def by_line(z_anchor, z_other):
    rows, width = z_anchor.shape
    total = rows * 4
    plane = lax.axis_index("dp")
    middle = ((plane == 1) | (plane == 2)).astype(jnp.int32).reshape(1)
    order = lax.axis_index("feat") ^ jnp.array([0, 2, 4, 6, 1, 3, 5, 7], jnp.int32)
    across, outward = [(1, 2), (2, 1)], [(1, 0), (2, 3)]
    half = rows // 2
    flat, block = ((1, width), jnp.float32), ((rows, width), jnp.bfloat16)

    stats = kernel_call(stats_kernel, [((2, width), jnp.float32)], scratch=12)(z_anchor)[0]
    all_stats = [stats] + [
        lax.ppermute(stats, "dp", [(i, (i + k) % 4) for i in range(4)]) for k in (1, 2, 3)
    ]
    ahead = after(z_anchor, stats)
    beside_in = lax.ppermute(ahead, "dp", [(i, i ^ 1) for i in range(4)])
    swapped = lax.ppermute(ahead, "dp", across)
    mean = (all_stats[0][:1] + all_stats[1][:1] + all_stats[2][:1] + all_stats[3][:1]) / 4
    spread = 0.0
    for one in all_stats:
        shift = one[:1] - mean
        spread = spread + (one[1:] + rows * shift * shift)

    def summands(n):
        return [((half, n), jnp.float32), ((half, n), jnp.bfloat16)]

    own, turned, own_square, kept, sent = kernel_call(
        own_kernel, [block, block, flat, *summands(rows + NORM)], smem=1, scratch=12
    )(order, z_anchor, mean)
    near_own = gather_chips(scatter(*halve(kept, sent, rows), last=rows))
    end = lax.ppermute(after(z_anchor, beside_in, swapped, near_own), "dp", [(0, 3), (3, 0)])

    beside, beside_square, swapped, swapped_square, kept, sent, _ = kernel_call(
        first_kernel, [block, flat, block, flat, *summands(rows), block], smem=2, scratch=12
    )(order, middle, after(turned, near_own), beside_in, swapped, mean)
    with_own = gather_cores(near_own, order)
    first = gather_cores(gather_chips(scatter(*halve(kept, sent))), order, end)
    ready = kernel_call(push_kernel, [block, block], smem=1, scratch=12)(
        middle, first, beside, swapped, beside_square, swapped_square
    )
    pushed = [lax.ppermute(x, "dp", p) for x, p in zip(ready, (outward, across))]

    opposite, opposite_square, kept, sent = kernel_call(
        second_kernel, [block, flat, *summands(2 * rows)], smem=1, scratch=12
    )(middle, after(turned, *ready), beside, swapped, swapped_square, end, mean)
    halved = halve(kept, sent)
    result = ((rows, width), jnp.float32)
    held = kernel_call(functools.partial(held_kernel, total), [result], scratch=12)(
        with_own, own, z_anchor, z_other,
        own_square, beside_square, after(opposite_square, halved[0]), mean, spread,
    )[0]
    second = gather_chips(after(scatter(*halved), held))
    second = gather_cores(after(second, *pushed), order)
    return kernel_call(functools.partial(last_kernel, total), [result], smem=1, scratch=12)(
        middle, first, second, beside, opposite, held, *pushed
    )[0]


def by_gather(z_anchor, z_other):
    rows_here, width = z_anchor.shape
    groups = lax.axis_size("dp")
    total = rows_here * groups
    mine = lax.axis_index("dp") * rows_here
    column = lax.all_gather(z_anchor, "dp", axis=0, tiled=True).astype(jnp.float32)
    mean = jnp.sum(column, axis=0) / total
    centered_all = column - mean
    variance = jnp.sum(centered_all * centered_all, axis=0) / (total - 1)
    rounded_all = centered_all.astype(jnp.bfloat16)
    widened = rounded_all.astype(jnp.float32)
    own_square = jnp.sum(widened * widened, axis=0)
    rounded = lax.dynamic_slice_in_dim(rounded_all, mine, rows_here, 0)
    inner = lax.psum(gram(rounded, rounded_all).astype(jnp.bfloat16), "feat")
    product = jnp.dot(inner, rounded_all, preferred_element_type=jnp.float32)
    product = product - rounded.astype(jnp.float32) * own_square
    return finish(z_anchor, z_other, mean, variance, total, product)


def finish(z_anchor, z_other, mean, variance, total, product):
    coef = 2.0 * total / (25.0 * (total - 1)) / (total - 1)
    anchor = z_anchor.astype(jnp.float32)
    centered = anchor - mean
    deviation = jnp.sqrt(variance + 0.0001)
    hinge = jnp.where(deviation < 1.0, centered / deviation, 0.0)
    factor = total / (4.0 * (total - 1))
    return anchor - z_other.astype(jnp.float32) - factor * hinge + coef * product


def solution(mesh):
    placed = (P("dp", "feat"), P("dp", "feat"))
    in_line = mesh.shape["dp"] == 4 and mesh.shape["feat"] == 8
    return jax.shard_map(
        by_line if in_line else by_gather,
        mesh=mesh, in_specs=placed, out_specs=P("dp", "feat"), check_vma=False,
    )
```

```python
import functools
import math

import jax
import jax.numpy as jnp
from jax import lax
from jax.experimental import pallas as pl
from jax.experimental.pallas import tpu as pltpu
from jax.sharding import PartitionSpec as P

NORM = 128


def kernel_call(body, outs, smem=0, scratch=4, temps=()):
    def call(*args):
        space = [pltpu.SMEM] * smem + [pltpu.VMEM] * (len(args) - smem)
        return pl.pallas_call(
            body,
            out_shape=[jax.ShapeDtypeStruct(s, t) for s, t in outs],
            in_specs=[pl.BlockSpec(memory_space=m) for m in space],
            out_specs=[pl.BlockSpec(memory_space=pltpu.VMEM) for _ in outs],
            scratch_shapes=[pltpu.VMEM(s, t) for s, t in temps],
            compiler_params=pltpu.CompilerParams(vmem_limit_bytes=scratch * 1024 * 1024),
            cost_estimate=pl.CostEstimate(flops=0, bytes_accessed=0, transcendentals=0),
        )(*args)

    return call


def gram(left, right):
    return lax.dot_general(
        left, right, (((1,), (1,)), ((), ())), preferred_element_type=jnp.float32
    )


def dot_t(left, right):
    return lax.dot_general(
        left, right, (((0,), (0,)), ((), ())), preferred_element_type=jnp.float32
    )


def dot(left, right):
    return jnp.dot(left, right, preferred_element_type=jnp.float32)


def centered_into(out, block, mean, square):
    out[...] = (block[...].astype(jnp.float32) - mean).astype(jnp.bfloat16)
    wide = out[...].astype(jnp.float32)
    square[...] = jnp.sum(wide * wide, axis=0, keepdims=True)


def high_low(n, like):
    high = n.astype(jnp.bfloat16).astype(jnp.float32)
    lane = lax.broadcasted_iota(jnp.int32, like, 1)
    return jnp.where(lane == 0, high, jnp.where(lane == 1, n - high, 0.0))


def turn_into(turned, order, block):
    eighth = block.shape[0] // 8
    for k in range(8):
        start = pl.multiple_of(order[k] * eighth, eighth)
        turned[k * eighth:(k + 1) * eighth, :] = block[pl.ds(start, eighth), :]


def own_kernel(order, z, mean, own, turned, square, kept, sent):
    rows = z.shape[0]
    eighth, half = rows // 8, rows // 2
    centered_into(own, z, mean[...], square)
    turn_into(turned, order, own)
    inner = gram(turned[...], own[...])
    wide = turned[...].astype(jnp.float32)
    norm = jnp.sum(wide * wide, axis=1, keepdims=True)
    column = lax.broadcasted_iota(jnp.int32, (eighth, rows), 1)
    row = lax.broadcasted_iota(jnp.int32, (eighth, rows), 0)
    for k in range(8):
        here = slice(k * eighth, (k + 1) * eighth)
        off = jnp.where(column == row + order[k] * eighth, 0.0, inner[here])
        if k < 4:
            kept[here, :rows] = off
        else:
            sent[k * eighth - half:(k + 1) * eighth - half, :rows] = off.astype(jnp.bfloat16)
    lane = lax.broadcasted_iota(jnp.int32, (half, NORM), 1)
    kept[:, rows:] = jnp.where(lane == 0, norm[:half], 0.0)
    sent[:, rows:] = high_low(norm[half:], (half, NORM)).astype(jnp.bfloat16)


def split_sum(inner, kept, sent, here):
    half = kept.shape[0]
    kept[:, here] = inner[:half]
    sent[:, here] = inner[half:].astype(jnp.bfloat16)


def first_kernel(
    order, middle, turned, beside_in, opposite_in, mean,
    beside, beside_square, opposite, opposite_square, kept, sent, turned_beside,
):
    centered_into(beside, beside_in, mean[...], beside_square)

    @pl.when(middle[0] == 1)
    def _():
        centered_into(opposite, opposite_in, mean[...], opposite_square)
        turn_into(turned_beside, order, beside)
        split_sum(gram(turned_beside[...], opposite[...]), kept, sent, slice(None))

    @pl.when(middle[0] == 0)
    def _():
        split_sum(gram(turned[...], beside[...]), kept, sent, slice(None))


def second_kernel(middle, turned, swapped, swapped_square, end, mean, opposite, square, kept, sent):
    @pl.when(middle[0] == 1)
    def _():
        opposite[...] = swapped[...]
        square[...] = swapped_square[...]

    @pl.when(middle[0] == 0)
    def _():
        centered_into(opposite, end, mean[...], square)

    split_sum(gram(turned[...], opposite[...]), kept, sent, slice(None))


def stats_kernel(z, out):
    rows = z.shape[0]
    base = z[:16, :].astype(jnp.float32)[:1]
    apart = z[...].astype(jnp.float32) - base
    total = jnp.sum(apart, axis=0, keepdims=True)
    away = total / rows
    out[:1, :] = base + away
    out[1:, :] = jnp.sum(apart * apart, axis=0, keepdims=True) - total * away


def with_norm(x, last):
    if not last:
        return x
    tail = x[:, last:]
    split = high_low(jnp.sum(tail, axis=1, keepdims=True), tail.shape)
    return jnp.concatenate([x[:, :last], split], axis=1)


def add_kernel(last, kept, got, mine, *out):
    total = with_norm(kept[...] + got[...].astype(jnp.float32), last)
    quarter = mine.shape[0]
    mine[...] = total[:quarter]
    for k, ref in enumerate(out, 1):
        ref[...] = total[k * quarter:(k + 1) * quarter].astype(jnp.bfloat16)


def total_kernel(last, mine, a, b, c, out):
    total = mine[...] + a[...].astype(jnp.float32)
    total = total + b[...].astype(jnp.float32) + c[...].astype(jnp.float32)
    out[...] = with_norm(total, last).astype(jnp.bfloat16)


def place_into(out, order, near, far):
    eighth = out.shape[0] // 8
    for k in range(4):
        here = slice(k * eighth, (k + 1) * eighth)
        out[pl.ds(pl.multiple_of(order[k] * eighth, eighth), eighth), :] = near[here, :]
        out[pl.ds(pl.multiple_of(order[4 + k] * eighth, eighth), eighth), :] = far[here, :]


def place_kernel(order, near, far, out):
    place_into(out, order, near, far)


def push_kernel(
    order, middle, near, far, beside, opposite, beside_square, opposite_square, inner, out, over
):
    place_into(inner, order, near, far)
    width = beside.shape[1]

    @pl.when(middle[0] == 1)
    def _():
        for k in range(2):
            here = slice(k * width // 2, (k + 1) * width // 2)
            outward = dot(inner[...], opposite[:, here])
            outward = outward - beside[:, here].astype(jnp.float32) * opposite_square[:, here]
            out[:, here] = outward.astype(jnp.bfloat16)
            across = dot_t(inner[...], beside[:, here])
            across = across - opposite[:, here].astype(jnp.float32) * beside_square[:, here]
            over[:, here] = across.astype(jnp.bfloat16)


def coefficient(total):
    return 2.0 * total / (25.0 * (total - 1)) / (total - 1)


def held_kernel(
    total, with_own, own, z, other,
    own_square, beside_square, opposite_square, mean, spread, held,
):
    rows, width = own.shape
    norm = jnp.sum(with_own[:, rows:].astype(jnp.float32), axis=1, keepdims=True)
    for k in range(4):
        here = slice(k * width // 4, (k + 1) * width // 4)
        anchor = z[:, here].astype(jnp.float32)
        deviation = jnp.sqrt(spread[:, here] / (total - 1) + 0.0001)
        centered = anchor - mean[:, here]
        hinge = jnp.where(deviation < 1.0, centered / deviation, 0.0)
        plain = anchor - other[:, here].astype(jnp.float32) - total / (4.0 * (total - 1)) * hinge
        square = own_square[:, here] + beside_square[:, here] + opposite_square[:, here]
        product = dot(with_own[:, :rows], own[:, here])
        product = product + own[:, here].astype(jnp.float32) * (norm - square)
        held[:, here] = plain + coefficient(total) * product


def last_kernel(
    total, order, middle, first, near, far, beside, opposite, held, out, over, result, second
):
    rows, width = beside.shape
    place_into(second, order, near, far)

    def put(product_of, with_beside, arrived):
        for k in range(4):
            here = slice(k * width // 4, (k + 1) * width // 4)
            product = product_of(with_beside, beside[:, here])
            product = product + dot(second[:, :rows], opposite[:, here])
            product = product + arrived[:, here].astype(jnp.float32)
            result[:, here] = held[:, here] + coefficient(total) * product

    pl.when(middle[0] == 1)(lambda: put(dot_t, second[:, rows:], over))
    pl.when(middle[0] == 0)(lambda: put(dot, first[...], out))


def to_partner(x, step):
    return lax.ppermute(x, "feat", [(i, i ^ step) for i in range(8)])


def halve(kept, sent, last=0):
    half, n = kept.shape
    part = (half // 4, n)
    return kernel_call(
        functools.partial(add_kernel, last), [(part, jnp.float32)] + [(part, jnp.bfloat16)] * 3
    )(kept, to_partner(sent, 1))


def scatter(mine, *out, last=0):
    got = [to_partner(x, 2 * k) for k, x in enumerate(out, 1)]
    return kernel_call(functools.partial(total_kernel, last), [(mine.shape, jnp.bfloat16)])(
        mine, *got
    )[0]


def gather_chips(x):
    return jnp.concatenate([x] + [to_partner(x, 2 * k) for k in (1, 2, 3)])


def gather_cores(near, order):
    shape = (2 * near.shape[0], near.shape[1])
    return kernel_call(place_kernel, [(shape, jnp.bfloat16)], smem=1)(
        order, near, to_partner(near, 1)
    )[0]


def after(x, *others):
    return lax.optimization_barrier((x, *others))[0]


def by_line(z_anchor, z_other):
    rows, width = z_anchor.shape
    total = rows * 4
    plane = lax.axis_index("dp")
    middle = ((plane == 1) | (plane == 2)).astype(jnp.int32).reshape(1)
    order = lax.axis_index("feat") ^ jnp.array([0, 2, 4, 6, 1, 3, 5, 7], jnp.int32)
    across, outward = [(1, 2), (2, 1)], [(1, 0), (2, 3)]
    half = rows // 2
    flat, block = ((1, width), jnp.float32), ((rows, width), jnp.bfloat16)

    stats = kernel_call(stats_kernel, [((2, width), jnp.float32)], scratch=12)(z_anchor)[0]
    all_stats = [stats] + [
        lax.ppermute(stats, "dp", [(i, (i + k) % 4) for i in range(4)]) for k in (1, 2, 3)
    ]
    ahead = after(z_anchor, stats)
    swapped = lax.ppermute(ahead, "dp", across)
    beside_in = lax.ppermute(ahead, "dp", [(i, i ^ 1) for i in range(4)])
    mean = (all_stats[0][:1] + all_stats[1][:1] + all_stats[2][:1] + all_stats[3][:1]) / 4
    spread = 0.0
    for one in all_stats:
        shift = one[:1] - mean
        spread = spread + (one[1:] + rows * shift * shift)

    def summands(n):
        return [((half, n), jnp.float32), ((half, n), jnp.bfloat16)]

    own, turned, own_square, kept, sent = kernel_call(
        own_kernel, [block, block, flat, *summands(rows + NORM)], smem=1, scratch=12
    )(order, z_anchor, mean)
    with_own = gather_chips(scatter(*halve(kept, sent, rows), last=rows))
    with_own = gather_cores(with_own, order)
    end = lax.ppermute(after(z_anchor, beside_in, swapped, with_own), "dp", [(0, 3), (3, 0)])

    beside, beside_square, swapped, swapped_square, kept, sent = kernel_call(
        first_kernel, [block, flat, block, flat, *summands(rows)],
        smem=2, scratch=12, temps=[block],
    )(order, middle, after(turned, with_own), beside_in, swapped, mean)
    first = scatter(*halve(kept, sent))
    crossed = lax.ppermute(first, "dp", [(0, 1), (3, 2)])
    near = gather_chips(first)
    first, *ready = kernel_call(
        push_kernel, [((rows, rows), jnp.bfloat16), block, block], smem=2, scratch=12
    )(order, middle, near, to_partner(near, 1), beside, swapped, beside_square, swapped_square)
    pushed = [lax.ppermute(x, "dp", p) for x, p in zip(ready, (outward, across))]

    opposite, opposite_square, kept, sent = kernel_call(
        second_kernel, [block, flat, *summands(rows)], smem=1, scratch=12
    )(middle, after(turned, *ready), swapped, swapped_square, end, mean)
    halved = halve(kept, sent)
    result = ((rows, width), jnp.float32)
    held = kernel_call(functools.partial(held_kernel, total), [result], scratch=12)(
        with_own, own, z_anchor, z_other,
        own_square, beside_square, after(opposite_square, halved[0]), mean, spread,
    )[0]
    second = jnp.concatenate([scatter(*halved), crossed], axis=1)
    near = after(gather_chips(after(second, held)), *pushed)
    return kernel_call(
        functools.partial(last_kernel, total), [result],
        smem=2, scratch=12, temps=[((rows, 2 * rows), jnp.bfloat16)],
    )(
        order, middle, first, near, to_partner(near, 1), beside, opposite, held, *pushed
    )[0]


def by_gather(z_anchor, z_other):
    rows_here, width = z_anchor.shape
    groups = lax.axis_size("dp")
    total = rows_here * groups
    mine = lax.axis_index("dp") * rows_here
    column = lax.all_gather(z_anchor, "dp", axis=0, tiled=True).astype(jnp.float32)
    mean = jnp.sum(column, axis=0) / total
    centered_all = column - mean
    variance = jnp.sum(centered_all * centered_all, axis=0) / (total - 1)
    rounded_all = centered_all.astype(jnp.bfloat16)
    widened = rounded_all.astype(jnp.float32)
    own_square = jnp.sum(widened * widened, axis=0)
    rounded = lax.dynamic_slice_in_dim(rounded_all, mine, rows_here, 0)
    inner = lax.psum(gram(rounded, rounded_all).astype(jnp.bfloat16), "feat")
    product = jnp.dot(inner, rounded_all, preferred_element_type=jnp.float32)
    product = product - rounded.astype(jnp.float32) * own_square
    return finish(z_anchor, z_other, mean, variance, total, product)


def finish(z_anchor, z_other, mean, variance, total, product):
    coef = 2.0 * total / (25.0 * (total - 1)) / (total - 1)
    anchor = z_anchor.astype(jnp.float32)
    centered = anchor - mean
    deviation = jnp.sqrt(variance + 0.0001)
    hinge = jnp.where(deviation < 1.0, centered / deviation, 0.0)
    factor = total / (4.0 * (total - 1))
    return anchor - z_other.astype(jnp.float32) - factor * hinge + coef * product


def solution(mesh):
    placed = (P("dp", "feat"), P("dp", "feat"))
    in_line = mesh.shape["dp"] == 4 and mesh.shape["feat"] == 8
    return jax.shard_map(
        by_line if in_line else by_gather,
        mesh=mesh, in_specs=placed, out_specs=P("dp", "feat"), check_vma=False,
    )
```

```python
import functools
import math

import jax
import jax.numpy as jnp
from jax import lax
from jax.experimental import pallas as pl
from jax.experimental.pallas import tpu as pltpu
from jax.sharding import PartitionSpec as P

NORM = 128


def kernel_call(body, outs, smem=0, scratch=4, temps=()):
    def call(*args):
        space = [pltpu.SMEM] * smem + [pltpu.VMEM] * (len(args) - smem)
        return pl.pallas_call(
            body,
            out_shape=[jax.ShapeDtypeStruct(s, t) for s, t in outs],
            in_specs=[pl.BlockSpec(memory_space=m) for m in space],
            out_specs=[pl.BlockSpec(memory_space=pltpu.VMEM) for _ in outs],
            scratch_shapes=[pltpu.VMEM(s, t) for s, t in temps],
            compiler_params=pltpu.CompilerParams(vmem_limit_bytes=scratch * 1024 * 1024),
            cost_estimate=pl.CostEstimate(flops=0, bytes_accessed=0, transcendentals=0),
        )(*args)

    return call


def gram(left, right):
    return lax.dot_general(
        left, right, (((1,), (1,)), ((), ())), preferred_element_type=jnp.float32
    )


def dot_t(left, right):
    return lax.dot_general(
        left, right, (((0,), (0,)), ((), ())), preferred_element_type=jnp.float32
    )


def dot(left, right):
    return jnp.dot(left, right, preferred_element_type=jnp.float32)


def centered_into(out, block, mean, square):
    out[...] = (block[...].astype(jnp.float32) - mean).astype(jnp.bfloat16)
    wide = out[...].astype(jnp.float32)
    square[...] = jnp.sum(wide * wide, axis=0, keepdims=True)


def high_low(n, like):
    high = n.astype(jnp.bfloat16).astype(jnp.float32)
    lane = lax.broadcasted_iota(jnp.int32, like, 1)
    return jnp.where(lane == 0, high, jnp.where(lane == 1, n - high, 0.0))


def turn_into(turned, order, block):
    eighth = block.shape[0] // 8
    for k in range(8):
        start = pl.multiple_of(order[k] * eighth, eighth)
        turned[k * eighth:(k + 1) * eighth, :] = block[pl.ds(start, eighth), :]


def own_kernel(order, z, mean, own, turned, square, kept, sent):
    rows = z.shape[0]
    eighth, half = rows // 8, rows // 2
    centered_into(own, z, mean[...], square)
    turn_into(turned, order, own)
    inner = gram(turned[...], own[...])
    wide = turned[...].astype(jnp.float32)
    norm = jnp.sum(wide * wide, axis=1, keepdims=True)
    column = lax.broadcasted_iota(jnp.int32, (eighth, rows), 1)
    row = lax.broadcasted_iota(jnp.int32, (eighth, rows), 0)
    for k in range(8):
        here = slice(k * eighth, (k + 1) * eighth)
        off = jnp.where(column == row + order[k] * eighth, 0.0, inner[here])
        if k < 4:
            kept[here, :rows] = off
        else:
            sent[k * eighth - half:(k + 1) * eighth - half, :rows] = off.astype(jnp.bfloat16)
    lane = lax.broadcasted_iota(jnp.int32, (half, NORM), 1)
    kept[:, rows:] = jnp.where(lane == 0, norm[:half], 0.0)
    sent[:, rows:] = high_low(norm[half:], (half, NORM)).astype(jnp.bfloat16)


def split_sum(inner, kept, sent, here):
    half = kept.shape[0]
    kept[:, here] = inner[:half]
    sent[:, here] = inner[half:].astype(jnp.bfloat16)


def first_kernel(
    order, middle, turned, beside_in, opposite_in, mean,
    beside, beside_square, opposite, opposite_square, kept, sent, turned_beside,
):
    centered_into(beside, beside_in, mean[...], beside_square)

    @pl.when(middle[0] == 1)
    def _():
        centered_into(opposite, opposite_in, mean[...], opposite_square)
        turn_into(turned_beside, order, beside)
        split_sum(gram(turned_beside[...], opposite[...]), kept, sent, slice(None))

    @pl.when(middle[0] == 0)
    def _():
        split_sum(gram(turned[...], beside[...]), kept, sent, slice(None))


def second_kernel(middle, turned, swapped, swapped_square, end, mean, opposite, square, kept, sent):
    @pl.when(middle[0] == 1)
    def _():
        opposite[...] = swapped[...]
        square[...] = swapped_square[...]

    @pl.when(middle[0] == 0)
    def _():
        centered_into(opposite, end, mean[...], square)

    split_sum(gram(turned[...], opposite[...]), kept, sent, slice(None))


def stats_kernel(z, out):
    rows = z.shape[0]
    base = z[:16, :].astype(jnp.float32)[:1]
    apart = z[...].astype(jnp.float32) - base
    total = jnp.sum(apart, axis=0, keepdims=True)
    away = total / rows
    out[:1, :] = base + away
    out[1:, :] = jnp.sum(apart * apart, axis=0, keepdims=True) - total * away


def with_norm(x, last):
    if not last:
        return x
    tail = x[:, last:]
    split = high_low(jnp.sum(tail, axis=1, keepdims=True), tail.shape)
    return jnp.concatenate([x[:, :last], split], axis=1)


def add_kernel(last, kept, got, mine, *out):
    total = with_norm(kept[...] + got[...].astype(jnp.float32), last)
    quarter = mine.shape[0]
    mine[...] = total[:quarter]
    for k, ref in enumerate(out, 1):
        ref[...] = total[k * quarter:(k + 1) * quarter].astype(jnp.bfloat16)


def total_kernel(last, mine, a, b, c, out):
    total = mine[...] + a[...].astype(jnp.float32)
    total = total + b[...].astype(jnp.float32) + c[...].astype(jnp.float32)
    out[...] = with_norm(total, last).astype(jnp.bfloat16)


def place_into(out, order, near, far):
    eighth = out.shape[0] // 8
    for k in range(4):
        here = slice(k * eighth, (k + 1) * eighth)
        out[pl.ds(pl.multiple_of(order[k] * eighth, eighth), eighth), :] = near[here, :]
        out[pl.ds(pl.multiple_of(order[4 + k] * eighth, eighth), eighth), :] = far[here, :]


def push_kernel(
    order, middle, near, far, beside, opposite, beside_square, opposite_square, out, over, inner
):
    width = beside.shape[1]

    @pl.when(middle[0] == 1)
    def _():
        place_into(inner, order, near, far)
        for k in range(2):
            here = slice(k * width // 2, (k + 1) * width // 2)
            outward = dot(inner[...], opposite[:, here])
            outward = outward - beside[:, here].astype(jnp.float32) * opposite_square[:, here]
            out[:, here] = outward.astype(jnp.bfloat16)
            across = dot_t(inner[...], beside[:, here])
            across = across - opposite[:, here].astype(jnp.float32) * beside_square[:, here]
            over[:, here] = across.astype(jnp.bfloat16)


def coefficient(total):
    return 2.0 * total / (25.0 * (total - 1)) / (total - 1)


def held_kernel(
    total, order, near, far, own, z, other,
    own_square, beside_square, opposite_square, mean, spread, held, with_own,
):
    rows, width = own.shape
    place_into(with_own, order, near, far)
    norm = jnp.sum(with_own[:, rows:].astype(jnp.float32), axis=1, keepdims=True)
    for k in range(4):
        here = slice(k * width // 4, (k + 1) * width // 4)
        anchor = z[:, here].astype(jnp.float32)
        deviation = jnp.sqrt(spread[:, here] / (total - 1) + 0.0001)
        centered = anchor - mean[:, here]
        hinge = jnp.where(deviation < 1.0, centered / deviation, 0.0)
        plain = anchor - other[:, here].astype(jnp.float32) - total / (4.0 * (total - 1)) * hinge
        square = own_square[:, here] + beside_square[:, here] + opposite_square[:, here]
        product = dot(with_own[:, :rows], own[:, here])
        product = product + own[:, here].astype(jnp.float32) * (norm - square)
        held[:, here] = plain + coefficient(total) * product


def last_kernel(
    total, order, middle, near, far, beside, opposite, held, out, over, result, second
):
    rows, width = beside.shape
    place_into(second, order, near, far)

    def put(product_of, arrived):
        for k in range(4):
            here = slice(k * width // 4, (k + 1) * width // 4)
            product = product_of(second[:, rows:], beside[:, here])
            product = product + dot(second[:, :rows], opposite[:, here])
            product = product + arrived[:, here].astype(jnp.float32)
            result[:, here] = held[:, here] + coefficient(total) * product

    pl.when(middle[0] == 1)(lambda: put(dot_t, over))
    pl.when(middle[0] == 0)(lambda: put(dot, out))


def to_partner(x, step):
    return lax.ppermute(x, "feat", [(i, i ^ step) for i in range(8)])


def halve(kept, sent, last=0):
    half, n = kept.shape
    part = (half // 4, n)
    return kernel_call(
        functools.partial(add_kernel, last), [(part, jnp.float32)] + [(part, jnp.bfloat16)] * 3
    )(kept, to_partner(sent, 1))


def scatter(mine, *out, last=0):
    got = [to_partner(x, 2 * k) for k, x in enumerate(out, 1)]
    return kernel_call(functools.partial(total_kernel, last), [(mine.shape, jnp.bfloat16)])(
        mine, *got
    )[0]


def pile_kernel(*refs):
    *pieces, out = refs
    rows = pieces[0].shape[0]
    for k, piece in enumerate(pieces):
        out[k * rows:(k + 1) * rows, :] = piece[...]


def gather_chips(x):
    pile = [((4 * x.shape[0], x.shape[1]), x.dtype)]
    return kernel_call(pile_kernel, pile)(x, *(to_partner(x, 2 * k) for k in (1, 2, 3)))[0]


def after(x, *others):
    return lax.optimization_barrier((x, *others))[0]


def by_line(z_anchor, z_other):
    rows, width = z_anchor.shape
    total = rows * 4
    plane = lax.axis_index("dp")
    middle = ((plane == 1) | (plane == 2)).astype(jnp.int32).reshape(1)
    order = lax.axis_index("feat") ^ jnp.array([0, 2, 4, 6, 1, 3, 5, 7], jnp.int32)
    across, outward = [(1, 2), (2, 1)], [(1, 0), (2, 3)]
    half = rows // 2
    flat, block = ((1, width), jnp.float32), ((rows, width), jnp.bfloat16)

    stats = kernel_call(stats_kernel, [((2, width), jnp.float32)], scratch=12)(z_anchor)[0]
    all_stats = [stats] + [
        lax.ppermute(stats, "dp", [(i, (i + k) % 4) for i in range(4)]) for k in (1, 2, 3)
    ]
    ahead = after(z_anchor, stats)
    beside_in = lax.ppermute(ahead, "dp", [(i, i ^ 1) for i in range(4)])
    swapped = lax.ppermute(ahead, "dp", across)
    mean = (all_stats[0][:1] + all_stats[1][:1] + all_stats[2][:1] + all_stats[3][:1]) / 4
    spread = 0.0
    for one in all_stats:
        shift = one[:1] - mean
        spread = spread + (one[1:] + rows * shift * shift)

    def summands(n):
        return [((half, n), jnp.float32), ((half, n), jnp.bfloat16)]

    own, turned, own_square, kept, sent = kernel_call(
        own_kernel, [block, block, flat, *summands(rows + NORM)], smem=1, scratch=12
    )(order, z_anchor, mean)
    near_own = gather_chips(scatter(*halve(kept, sent, rows), last=rows))
    end = lax.ppermute(after(z_anchor, beside_in, swapped, near_own), "dp", [(0, 3), (3, 0)])

    beside, beside_square, swapped, swapped_square, kept, sent = kernel_call(
        first_kernel, [block, flat, block, flat, *summands(rows)],
        smem=2, scratch=12, temps=[block],
    )(order, middle, after(turned, near_own), beside_in, swapped, mean)
    first = scatter(*halve(kept, sent))
    crossed = lax.ppermute(first, "dp", [(0, 1), (3, 2)])

    def gather(x):
        near = gather_chips(x)
        return near, to_partner(near, 1)

    near, far = lax.cond(
        middle[0] == 1, gather, lambda x: (jnp.zeros((half, rows), x.dtype),) * 2, first
    )
    ready = kernel_call(
        push_kernel, [block, block], smem=2, scratch=12, temps=[((rows, rows), jnp.bfloat16)]
    )(order, middle, near, far, beside, swapped, beside_square, swapped_square)
    pushed = [lax.ppermute(x, "dp", p) for x, p in zip(ready, (outward, across))]

    opposite, opposite_square, kept, sent = kernel_call(
        second_kernel, [block, flat, *summands(rows)], smem=1, scratch=12
    )(middle, after(turned, *ready), swapped, swapped_square, end, mean)
    halved = halve(kept, sent)
    result = ((rows, width), jnp.float32)
    held = kernel_call(
        functools.partial(held_kernel, total), [result],
        smem=1, scratch=12, temps=[((rows, rows + NORM), jnp.bfloat16)],
    )(
        order, near_own, to_partner(near_own, 1), own, z_anchor, z_other,
        own_square, beside_square, after(opposite_square, halved[0]), mean, spread,
    )[0]
    crossed = jnp.where(middle == 1, crossed, first)
    second = jnp.concatenate([scatter(*halved), crossed], axis=1)
    near = after(gather_chips(after(second, held)), *pushed)
    return kernel_call(
        functools.partial(last_kernel, total), [result],
        smem=2, scratch=12, temps=[((rows, 2 * rows), jnp.bfloat16)],
    )(
        order, middle, near, to_partner(near, 1), beside, opposite, held, *pushed
    )[0]


def by_gather(z_anchor, z_other):
    rows_here, width = z_anchor.shape
    groups = lax.axis_size("dp")
    total = rows_here * groups
    mine = lax.axis_index("dp") * rows_here
    column = lax.all_gather(z_anchor, "dp", axis=0, tiled=True).astype(jnp.float32)
    mean = jnp.sum(column, axis=0) / total
    centered_all = column - mean
    variance = jnp.sum(centered_all * centered_all, axis=0) / (total - 1)
    rounded_all = centered_all.astype(jnp.bfloat16)
    widened = rounded_all.astype(jnp.float32)
    own_square = jnp.sum(widened * widened, axis=0)
    rounded = lax.dynamic_slice_in_dim(rounded_all, mine, rows_here, 0)
    inner = lax.psum(gram(rounded, rounded_all).astype(jnp.bfloat16), "feat")
    product = jnp.dot(inner, rounded_all, preferred_element_type=jnp.float32)
    product = product - rounded.astype(jnp.float32) * own_square
    return finish(z_anchor, z_other, mean, variance, total, product)


def finish(z_anchor, z_other, mean, variance, total, product):
    coef = 2.0 * total / (25.0 * (total - 1)) / (total - 1)
    anchor = z_anchor.astype(jnp.float32)
    centered = anchor - mean
    deviation = jnp.sqrt(variance + 0.0001)
    hinge = jnp.where(deviation < 1.0, centered / deviation, 0.0)
    factor = total / (4.0 * (total - 1))
    return anchor - z_other.astype(jnp.float32) - factor * hinge + coef * product


def solution(mesh):
    placed = (P("dp", "feat"), P("dp", "feat"))
    in_line = mesh.shape["dp"] == 4 and mesh.shape["feat"] == 8
    return jax.shard_map(
        by_line if in_line else by_gather,
        mesh=mesh, in_specs=placed, out_specs=P("dp", "feat"), check_vma=False,
    )
```

```python
import functools
import math

import jax
import jax.numpy as jnp
from jax import lax
from jax.experimental import pallas as pl
from jax.experimental.pallas import tpu as pltpu
from jax.sharding import PartitionSpec as P

NORM = 128


def kernel_call(body, outs, smem=0, scratch=4, temps=()):
    def call(*args):
        space = [pltpu.SMEM] * smem + [pltpu.VMEM] * (len(args) - smem)
        return pl.pallas_call(
            body,
            out_shape=[jax.ShapeDtypeStruct(s, t) for s, t in outs],
            in_specs=[pl.BlockSpec(memory_space=m) for m in space],
            out_specs=[pl.BlockSpec(memory_space=pltpu.VMEM) for _ in outs],
            scratch_shapes=[pltpu.VMEM(s, t) for s, t in temps],
            compiler_params=pltpu.CompilerParams(vmem_limit_bytes=scratch * 1024 * 1024),
            cost_estimate=pl.CostEstimate(flops=0, bytes_accessed=0, transcendentals=0),
        )(*args)

    return call


def gram(left, right):
    return lax.dot_general(
        left, right, (((1,), (1,)), ((), ())), preferred_element_type=jnp.float32
    )


def dot_t(left, right):
    return lax.dot_general(
        left, right, (((0,), (0,)), ((), ())), preferred_element_type=jnp.float32
    )


def dot(left, right):
    return jnp.dot(left, right, preferred_element_type=jnp.float32)


def centered_into(out, block, mean, square):
    out[...] = (block[...].astype(jnp.float32) - mean).astype(jnp.bfloat16)
    wide = out[...].astype(jnp.float32)
    square[...] = jnp.sum(wide * wide, axis=0, keepdims=True)


def high_low(n, like):
    high = n.astype(jnp.bfloat16).astype(jnp.float32)
    lane = lax.broadcasted_iota(jnp.int32, like, 1)
    return jnp.where(lane == 0, high, jnp.where(lane == 1, n - high, 0.0))


def turn_into(turned, order, block):
    eighth = block.shape[0] // 8
    for k in range(8):
        start = pl.multiple_of(order[k] * eighth, eighth)
        turned[k * eighth:(k + 1) * eighth, :] = block[pl.ds(start, eighth), :]


def own_kernel(order, z, mean, own, turned, square, kept, sent):
    rows = z.shape[0]
    eighth, half = rows // 8, rows // 2
    centered_into(own, z, mean[...], square)
    turn_into(turned, order, own)
    inner = gram(turned[...], own[...])
    wide = turned[...].astype(jnp.float32)
    norm = jnp.sum(wide * wide, axis=1, keepdims=True)
    column = lax.broadcasted_iota(jnp.int32, (eighth, rows), 1)
    row = lax.broadcasted_iota(jnp.int32, (eighth, rows), 0)
    for k in range(8):
        here = slice(k * eighth, (k + 1) * eighth)
        off = jnp.where(column == row + order[k] * eighth, 0.0, inner[here])
        if k < 4:
            kept[here, :rows] = off
        else:
            sent[k * eighth - half:(k + 1) * eighth - half, :rows] = off.astype(jnp.bfloat16)
    lane = lax.broadcasted_iota(jnp.int32, (half, NORM), 1)
    kept[:, rows:] = jnp.where(lane == 0, norm[:half], 0.0)
    sent[:, rows:] = high_low(norm[half:], (half, NORM)).astype(jnp.bfloat16)


def split_sum(inner, kept, sent, here):
    half = kept.shape[0]
    kept[:, here] = inner[:half]
    sent[:, here] = inner[half:].astype(jnp.bfloat16)


def first_kernel(
    order, middle, turned, beside_in, opposite_in, mean,
    beside, beside_square, opposite, opposite_square, kept, sent, turned_beside,
):
    centered_into(beside, beside_in, mean[...], beside_square)

    @pl.when(middle[0] == 1)
    def _():
        centered_into(opposite, opposite_in, mean[...], opposite_square)
        turn_into(turned_beside, order, beside)
        split_sum(gram(turned_beside[...], opposite[...]), kept, sent, slice(None))

    @pl.when(middle[0] == 0)
    def _():
        split_sum(gram(turned[...], beside[...]), kept, sent, slice(None))


def second_kernel(middle, turned, swapped, swapped_square, end, mean, opposite, square, kept, sent):
    @pl.when(middle[0] == 1)
    def _():
        opposite[...] = swapped[...]
        square[...] = swapped_square[...]

    @pl.when(middle[0] == 0)
    def _():
        centered_into(opposite, end, mean[...], square)

    split_sum(gram(turned[...], opposite[...]), kept, sent, slice(None))


def stats_kernel(z, out):
    rows = z.shape[0]
    base = z[:16, :].astype(jnp.float32)[:1]
    apart = z[...].astype(jnp.float32) - base
    total = jnp.sum(apart, axis=0, keepdims=True)
    away = total / rows
    out[:1, :] = base + away
    out[1:, :] = jnp.sum(apart * apart, axis=0, keepdims=True) - total * away


def with_norm(x, last):
    if not last:
        return x
    tail = x[:, last:]
    split = high_low(jnp.sum(tail, axis=1, keepdims=True), tail.shape)
    return jnp.concatenate([x[:, :last], split], axis=1)


def add_kernel(last, kept, got, mine, *out):
    total = with_norm(kept[...] + got[...].astype(jnp.float32), last)
    quarter = mine.shape[0]
    mine[...] = total[:quarter]
    for k, ref in enumerate(out, 1):
        ref[...] = total[k * quarter:(k + 1) * quarter].astype(jnp.bfloat16)


def total_kernel(last, mine, a, b, c, out):
    total = mine[...] + a[...].astype(jnp.float32)
    total = total + b[...].astype(jnp.float32) + c[...].astype(jnp.float32)
    out[...] = with_norm(total, last).astype(jnp.bfloat16)


def place_into(out, order, near, far):
    eighth = out.shape[0] // 8
    for k in range(4):
        here = slice(k * eighth, (k + 1) * eighth)
        out[pl.ds(pl.multiple_of(order[k] * eighth, eighth), eighth), :] = near[here, :]
        out[pl.ds(pl.multiple_of(order[4 + k] * eighth, eighth), eighth), :] = far[here, :]


def push_kernel(
    order, middle, near, far, beside, opposite, beside_square, opposite_square, out, over, inner
):
    width = beside.shape[1]

    @pl.when(middle[0] == 1)
    def _():
        place_into(inner, order, near, far)
        for k in range(2):
            here = slice(k * width // 2, (k + 1) * width // 2)
            outward = dot(inner[...], opposite[:, here])
            outward = outward - beside[:, here].astype(jnp.float32) * opposite_square[:, here]
            out[:, here] = outward.astype(jnp.bfloat16)
            across = dot_t(inner[...], beside[:, here])
            across = across - opposite[:, here].astype(jnp.float32) * beside_square[:, here]
            over[:, here] = across.astype(jnp.bfloat16)


def coefficient(total):
    return 2.0 * total / (25.0 * (total - 1)) / (total - 1)


def held_kernel(
    total, order, near, far, own, z, other,
    own_square, beside_square, opposite_square, mean, spread, held, with_own,
):
    rows, width = own.shape
    place_into(with_own, order, near, far)
    norm = jnp.sum(with_own[:, rows:].astype(jnp.float32), axis=1, keepdims=True)
    for k in range(4):
        here = slice(k * width // 4, (k + 1) * width // 4)
        anchor = z[:, here].astype(jnp.float32)
        deviation = jnp.sqrt(spread[:, here] / (total - 1) + 0.0001)
        centered = anchor - mean[:, here]
        hinge = jnp.where(deviation < 1.0, centered / deviation, 0.0)
        plain = anchor - other[:, here].astype(jnp.float32) - total / (4.0 * (total - 1)) * hinge
        square = own_square[:, here] + beside_square[:, here] + opposite_square[:, here]
        product = dot(with_own[:, :rows], own[:, here])
        product = product + own[:, here].astype(jnp.float32) * (norm - square)
        held[:, here] = plain + coefficient(total) * product


def last_kernel(
    total, order, middle, near, far, beside, opposite, held, out, over, result, second
):
    rows, width = beside.shape
    place_into(second, order, near, far)

    def put(product_of, arrived):
        for k in range(4):
            here = slice(k * width // 4, (k + 1) * width // 4)
            product = product_of(second[:, rows:], beside[:, here])
            product = product + dot(second[:, :rows], opposite[:, here])
            product = product + arrived[:, here].astype(jnp.float32)
            result[:, here] = held[:, here] + coefficient(total) * product

    pl.when(middle[0] == 1)(lambda: put(dot_t, over))
    pl.when(middle[0] == 0)(lambda: put(dot, out))


def to_partner(x, step):
    return lax.ppermute(x, "feat", [(i, i ^ step) for i in range(8)])


def halve(kept, sent, last=0):
    half, n = kept.shape
    part = (half // 4, n)
    return kernel_call(
        functools.partial(add_kernel, last), [(part, jnp.float32)] + [(part, jnp.bfloat16)] * 3
    )(kept, to_partner(sent, 1))


def scatter(mine, *out, last=0):
    got = [to_partner(x, 2 * k) for k, x in enumerate(out, 1)]
    return kernel_call(functools.partial(total_kernel, last), [(mine.shape, jnp.bfloat16)])(
        mine, *got
    )[0]


def pile_kernel(*refs):
    *pieces, out = refs
    rows = pieces[0].shape[0]
    for k, piece in enumerate(pieces):
        out[k * rows:(k + 1) * rows, :] = piece[...]


def gather_chips(x):
    pile = [((4 * x.shape[0], x.shape[1]), x.dtype)]
    return kernel_call(pile_kernel, pile)(x, *(to_partner(x, 2 * k) for k in (1, 2, 3)))[0]


def after(x, *others):
    return lax.optimization_barrier((x, *others))[0]


def by_line(z_anchor, z_other):
    rows, width = z_anchor.shape
    total = rows * 4
    plane = lax.axis_index("dp")
    middle = ((plane == 1) | (plane == 2)).astype(jnp.int32).reshape(1)
    order = lax.axis_index("feat") ^ jnp.array([0, 2, 4, 6, 1, 3, 5, 7], jnp.int32)
    across, outward = [(1, 2), (2, 1)], [(1, 0), (2, 3)]
    half = rows // 2
    flat, block = ((1, width), jnp.float32), ((rows, width), jnp.bfloat16)

    stats = kernel_call(stats_kernel, [((2, width), jnp.float32)], scratch=12)(z_anchor)[0]
    all_stats = [stats] + [
        lax.ppermute(stats, "dp", [(i, (i + k) % 4) for i in range(4)]) for k in (1, 2, 3)
    ]
    ahead = after(z_anchor, *all_stats)
    beside_in = lax.ppermute(ahead, "dp", [(i, i ^ 1) for i in range(4)])
    swapped = lax.ppermute(ahead, "dp", across)
    mean = (all_stats[0][:1] + all_stats[1][:1] + all_stats[2][:1] + all_stats[3][:1]) / 4
    spread = 0.0
    for one in all_stats:
        shift = one[:1] - mean
        spread = spread + (one[1:] + rows * shift * shift)

    def summands(n):
        return [((half, n), jnp.float32), ((half, n), jnp.bfloat16)]

    own, turned, own_square, kept, sent = kernel_call(
        own_kernel, [block, block, flat, *summands(rows + NORM)], smem=1, scratch=12
    )(order, z_anchor, mean)
    near_own = gather_chips(scatter(*halve(kept, sent, rows), last=rows))
    end = lax.ppermute(after(z_anchor, beside_in, swapped, near_own), "dp", [(0, 3), (3, 0)])

    beside, beside_square, swapped, swapped_square, kept, sent = kernel_call(
        first_kernel, [block, flat, block, flat, *summands(rows)],
        smem=2, scratch=12, temps=[block],
    )(order, middle, after(turned, near_own), beside_in, swapped, mean)
    first = scatter(*halve(kept, sent))
    crossed = lax.ppermute(first, "dp", [(0, 1), (3, 2)])
    near = gather_chips(first)
    ready = kernel_call(
        push_kernel, [block, block], smem=2, scratch=12, temps=[((rows, rows), jnp.bfloat16)]
    )(order, middle, near, to_partner(near, 1), beside, swapped, beside_square, swapped_square)
    out, over = ready
    pushed = [
        lax.ppermute(out, "dp", outward), lax.ppermute(after(over, end), "dp", across)
    ]

    opposite, opposite_square, kept, sent = kernel_call(
        second_kernel, [block, flat, *summands(rows)], smem=1, scratch=12
    )(middle, after(turned, *ready), swapped, swapped_square, end, mean)
    halved = halve(kept, after(sent, crossed))
    result = ((rows, width), jnp.float32)
    held = kernel_call(
        functools.partial(held_kernel, total), [result],
        smem=1, scratch=12, temps=[((rows, rows + NORM), jnp.bfloat16)],
    )(
        order, near_own, to_partner(near_own, 1), own, z_anchor, z_other,
        own_square, beside_square, after(opposite_square, halved[0]), mean, spread,
    )[0]
    crossed = jnp.where(middle == 1, crossed, first)
    second = jnp.concatenate([scatter(*halved), crossed], axis=1)
    near = after(gather_chips(after(second, held)), *pushed)
    return kernel_call(
        functools.partial(last_kernel, total), [result],
        smem=2, scratch=12, temps=[((rows, 2 * rows), jnp.bfloat16)],
    )(
        order, middle, near, to_partner(near, 1), beside, opposite, held, *pushed
    )[0]


def by_gather(z_anchor, z_other):
    rows_here, width = z_anchor.shape
    groups = lax.axis_size("dp")
    total = rows_here * groups
    mine = lax.axis_index("dp") * rows_here
    column = lax.all_gather(z_anchor, "dp", axis=0, tiled=True).astype(jnp.float32)
    mean = jnp.sum(column, axis=0) / total
    centered_all = column - mean
    variance = jnp.sum(centered_all * centered_all, axis=0) / (total - 1)
    rounded_all = centered_all.astype(jnp.bfloat16)
    widened = rounded_all.astype(jnp.float32)
    own_square = jnp.sum(widened * widened, axis=0)
    rounded = lax.dynamic_slice_in_dim(rounded_all, mine, rows_here, 0)
    inner = lax.psum(gram(rounded, rounded_all).astype(jnp.bfloat16), "feat")
    product = jnp.dot(inner, rounded_all, preferred_element_type=jnp.float32)
    product = product - rounded.astype(jnp.float32) * own_square
    return finish(z_anchor, z_other, mean, variance, total, product)


def finish(z_anchor, z_other, mean, variance, total, product):
    coef = 2.0 * total / (25.0 * (total - 1)) / (total - 1)
    anchor = z_anchor.astype(jnp.float32)
    centered = anchor - mean
    deviation = jnp.sqrt(variance + 0.0001)
    hinge = jnp.where(deviation < 1.0, centered / deviation, 0.0)
    factor = total / (4.0 * (total - 1))
    return anchor - z_other.astype(jnp.float32) - factor * hinge + coef * product


def solution(mesh):
    placed = (P("dp", "feat"), P("dp", "feat"))
    in_line = mesh.shape["dp"] == 4 and mesh.shape["feat"] == 8
    return jax.shard_map(
        by_line if in_line else by_gather,
        mesh=mesh, in_specs=placed, out_specs=P("dp", "feat"), check_vma=False,
    )
```

```python
import functools
import math

import jax
import jax.numpy as jnp
from jax import lax
from jax.experimental import pallas as pl
from jax.experimental.pallas import tpu as pltpu
from jax.sharding import PartitionSpec as P

NORM = 128


def kernel_call(body, outs, smem=0, scratch=4, temps=()):
    def call(*args):
        space = [pltpu.SMEM] * smem + [pltpu.VMEM] * (len(args) - smem)
        return pl.pallas_call(
            body,
            out_shape=[jax.ShapeDtypeStruct(s, t) for s, t in outs],
            in_specs=[pl.BlockSpec(memory_space=m) for m in space],
            out_specs=[pl.BlockSpec(memory_space=pltpu.VMEM) for _ in outs],
            scratch_shapes=[pltpu.VMEM(s, t) for s, t in temps],
            compiler_params=pltpu.CompilerParams(vmem_limit_bytes=scratch * 1024 * 1024),
            cost_estimate=pl.CostEstimate(flops=0, bytes_accessed=0, transcendentals=0),
        )(*args)

    return call


def gram(left, right):
    return lax.dot_general(
        left, right, (((1,), (1,)), ((), ())), preferred_element_type=jnp.float32
    )


def dot_t(left, right):
    return lax.dot_general(
        left, right, (((0,), (0,)), ((), ())), preferred_element_type=jnp.float32
    )


def dot(left, right):
    return jnp.dot(left, right, preferred_element_type=jnp.float32)


def centered_into(out, block, mean, square):
    out[...] = (block[...].astype(jnp.float32) - mean).astype(jnp.bfloat16)
    wide = out[...].astype(jnp.float32)
    square[...] = jnp.sum(wide * wide, axis=0, keepdims=True)


def high_low(n, like):
    high = n.astype(jnp.bfloat16).astype(jnp.float32)
    lane = lax.broadcasted_iota(jnp.int32, like, 1)
    return jnp.where(lane == 0, high, jnp.where(lane == 1, n - high, 0.0))


def turn_into(turned, order, block):
    eighth = block.shape[0] // 8
    for k in range(8):
        start = pl.multiple_of(order[k] * eighth, eighth)
        turned[k * eighth:(k + 1) * eighth, :] = block[pl.ds(start, eighth), :]


def own_kernel(order, z, mean, own, turned, square, kept, sent):
    rows = z.shape[0]
    eighth, half = rows // 8, rows // 2
    centered_into(own, z, mean[...], square)
    turn_into(turned, order, own)
    inner = gram(turned[...], own[...])
    wide = turned[...].astype(jnp.float32)
    norm = jnp.sum(wide * wide, axis=1, keepdims=True)
    column = lax.broadcasted_iota(jnp.int32, (eighth, rows), 1)
    row = lax.broadcasted_iota(jnp.int32, (eighth, rows), 0)
    for k in range(8):
        here = slice(k * eighth, (k + 1) * eighth)
        off = jnp.where(column == row + order[k] * eighth, 0.0, inner[here])
        if k < 4:
            kept[here, :rows] = off
        else:
            sent[k * eighth - half:(k + 1) * eighth - half, :rows] = off.astype(jnp.bfloat16)
    lane = lax.broadcasted_iota(jnp.int32, (half, NORM), 1)
    kept[:, rows:] = jnp.where(lane == 0, norm[:half], 0.0)
    sent[:, rows:] = high_low(norm[half:], (half, NORM)).astype(jnp.bfloat16)


def split_sum(inner, kept, sent, here):
    half = kept.shape[0]
    kept[:, here] = inner[:half]
    sent[:, here] = inner[half:].astype(jnp.bfloat16)


def first_kernel(
    order, middle, turned, beside_in, opposite_in, mean,
    beside, beside_square, opposite, opposite_square, kept, sent, turned_beside,
):
    centered_into(beside, beside_in, mean[...], beside_square)

    @pl.when(middle[0] == 1)
    def _():
        centered_into(opposite, opposite_in, mean[...], opposite_square)
        turn_into(turned_beside, order, beside)
        split_sum(gram(turned_beside[...], opposite[...]), kept, sent, slice(None))

    @pl.when(middle[0] == 0)
    def _():
        split_sum(gram(turned[...], beside[...]), kept, sent, slice(None))


def early_kernel(middle, turned, beside, opposite, kept, sent):
    rows = beside.shape[0]

    @pl.when(middle[0] == 1)
    def _():
        split_sum(gram(turned[...], opposite[...]), kept, sent, slice(0, rows))
        split_sum(gram(turned[...], beside[...]), kept, sent, slice(rows, 2 * rows))


def late_kernel(middle, turned, sent_early, end_in, mean, end, square, kept, sent):
    rows = end.shape[0]

    @pl.when(middle[0] == 1)
    def _():
        sent[...] = sent_early[...]

    @pl.when(middle[0] == 0)
    def _():
        centered_into(end, end_in, mean[...], square)
        split_sum(gram(turned[...], end[...]), kept, sent, slice(0, rows))
        sent[:, rows:] = jnp.zeros_like(sent[:, rows:])


def stats_kernel(z, out):
    rows = z.shape[0]
    base = z[:16, :].astype(jnp.float32)[:1]
    apart = z[...].astype(jnp.float32) - base
    total = jnp.sum(apart, axis=0, keepdims=True)
    away = total / rows
    out[:1, :] = base + away
    out[1:, :] = jnp.sum(apart * apart, axis=0, keepdims=True) - total * away


def with_norm(x, last):
    if not last:
        return x
    tail = x[:, last:]
    split = high_low(jnp.sum(tail, axis=1, keepdims=True), tail.shape)
    return jnp.concatenate([x[:, :last], split], axis=1)


def add_kernel(last, kept, got, mine, *out):
    total = with_norm(kept[...] + got[...].astype(jnp.float32), last)
    quarter = mine.shape[0]
    mine[...] = total[:quarter]
    for k, ref in enumerate(out, 1):
        ref[...] = total[k * quarter:(k + 1) * quarter].astype(jnp.bfloat16)


def add_either_kernel(middle, kept_early, kept, got, mine, *out):
    quarter, rows = mine.shape[0], kept.shape[1]

    def put(total, here):
        mine[:, here] = total[:quarter]
        for k, ref in enumerate(out, 1):
            ref[:, here] = total[k * quarter:(k + 1) * quarter].astype(jnp.bfloat16)

    @pl.when(middle[0] == 1)
    def _():
        put(kept_early[...] + got[...].astype(jnp.float32), slice(None))

    @pl.when(middle[0] == 0)
    def _():
        put(kept[...] + got[:, :rows].astype(jnp.float32), slice(0, rows))
        put(jnp.zeros((4 * quarter, rows), jnp.float32), slice(rows, 2 * rows))


def total_kernel(last, mine, a, b, c, out):
    total = mine[...] + a[...].astype(jnp.float32)
    total = total + b[...].astype(jnp.float32) + c[...].astype(jnp.float32)
    out[...] = with_norm(total, last).astype(jnp.bfloat16)


def total_either_kernel(middle, first, mine, a, b, c, out):
    rows = first.shape[1]

    def put(here):
        total = mine[:, here] + a[:, here].astype(jnp.float32)
        total = total + b[:, here].astype(jnp.float32) + c[:, here].astype(jnp.float32)
        out[:, here] = total.astype(jnp.bfloat16)

    put(slice(0, rows))
    pl.when(middle[0] == 1)(lambda: put(slice(rows, 2 * rows)))

    @pl.when(middle[0] == 0)
    def _():
        out[:, rows:] = first[...]


def place_into(out, order, near, far):
    eighth = out.shape[0] // 8
    for k in range(4):
        here = slice(k * eighth, (k + 1) * eighth)
        out[pl.ds(pl.multiple_of(order[k] * eighth, eighth), eighth), :] = near[here, :]
        out[pl.ds(pl.multiple_of(order[4 + k] * eighth, eighth), eighth), :] = far[here, :]


def push_kernel(
    order, middle, near, far, beside, opposite, beside_square, opposite_square, out, over, inner
):
    width = beside.shape[1]

    @pl.when(middle[0] == 1)
    def _():
        place_into(inner, order, near, far)
        for k in range(2):
            here = slice(k * width // 2, (k + 1) * width // 2)
            outward = dot(inner[...], opposite[:, here])
            outward = outward - beside[:, here].astype(jnp.float32) * opposite_square[:, here]
            out[:, here] = outward.astype(jnp.bfloat16)
            across = dot_t(inner[...], beside[:, here])
            across = across - opposite[:, here].astype(jnp.float32) * beside_square[:, here]
            over[:, here] = across.astype(jnp.bfloat16)


def coefficient(total):
    return 2.0 * total / (25.0 * (total - 1)) / (total - 1)


def held_kernel(
    total, order, middle, near, far, own, z, other,
    own_square, beside_square, swapped_square, end_square, mean, spread, held, with_own,
):
    rows, width = own.shape
    place_into(with_own, order, near, far)
    norm = jnp.sum(with_own[:, rows:].astype(jnp.float32), axis=1, keepdims=True)
    for k in range(4):
        here = slice(k * width // 4, (k + 1) * width // 4)
        anchor = z[:, here].astype(jnp.float32)
        deviation = jnp.sqrt(spread[:, here] / (total - 1) + 0.0001)
        centered = anchor - mean[:, here]
        hinge = jnp.where(deviation < 1.0, centered / deviation, 0.0)
        plain = anchor - other[:, here].astype(jnp.float32) - total / (4.0 * (total - 1)) * hinge
        opposite = jnp.where(middle[0] == 1, swapped_square[:, here], end_square[:, here])
        square = own_square[:, here] + beside_square[:, here] + opposite
        product = dot(with_own[:, :rows], own[:, here])
        product = product + own[:, here].astype(jnp.float32) * (norm - square)
        held[:, here] = plain + coefficient(total) * product


def last_kernel(
    total, order, middle, near, far, beside, swapped, end, held, out, over, result, second
):
    rows, width = beside.shape
    place_into(second, order, near, far)

    def put(opposite, arrived):
        for k in range(4):
            here = slice(k * width // 4, (k + 1) * width // 4)
            product = dot(second[:, rows:], beside[:, here])
            product = product + dot(second[:, :rows], opposite[:, here])
            product = product + arrived[:, here].astype(jnp.float32)
            result[:, here] = held[:, here] + coefficient(total) * product

    pl.when(middle[0] == 1)(lambda: put(swapped, over))
    pl.when(middle[0] == 0)(lambda: put(end, out))


def to_partner(x, step):
    return lax.ppermute(x, "feat", [(i, i ^ step) for i in range(8)])


def halve(kept, sent, last=0):
    half, n = kept.shape
    part = (half // 4, n)
    return kernel_call(
        functools.partial(add_kernel, last), [(part, jnp.float32)] + [(part, jnp.bfloat16)] * 3
    )(kept, to_partner(sent, 1))


def scatter(mine, *out, last=0):
    got = [to_partner(x, 2 * k) for k, x in enumerate(out, 1)]
    return kernel_call(functools.partial(total_kernel, last), [(mine.shape, jnp.bfloat16)])(
        mine, *got
    )[0]


def pile_kernel(*refs):
    *pieces, out = refs
    rows = pieces[0].shape[0]
    for k, piece in enumerate(pieces):
        out[k * rows:(k + 1) * rows, :] = piece[...]


def gather_chips(x):
    pile = [((4 * x.shape[0], x.shape[1]), x.dtype)]
    return kernel_call(pile_kernel, pile)(x, *(to_partner(x, 2 * k) for k in (1, 2, 3)))[0]


def after(x, *others):
    return lax.optimization_barrier((x, *others))[0]


def by_line(z_anchor, z_other):
    rows, width = z_anchor.shape
    total = rows * 4
    plane = lax.axis_index("dp")
    middle = ((plane == 1) | (plane == 2)).astype(jnp.int32).reshape(1)
    order = lax.axis_index("feat") ^ jnp.array([0, 2, 4, 6, 1, 3, 5, 7], jnp.int32)
    across, outward = [(1, 2), (2, 1)], [(1, 0), (2, 3)]
    half = rows // 2
    flat, block = ((1, width), jnp.float32), ((rows, width), jnp.bfloat16)

    stats = kernel_call(stats_kernel, [((2, width), jnp.float32)], scratch=12)(z_anchor)[0]
    all_stats = [stats] + [
        lax.ppermute(stats, "dp", [(i, (i + k) % 4) for i in range(4)]) for k in (1, 2, 3)
    ]
    ahead = after(z_anchor, *all_stats)
    beside_in = lax.ppermute(ahead, "dp", [(i, i ^ 1) for i in range(4)])
    swapped = lax.ppermute(ahead, "dp", across)
    mean = (all_stats[0][:1] + all_stats[1][:1] + all_stats[2][:1] + all_stats[3][:1]) / 4
    spread = 0.0
    for one in all_stats:
        shift = one[:1] - mean
        spread = spread + (one[1:] + rows * shift * shift)

    def summands(n):
        return [((half, n), jnp.float32), ((half, n), jnp.bfloat16)]

    own, turned, own_square, kept, sent = kernel_call(
        own_kernel, [block, block, flat, *summands(rows + NORM)], smem=1, scratch=12
    )(order, z_anchor, mean)
    near_own = gather_chips(scatter(*halve(kept, sent, rows), last=rows))
    end = lax.ppermute(after(z_anchor, beside_in, swapped, near_own), "dp", [(0, 3), (3, 0)])

    beside, beside_square, swapped, swapped_square, kept, sent = kernel_call(
        first_kernel, [block, flat, block, flat, *summands(rows)],
        smem=2, scratch=12, temps=[block],
    )(order, middle, after(turned, near_own), beside_in, swapped, mean)
    first = scatter(*halve(kept, sent))
    kept_early, sent_early = kernel_call(
        early_kernel, summands(2 * rows), smem=1, scratch=12
    )(middle, after(turned, first), beside, swapped)
    near = after(gather_chips(first), sent_early)
    ready = kernel_call(
        push_kernel, [block, block], smem=2, scratch=12, temps=[((rows, rows), jnp.bfloat16)]
    )(order, middle, near, to_partner(near, 1), beside, swapped, beside_square, swapped_square)
    out, over = ready
    pushed = [
        lax.ppermute(out, "dp", outward), lax.ppermute(after(over, end), "dp", across)
    ]

    end, end_square, kept, sent = kernel_call(
        late_kernel, [block, flat, summands(rows)[0], summands(2 * rows)[1]], smem=1, scratch=12
    )(middle, after(turned, *ready), sent_early, end, mean)
    eighth = (rows // 8, 2 * rows)
    halved = kernel_call(
        add_either_kernel, [(eighth, jnp.float32)] + [(eighth, jnp.bfloat16)] * 3, smem=1
    )(middle, kept_early, kept, to_partner(sent, 1))
    result = ((rows, width), jnp.float32)
    held = kernel_call(
        functools.partial(held_kernel, total), [result],
        smem=2, scratch=12, temps=[((rows, rows + NORM), jnp.bfloat16)],
    )(
        order, middle, near_own, to_partner(near_own, 1), own, z_anchor, z_other,
        own_square, beside_square, swapped_square, after(end_square, halved[0]), mean, spread,
    )[0]
    got = [to_partner(x, 2 * k) for k, x in enumerate(halved[1:], 1)]
    second = kernel_call(total_either_kernel, [(eighth, jnp.bfloat16)], smem=1)(
        middle, first, halved[0], *got
    )[0]
    near = after(gather_chips(after(second, held)), *pushed)
    return kernel_call(
        functools.partial(last_kernel, total), [result],
        smem=2, scratch=12, temps=[((rows, 2 * rows), jnp.bfloat16)],
    )(
        order, middle, near, to_partner(near, 1), beside, swapped, end, held, *pushed
    )[0]


def by_gather(z_anchor, z_other):
    rows_here, width = z_anchor.shape
    groups = lax.axis_size("dp")
    total = rows_here * groups
    mine = lax.axis_index("dp") * rows_here
    column = lax.all_gather(z_anchor, "dp", axis=0, tiled=True).astype(jnp.float32)
    mean = jnp.sum(column, axis=0) / total
    centered_all = column - mean
    variance = jnp.sum(centered_all * centered_all, axis=0) / (total - 1)
    rounded_all = centered_all.astype(jnp.bfloat16)
    widened = rounded_all.astype(jnp.float32)
    own_square = jnp.sum(widened * widened, axis=0)
    rounded = lax.dynamic_slice_in_dim(rounded_all, mine, rows_here, 0)
    inner = lax.psum(gram(rounded, rounded_all).astype(jnp.bfloat16), "feat")
    product = jnp.dot(inner, rounded_all, preferred_element_type=jnp.float32)
    product = product - rounded.astype(jnp.float32) * own_square
    return finish(z_anchor, z_other, mean, variance, total, product)


def finish(z_anchor, z_other, mean, variance, total, product):
    coef = 2.0 * total / (25.0 * (total - 1)) / (total - 1)
    anchor = z_anchor.astype(jnp.float32)
    centered = anchor - mean
    deviation = jnp.sqrt(variance + 0.0001)
    hinge = jnp.where(deviation < 1.0, centered / deviation, 0.0)
    factor = total / (4.0 * (total - 1))
    return anchor - z_other.astype(jnp.float32) - factor * hinge + coef * product


def solution(mesh):
    placed = (P("dp", "feat"), P("dp", "feat"))
    in_line = mesh.shape["dp"] == 4 and mesh.shape["feat"] == 8
    return jax.shard_map(
        by_line if in_line else by_gather,
        mesh=mesh, in_specs=placed, out_specs=P("dp", "feat"), check_vma=False,
    )
```

```python
import functools
import math

import jax
import jax.numpy as jnp
from jax import lax
from jax.experimental import pallas as pl
from jax.experimental.pallas import tpu as pltpu
from jax.sharding import PartitionSpec as P

NORM = 128


def kernel_call(body, outs, smem=0, scratch=4, temps=()):
    def call(*args):
        space = [pltpu.SMEM] * smem + [pltpu.VMEM] * (len(args) - smem)
        return pl.pallas_call(
            body,
            out_shape=[jax.ShapeDtypeStruct(s, t) for s, t in outs],
            in_specs=[pl.BlockSpec(memory_space=m) for m in space],
            out_specs=[pl.BlockSpec(memory_space=pltpu.VMEM) for _ in outs],
            scratch_shapes=[pltpu.VMEM(s, t) for s, t in temps],
            compiler_params=pltpu.CompilerParams(vmem_limit_bytes=scratch * 1024 * 1024),
            cost_estimate=pl.CostEstimate(flops=0, bytes_accessed=0, transcendentals=0),
        )(*args)

    return call


def gram(left, right):
    return lax.dot_general(
        left, right, (((1,), (1,)), ((), ())), preferred_element_type=jnp.float32
    )


def dot_t(left, right):
    return lax.dot_general(
        left, right, (((0,), (0,)), ((), ())), preferred_element_type=jnp.float32
    )


def dot(left, right):
    return jnp.dot(left, right, preferred_element_type=jnp.float32)


def centered_into(out, block, mean, square):
    out[...] = (block[...].astype(jnp.float32) - mean).astype(jnp.bfloat16)
    wide = out[...].astype(jnp.float32)
    square[...] = jnp.sum(wide * wide, axis=0, keepdims=True)


def high_low(n, like):
    high = n.astype(jnp.bfloat16).astype(jnp.float32)
    lane = lax.broadcasted_iota(jnp.int32, like, 1)
    return jnp.where(lane == 0, high, jnp.where(lane == 1, n - high, 0.0))


def turn_into(turned, order, block):
    eighth = block.shape[0] // 8
    for k in range(8):
        start = pl.multiple_of(order[k] * eighth, eighth)
        turned[k * eighth:(k + 1) * eighth, :] = block[pl.ds(start, eighth), :]


def own_kernel(order, z, mean, own, turned, square, kept, sent):
    rows = z.shape[0]
    eighth, half = rows // 8, rows // 2
    centered_into(own, z, mean[...], square)
    turn_into(turned, order, own)
    inner = gram(turned[...], own[...])
    wide = turned[...].astype(jnp.float32)
    norm = jnp.sum(wide * wide, axis=1, keepdims=True)
    column = lax.broadcasted_iota(jnp.int32, (eighth, rows), 1)
    row = lax.broadcasted_iota(jnp.int32, (eighth, rows), 0)
    for k in range(8):
        here = slice(k * eighth, (k + 1) * eighth)
        off = jnp.where(column == row + order[k] * eighth, 0.0, inner[here])
        if k < 4:
            kept[here, :rows] = off
        else:
            sent[k * eighth - half:(k + 1) * eighth - half, :rows] = off.astype(jnp.bfloat16)
    lane = lax.broadcasted_iota(jnp.int32, (half, NORM), 1)
    kept[:, rows:] = jnp.where(lane == 0, norm[:half], 0.0)
    sent[:, rows:] = high_low(norm[half:], (half, NORM)).astype(jnp.bfloat16)


def split_sum(inner, kept, sent, here):
    half = kept.shape[0]
    kept[:, here] = inner[:half]
    sent[:, here] = inner[half:].astype(jnp.bfloat16)


def first_kernel(
    order, middle, turned, beside_in, opposite_in, mean,
    beside, beside_square, opposite, opposite_square, kept, sent, turned_beside,
):
    centered_into(beside, beside_in, mean[...], beside_square)

    @pl.when(middle[0] == 1)
    def _():
        centered_into(opposite, opposite_in, mean[...], opposite_square)
        turn_into(turned_beside, order, beside)
        split_sum(gram(turned_beside[...], opposite[...]), kept, sent, slice(None))

    @pl.when(middle[0] == 0)
    def _():
        split_sum(gram(turned[...], beside[...]), kept, sent, slice(None))


def early_kernel(middle, turned, beside, opposite, kept, sent):
    rows = beside.shape[0]

    @pl.when(middle[0] == 1)
    def _():
        split_sum(gram(turned[...], opposite[...]), kept, sent, slice(0, rows))
        split_sum(gram(turned[...], beside[...]), kept, sent, slice(rows, 2 * rows))


def late_kernel(middle, turned, sent_early, end_in, mean, end, square, kept, sent):
    rows = end.shape[0]

    @pl.when(middle[0] == 1)
    def _():
        sent[...] = sent_early[...]

    @pl.when(middle[0] == 0)
    def _():
        centered_into(end, end_in, mean[...], square)
        split_sum(gram(turned[...], end[...]), kept, sent, slice(0, rows))
        sent[:, rows:] = jnp.zeros_like(sent[:, rows:])


def stats_kernel(z, out):
    rows = z.shape[0]
    base = z[:16, :].astype(jnp.float32)[:1]
    apart = z[...].astype(jnp.float32) - base
    total = jnp.sum(apart, axis=0, keepdims=True)
    away = total / rows
    out[:1, :] = base + away
    out[1:, :] = jnp.sum(apart * apart, axis=0, keepdims=True) - total * away


def with_norm(x, last):
    if not last:
        return x
    tail = x[:, last:]
    split = high_low(jnp.sum(tail, axis=1, keepdims=True), tail.shape)
    return jnp.concatenate([x[:, :last], split], axis=1)


def add_kernel(last, kept, got, mine, *out):
    total = with_norm(kept[...] + got[...].astype(jnp.float32), last)
    quarter = mine.shape[0]
    mine[...] = total[:quarter]
    for k, ref in enumerate(out, 1):
        ref[...] = total[k * quarter:(k + 1) * quarter].astype(jnp.bfloat16)


def add_either_kernel(middle, kept_early, kept, got, mine, *out):
    quarter, rows = mine.shape[0], kept.shape[1]

    def put(total, here):
        mine[:, here] = total[:quarter]
        for k, ref in enumerate(out, 1):
            ref[:, here] = total[k * quarter:(k + 1) * quarter].astype(jnp.bfloat16)

    @pl.when(middle[0] == 1)
    def _():
        put(kept_early[...] + got[...].astype(jnp.float32), slice(None))

    @pl.when(middle[0] == 0)
    def _():
        put(kept[...] + got[:, :rows].astype(jnp.float32), slice(0, rows))
        put(jnp.zeros((4 * quarter, rows), jnp.float32), slice(rows, 2 * rows))


def total_kernel(last, mine, a, b, c, out):
    total = mine[...] + a[...].astype(jnp.float32)
    total = total + b[...].astype(jnp.float32) + c[...].astype(jnp.float32)
    out[...] = with_norm(total, last).astype(jnp.bfloat16)


def total_either_kernel(middle, first, mine, a, b, c, out):
    rows = first.shape[1]

    def put(here):
        total = mine[:, here] + a[:, here].astype(jnp.float32)
        total = total + b[:, here].astype(jnp.float32) + c[:, here].astype(jnp.float32)
        out[:, here] = total.astype(jnp.bfloat16)

    put(slice(0, rows))
    pl.when(middle[0] == 1)(lambda: put(slice(rows, 2 * rows)))

    @pl.when(middle[0] == 0)
    def _():
        out[:, rows:] = first[...]


def place_into(out, order, near, far):
    eighth = out.shape[0] // 8
    for k in range(4):
        here = slice(k * eighth, (k + 1) * eighth)
        out[pl.ds(pl.multiple_of(order[k] * eighth, eighth), eighth), :] = near[here, :]
        out[pl.ds(pl.multiple_of(order[4 + k] * eighth, eighth), eighth), :] = far[here, :]


def push_kernel(
    order, middle, near, far, beside, opposite, beside_square, opposite_square, out, over, inner
):
    width = beside.shape[1]

    @pl.when(middle[0] == 1)
    def _():
        place_into(inner, order, near, far)
        for k in range(2):
            here = slice(k * width // 2, (k + 1) * width // 2)
            outward = dot(inner[...], opposite[:, here])
            outward = outward - beside[:, here].astype(jnp.float32) * opposite_square[:, here]
            out[:, here] = outward.astype(jnp.bfloat16)
            across = dot_t(inner[...], beside[:, here])
            across = across - opposite[:, here].astype(jnp.float32) * beside_square[:, here]
            over[:, here] = across.astype(jnp.bfloat16)


def coefficient(total):
    return 2.0 * total / (25.0 * (total - 1)) / (total - 1)


def held_kernel(
    total, order, middle, near, far, own, z, other,
    own_square, beside_square, swapped_square, end_square, mean, spread, held, with_own,
):
    rows, width = own.shape
    place_into(with_own, order, near, far)
    norm = jnp.sum(with_own[:, rows:].astype(jnp.float32), axis=1, keepdims=True)
    for k in range(4):
        here = slice(k * width // 4, (k + 1) * width // 4)
        anchor = z[:, here].astype(jnp.float32)
        deviation = jnp.sqrt(spread[:, here] / (total - 1) + 0.0001)
        centered = anchor - mean[:, here]
        hinge = jnp.where(deviation < 1.0, centered / deviation, 0.0)
        plain = anchor - other[:, here].astype(jnp.float32) - total / (4.0 * (total - 1)) * hinge
        opposite = jnp.where(middle[0] == 1, swapped_square[:, here], end_square[:, here])
        square = own_square[:, here] + beside_square[:, here] + opposite
        product = dot(with_own[:, :rows], own[:, here])
        product = product + own[:, here].astype(jnp.float32) * (norm - square)
        held[:, here] = plain + coefficient(total) * product


def last_kernel(
    total, order, middle, near, far, beside, swapped, end, held, out, over, result, second
):
    rows, width = beside.shape
    place_into(second, order, near, far)

    def put(opposite, arrived):
        for k in range(4):
            here = slice(k * width // 4, (k + 1) * width // 4)
            product = dot(second[:, rows:], beside[:, here])
            product = product + dot(second[:, :rows], opposite[:, here])
            product = product + arrived[:, here].astype(jnp.float32)
            result[:, here] = held[:, here] + coefficient(total) * product

    pl.when(middle[0] == 1)(lambda: put(swapped, over))
    pl.when(middle[0] == 0)(lambda: put(end, out))


def to_partner(x, step):
    return lax.ppermute(x, "feat", [(i, i ^ step) for i in range(8)])


def halve(kept, sent, last=0):
    half, n = kept.shape
    part = (half // 4, n)
    return kernel_call(
        functools.partial(add_kernel, last), [(part, jnp.float32)] + [(part, jnp.bfloat16)] * 3
    )(kept, to_partner(sent, 1))


def scatter(mine, *out, last=0):
    got = [to_partner(x, 2 * k) for k, x in enumerate(out, 1)]
    return kernel_call(functools.partial(total_kernel, last), [(mine.shape, jnp.bfloat16)])(
        mine, *got
    )[0]


def pile_kernel(*refs):
    *pieces, out = refs
    rows = pieces[0].shape[0]
    for k, piece in enumerate(pieces):
        out[k * rows:(k + 1) * rows, :] = piece[...]


def gather_chips(x):
    pile = [((4 * x.shape[0], x.shape[1]), x.dtype)]
    return kernel_call(pile_kernel, pile)(x, *(to_partner(x, 2 * k) for k in (1, 2, 3)))[0]


def after(x, *others):
    return lax.optimization_barrier((x, *others))[0]


def by_line(z_anchor, z_other):
    rows, width = z_anchor.shape
    total = rows * 4
    plane = lax.axis_index("dp")
    middle = ((plane == 1) | (plane == 2)).astype(jnp.int32).reshape(1)
    order = lax.axis_index("feat") ^ jnp.array([0, 2, 4, 6, 1, 3, 5, 7], jnp.int32)
    across, outward = [(1, 2), (2, 1)], [(1, 0), (2, 3)]
    half = rows // 2
    flat, block = ((1, width), jnp.float32), ((rows, width), jnp.bfloat16)

    stats = kernel_call(stats_kernel, [((2, width), jnp.float32)], scratch=12)(z_anchor)[0]
    all_stats = [stats] + [
        lax.ppermute(stats, "dp", [(i, (i + k) % 4) for i in range(4)]) for k in (1, 2, 3)
    ]
    ahead = after(z_anchor, stats)
    beside_in = lax.ppermute(ahead, "dp", [(i, i ^ 1) for i in range(4)])
    swapped = lax.ppermute(ahead, "dp", across)
    mean = (all_stats[0][:1] + all_stats[1][:1] + all_stats[2][:1] + all_stats[3][:1]) / 4
    spread = 0.0
    for one in all_stats:
        shift = one[:1] - mean
        spread = spread + (one[1:] + rows * shift * shift)

    def summands(n):
        return [((half, n), jnp.float32), ((half, n), jnp.bfloat16)]

    own, turned, own_square, kept, sent = kernel_call(
        own_kernel, [block, block, flat, *summands(rows + NORM)], smem=1, scratch=12
    )(order, z_anchor, mean)
    near_own = scatter(*halve(kept, sent, rows), last=rows)
    near_own = jnp.concatenate([near_own] + [to_partner(near_own, 2 * k) for k in (1, 2, 3)])
    end = lax.ppermute(after(z_anchor, swapped, near_own), "dp", [(0, 3), (3, 0)])

    beside, beside_square, swapped, swapped_square, kept, sent = kernel_call(
        first_kernel, [block, flat, block, flat, *summands(rows)],
        smem=2, scratch=12, temps=[block],
    )(order, middle, after(turned, near_own), beside_in, swapped, mean)
    first = scatter(*halve(kept, sent))
    kept_early, sent_early = kernel_call(
        early_kernel, summands(2 * rows), smem=1, scratch=12
    )(middle, after(turned, first), beside, swapped)
    near = after(gather_chips(first), sent_early)
    ready = kernel_call(
        push_kernel, [block, block], smem=2, scratch=12, temps=[((rows, rows), jnp.bfloat16)]
    )(order, middle, near, to_partner(near, 1), beside, swapped, beside_square, swapped_square)
    out, over = ready
    pushed = [
        lax.ppermute(out, "dp", outward), lax.ppermute(after(over, end), "dp", across)
    ]

    end, end_square, kept, sent = kernel_call(
        late_kernel, [block, flat, summands(rows)[0], summands(2 * rows)[1]], smem=1, scratch=12
    )(middle, after(turned, *ready), sent_early, end, mean)
    eighth = (rows // 8, 2 * rows)
    halved = kernel_call(
        add_either_kernel, [(eighth, jnp.float32)] + [(eighth, jnp.bfloat16)] * 3, smem=1
    )(middle, kept_early, kept, to_partner(sent, 1))
    result = ((rows, width), jnp.float32)
    held = kernel_call(
        functools.partial(held_kernel, total), [result],
        smem=2, scratch=12, temps=[((rows, rows + NORM), jnp.bfloat16)],
    )(
        order, middle, near_own, to_partner(near_own, 1), own, z_anchor, z_other,
        own_square, beside_square, swapped_square, after(end_square, halved[0]), mean, spread,
    )[0]
    got = [to_partner(x, 2 * k) for k, x in enumerate(halved[1:], 1)]
    second = kernel_call(total_either_kernel, [(eighth, jnp.bfloat16)], smem=1)(
        middle, first, halved[0], *got
    )[0]
    near = after(gather_chips(after(second, held)), *pushed)
    return kernel_call(
        functools.partial(last_kernel, total), [result],
        smem=2, scratch=12, temps=[((rows, 2 * rows), jnp.bfloat16)],
    )(
        order, middle, near, to_partner(near, 1), beside, swapped, end, held, *pushed
    )[0]


def by_gather(z_anchor, z_other):
    rows_here, width = z_anchor.shape
    groups = lax.axis_size("dp")
    total = rows_here * groups
    mine = lax.axis_index("dp") * rows_here
    column = lax.all_gather(z_anchor, "dp", axis=0, tiled=True).astype(jnp.float32)
    mean = jnp.sum(column, axis=0) / total
    centered_all = column - mean
    variance = jnp.sum(centered_all * centered_all, axis=0) / (total - 1)
    rounded_all = centered_all.astype(jnp.bfloat16)
    widened = rounded_all.astype(jnp.float32)
    own_square = jnp.sum(widened * widened, axis=0)
    rounded = lax.dynamic_slice_in_dim(rounded_all, mine, rows_here, 0)
    inner = lax.psum(gram(rounded, rounded_all).astype(jnp.bfloat16), "feat")
    product = jnp.dot(inner, rounded_all, preferred_element_type=jnp.float32)
    product = product - rounded.astype(jnp.float32) * own_square
    return finish(z_anchor, z_other, mean, variance, total, product)


def finish(z_anchor, z_other, mean, variance, total, product):
    coef = 2.0 * total / (25.0 * (total - 1)) / (total - 1)
    anchor = z_anchor.astype(jnp.float32)
    centered = anchor - mean
    deviation = jnp.sqrt(variance + 0.0001)
    hinge = jnp.where(deviation < 1.0, centered / deviation, 0.0)
    factor = total / (4.0 * (total - 1))
    return anchor - z_other.astype(jnp.float32) - factor * hinge + coef * product


def solution(mesh):
    placed = (P("dp", "feat"), P("dp", "feat"))
    in_line = mesh.shape["dp"] == 4 and mesh.shape["feat"] == 8
    return jax.shard_map(
        by_line if in_line else by_gather,
        mesh=mesh, in_specs=placed, out_specs=P("dp", "feat"), check_vma=False,
    )
```

```python
import functools
import math

import jax
import jax.numpy as jnp
from jax import lax
from jax.experimental import pallas as pl
from jax.experimental.pallas import tpu as pltpu
from jax.sharding import PartitionSpec as P

NORM = 128


def kernel_call(body, outs, smem=0, scratch=4, temps=()):
    def call(*args):
        space = [pltpu.SMEM] * smem + [pltpu.VMEM] * (len(args) - smem)
        return pl.pallas_call(
            body,
            out_shape=[jax.ShapeDtypeStruct(s, t) for s, t in outs],
            in_specs=[pl.BlockSpec(memory_space=m) for m in space],
            out_specs=[pl.BlockSpec(memory_space=pltpu.VMEM) for _ in outs],
            scratch_shapes=[pltpu.VMEM(s, t) for s, t in temps],
            compiler_params=pltpu.CompilerParams(vmem_limit_bytes=scratch * 1024 * 1024),
            cost_estimate=pl.CostEstimate(flops=0, bytes_accessed=0, transcendentals=0),
        )(*args)

    return call


def gram(left, right):
    return lax.dot_general(
        left, right, (((1,), (1,)), ((), ())), preferred_element_type=jnp.float32
    )


def dot_t(left, right):
    return lax.dot_general(
        left, right, (((0,), (0,)), ((), ())), preferred_element_type=jnp.float32
    )


def dot(left, right):
    return jnp.dot(left, right, preferred_element_type=jnp.float32)


def centered_into(out, block, mean, square):
    out[...] = (block[...].astype(jnp.float32) - mean).astype(jnp.bfloat16)
    wide = out[...].astype(jnp.float32)
    square[...] = jnp.sum(wide * wide, axis=0, keepdims=True)


def high_low(n, like):
    high = n.astype(jnp.bfloat16).astype(jnp.float32)
    lane = lax.broadcasted_iota(jnp.int32, like, 1)
    return jnp.where(lane == 0, high, jnp.where(lane == 1, n - high, 0.0))


def turn_into(turned, order, block):
    eighth = block.shape[0] // 8
    for k in range(8):
        start = pl.multiple_of(order[k] * eighth, eighth)
        turned[k * eighth:(k + 1) * eighth, :] = block[pl.ds(start, eighth), :]


def own_kernel(order, z, mean, own, turned, square, kept, sent):
    rows = z.shape[0]
    eighth, half = rows // 8, rows // 2
    centered_into(own, z, mean[...], square)
    turn_into(turned, order, own)
    inner = gram(turned[...], own[...])
    wide = turned[...].astype(jnp.float32)
    norm = jnp.sum(wide * wide, axis=1, keepdims=True)
    column = lax.broadcasted_iota(jnp.int32, (eighth, rows), 1)
    row = lax.broadcasted_iota(jnp.int32, (eighth, rows), 0)
    for k in range(8):
        here = slice(k * eighth, (k + 1) * eighth)
        off = jnp.where(column == row + order[k] * eighth, 0.0, inner[here])
        if k < 4:
            kept[here, :rows] = off
        else:
            sent[k * eighth - half:(k + 1) * eighth - half, :rows] = off.astype(jnp.bfloat16)
    lane = lax.broadcasted_iota(jnp.int32, (half, NORM), 1)
    kept[:, rows:] = jnp.where(lane == 0, norm[:half], 0.0)
    sent[:, rows:] = high_low(norm[half:], (half, NORM)).astype(jnp.bfloat16)


def split_sum(inner, kept, sent, here):
    half = kept.shape[0]
    kept[:, here] = inner[:half]
    sent[:, here] = inner[half:].astype(jnp.bfloat16)


def first_kernel(
    order, middle, turned, beside_in, opposite_in, mean,
    beside, beside_square, opposite, opposite_square, kept, sent, turned_beside,
):
    centered_into(beside, beside_in, mean[...], beside_square)

    @pl.when(middle[0] == 1)
    def _():
        centered_into(opposite, opposite_in, mean[...], opposite_square)
        turn_into(turned_beside, order, beside)
        split_sum(gram(turned_beside[...], opposite[...]), kept, sent, slice(None))

    @pl.when(middle[0] == 0)
    def _():
        split_sum(gram(turned[...], beside[...]), kept, sent, slice(None))


def early_kernel(middle, turned, beside, opposite, kept, sent):
    rows = beside.shape[0]

    @pl.when(middle[0] == 1)
    def _():
        split_sum(gram(turned[...], opposite[...]), kept, sent, slice(0, rows))
        split_sum(gram(turned[...], beside[...]), kept, sent, slice(rows, 2 * rows))


def late_kernel(middle, turned, sent_early, end_in, mean, end, square, kept, sent):
    rows = end.shape[0]

    @pl.when(middle[0] == 1)
    def _():
        sent[...] = sent_early[...]

    @pl.when(middle[0] == 0)
    def _():
        centered_into(end, end_in, mean[...], square)
        split_sum(gram(turned[...], end[...]), kept, sent, slice(0, rows))
        sent[:, rows:] = jnp.zeros_like(sent[:, rows:])


def stats_kernel(z, out):
    rows = z.shape[0]
    base = z[:16, :].astype(jnp.float32)[:1]
    apart = z[...].astype(jnp.float32) - base
    total = jnp.sum(apart, axis=0, keepdims=True)
    away = total / rows
    out[:1, :] = base + away
    out[1:, :] = jnp.sum(apart * apart, axis=0, keepdims=True) - total * away


def with_norm(x, last):
    if not last:
        return x
    tail = x[:, last:]
    split = high_low(jnp.sum(tail, axis=1, keepdims=True), tail.shape)
    return jnp.concatenate([x[:, :last], split], axis=1)


def add_kernel(last, kept, got, mine, *out):
    total = with_norm(kept[...] + got[...].astype(jnp.float32), last)
    quarter = mine.shape[0]
    mine[...] = total[:quarter]
    for k, ref in enumerate(out, 1):
        ref[...] = total[k * quarter:(k + 1) * quarter].astype(jnp.bfloat16)


def add_either_kernel(middle, kept_early, kept, got, mine, *out):
    quarter, rows = mine.shape[0], kept.shape[1]

    def put(total, here):
        mine[:, here] = total[:quarter]
        for k, ref in enumerate(out, 1):
            ref[:, here] = total[k * quarter:(k + 1) * quarter].astype(jnp.bfloat16)

    @pl.when(middle[0] == 1)
    def _():
        put(kept_early[...] + got[...].astype(jnp.float32), slice(None))

    @pl.when(middle[0] == 0)
    def _():
        put(kept[...] + got[:, :rows].astype(jnp.float32), slice(0, rows))
        put(jnp.zeros((4 * quarter, rows), jnp.float32), slice(rows, 2 * rows))


def total_kernel(last, mine, a, b, c, out):
    total = mine[...] + a[...].astype(jnp.float32)
    total = total + b[...].astype(jnp.float32) + c[...].astype(jnp.float32)
    out[...] = with_norm(total, last).astype(jnp.bfloat16)


def total_either_kernel(middle, first, mine, a, b, c, out):
    rows = first.shape[1]

    def put(here):
        total = mine[:, here] + a[:, here].astype(jnp.float32)
        total = total + b[:, here].astype(jnp.float32) + c[:, here].astype(jnp.float32)
        out[:, here] = total.astype(jnp.bfloat16)

    put(slice(0, rows))
    pl.when(middle[0] == 1)(lambda: put(slice(rows, 2 * rows)))

    @pl.when(middle[0] == 0)
    def _():
        out[:, rows:] = first[...]


def place_into(out, order, near, far):
    eighth = out.shape[0] // 8
    for k in range(4):
        here = slice(k * eighth, (k + 1) * eighth)
        out[pl.ds(pl.multiple_of(order[k] * eighth, eighth), eighth), :] = near[here, :]
        out[pl.ds(pl.multiple_of(order[4 + k] * eighth, eighth), eighth), :] = far[here, :]


def push_kernel(
    order, middle, near, far, beside, opposite, beside_square, opposite_square, out, over, inner
):
    width = beside.shape[1]

    @pl.when(middle[0] == 1)
    def _():
        place_into(inner, order, near, far)
        for k in range(2):
            here = slice(k * width // 2, (k + 1) * width // 2)
            outward = dot(inner[...], opposite[:, here])
            outward = outward - beside[:, here].astype(jnp.float32) * opposite_square[:, here]
            out[:, here] = outward.astype(jnp.bfloat16)
            across = dot_t(inner[...], beside[:, here])
            across = across - opposite[:, here].astype(jnp.float32) * beside_square[:, here]
            over[:, here] = across.astype(jnp.bfloat16)


def coefficient(total):
    return 2.0 * total / (25.0 * (total - 1)) / (total - 1)


def held_kernel(
    total, order, middle, near, far, own, z, other,
    own_square, beside_square, swapped_square, end_square, mean, spread, held, with_own,
):
    rows, width = own.shape
    place_into(with_own, order, near, far)
    norm = jnp.sum(with_own[:, rows:].astype(jnp.float32), axis=1, keepdims=True)
    for k in range(4):
        here = slice(k * width // 4, (k + 1) * width // 4)
        anchor = z[:, here].astype(jnp.float32)
        deviation = jnp.sqrt(spread[:, here] / (total - 1) + 0.0001)
        centered = anchor - mean[:, here]
        hinge = jnp.where(deviation < 1.0, centered / deviation, 0.0)
        plain = anchor - other[:, here].astype(jnp.float32) - total / (4.0 * (total - 1)) * hinge
        opposite = jnp.where(middle[0] == 1, swapped_square[:, here], end_square[:, here])
        square = own_square[:, here] + beside_square[:, here] + opposite
        product = dot(with_own[:, :rows], own[:, here])
        product = product + own[:, here].astype(jnp.float32) * (norm - square)
        held[:, here] = plain + coefficient(total) * product


def last_kernel(
    total, order, middle, near, far, beside, swapped, end, held, out, over, result, second
):
    rows, width = beside.shape
    place_into(second, order, near, far)

    def put(opposite, arrived):
        for k in range(4):
            here = slice(k * width // 4, (k + 1) * width // 4)
            product = dot(second[:, rows:], beside[:, here])
            product = product + dot(second[:, :rows], opposite[:, here])
            product = product + arrived[:, here].astype(jnp.float32)
            result[:, here] = held[:, here] + coefficient(total) * product

    pl.when(middle[0] == 1)(lambda: put(swapped, over))
    pl.when(middle[0] == 0)(lambda: put(end, out))


def to_partner(x, step):
    return lax.ppermute(x, "feat", [(i, i ^ step) for i in range(8)])


def halve(kept, sent, last=0):
    half, n = kept.shape
    part = (half // 4, n)
    return kernel_call(
        functools.partial(add_kernel, last), [(part, jnp.float32)] + [(part, jnp.bfloat16)] * 3
    )(kept, to_partner(sent, 1))


def scatter(mine, *out, last=0):
    got = [to_partner(x, 2 * k) for k, x in enumerate(out, 1)]
    return kernel_call(functools.partial(total_kernel, last), [(mine.shape, jnp.bfloat16)])(
        mine, *got
    )[0]


def pile_kernel(*refs):
    *pieces, out = refs
    rows = pieces[0].shape[0]
    for k, piece in enumerate(pieces):
        out[k * rows:(k + 1) * rows, :] = piece[...]


def gather_chips(x):
    pile = [((4 * x.shape[0], x.shape[1]), x.dtype)]
    return kernel_call(pile_kernel, pile)(x, *(to_partner(x, 2 * k) for k in (1, 2, 3)))[0]


def after(x, *others):
    return lax.optimization_barrier((x, *others))[0]


def by_line(z_anchor, z_other):
    rows, width = z_anchor.shape
    total = rows * 4
    plane = lax.axis_index("dp")
    middle = ((plane == 1) | (plane == 2)).astype(jnp.int32).reshape(1)
    order = lax.axis_index("feat") ^ jnp.array([0, 2, 4, 6, 1, 3, 5, 7], jnp.int32)
    across, outward = [(1, 2), (2, 1)], [(1, 0), (2, 3)]
    half = rows // 2
    flat, block = ((1, width), jnp.float32), ((rows, width), jnp.bfloat16)

    stats = kernel_call(stats_kernel, [((2, width), jnp.float32)], scratch=12)(z_anchor)[0]
    all_stats = [stats] + [
        lax.ppermute(stats, "dp", [(i, (i + k) % 4) for i in range(4)]) for k in (1, 2, 3)
    ]
    ahead = after(z_anchor, stats)
    beside_in = lax.ppermute(ahead, "dp", [(i, i ^ 1) for i in range(4)])
    swapped = lax.ppermute(ahead, "dp", across)
    mean = (all_stats[0][:1] + all_stats[1][:1] + all_stats[2][:1] + all_stats[3][:1]) / 4
    spread = 0.0
    for one in all_stats:
        shift = one[:1] - mean
        spread = spread + (one[1:] + rows * shift * shift)

    def summands(n):
        return [((half, n), jnp.float32), ((half, n), jnp.bfloat16)]

    own, turned, own_square, kept, sent = kernel_call(
        own_kernel, [block, block, flat, *summands(rows + NORM)], smem=1, scratch=12
    )(order, z_anchor, mean)
    near_own = scatter(*halve(kept, sent, rows), last=rows)
    near_own = jnp.concatenate([near_own] + [to_partner(near_own, 2 * k) for k in (1, 2, 3)])
    end = lax.ppermute(after(z_anchor, beside_in, swapped, near_own), "dp", [(0, 3), (3, 0)])

    beside, beside_square, swapped, swapped_square, kept, sent = kernel_call(
        first_kernel, [block, flat, block, flat, *summands(rows)],
        smem=2, scratch=12, temps=[block],
    )(order, middle, after(turned, near_own), beside_in, swapped, mean)
    first = scatter(*halve(kept, sent))
    kept_early, sent_early = kernel_call(
        early_kernel, summands(2 * rows), smem=1, scratch=12
    )(middle, after(turned, first), beside, swapped)
    near = after(gather_chips(first), sent_early)
    ready = kernel_call(
        push_kernel, [block, block], smem=2, scratch=12, temps=[((rows, rows), jnp.bfloat16)]
    )(order, middle, near, to_partner(near, 1), beside, swapped, beside_square, swapped_square)
    out, over = ready
    pushed = [
        lax.ppermute(out, "dp", outward), lax.ppermute(after(over, end), "dp", across)
    ]

    end, end_square, kept, sent = kernel_call(
        late_kernel, [block, flat, summands(rows)[0], summands(2 * rows)[1]], smem=1, scratch=12
    )(middle, after(turned, *ready), sent_early, end, mean)
    eighth = (rows // 8, 2 * rows)
    halved = kernel_call(
        add_either_kernel, [(eighth, jnp.float32)] + [(eighth, jnp.bfloat16)] * 3, smem=1
    )(middle, kept_early, kept, to_partner(sent, 1))
    result = ((rows, width), jnp.float32)
    held = kernel_call(
        functools.partial(held_kernel, total), [result],
        smem=2, scratch=12, temps=[((rows, rows + NORM), jnp.bfloat16)],
    )(
        order, middle, near_own, to_partner(near_own, 1), own, z_anchor, z_other,
        own_square, beside_square, swapped_square, after(end_square, halved[0]), mean, spread,
    )[0]
    got = [to_partner(x, 2 * k) for k, x in enumerate(halved[1:], 1)]
    second = kernel_call(total_either_kernel, [(eighth, jnp.bfloat16)], smem=1)(
        middle, first, halved[0], *got
    )[0]
    near = after(gather_chips(after(second, held)), *pushed)
    return kernel_call(
        functools.partial(last_kernel, total), [result],
        smem=2, scratch=12, temps=[((rows, 2 * rows), jnp.bfloat16)],
    )(
        order, middle, near, to_partner(near, 1), beside, swapped, end, held, *pushed
    )[0]


def by_gather(z_anchor, z_other):
    rows_here, width = z_anchor.shape
    groups = lax.axis_size("dp")
    total = rows_here * groups
    mine = lax.axis_index("dp") * rows_here
    column = lax.all_gather(z_anchor, "dp", axis=0, tiled=True).astype(jnp.float32)
    mean = jnp.sum(column, axis=0) / total
    centered_all = column - mean
    variance = jnp.sum(centered_all * centered_all, axis=0) / (total - 1)
    rounded_all = centered_all.astype(jnp.bfloat16)
    widened = rounded_all.astype(jnp.float32)
    own_square = jnp.sum(widened * widened, axis=0)
    rounded = lax.dynamic_slice_in_dim(rounded_all, mine, rows_here, 0)
    inner = lax.psum(gram(rounded, rounded_all).astype(jnp.bfloat16), "feat")
    product = jnp.dot(inner, rounded_all, preferred_element_type=jnp.float32)
    product = product - rounded.astype(jnp.float32) * own_square
    return finish(z_anchor, z_other, mean, variance, total, product)


def finish(z_anchor, z_other, mean, variance, total, product):
    coef = 2.0 * total / (25.0 * (total - 1)) / (total - 1)
    anchor = z_anchor.astype(jnp.float32)
    centered = anchor - mean
    deviation = jnp.sqrt(variance + 0.0001)
    hinge = jnp.where(deviation < 1.0, centered / deviation, 0.0)
    factor = total / (4.0 * (total - 1))
    return anchor - z_other.astype(jnp.float32) - factor * hinge + coef * product


def solution(mesh):
    placed = (P("dp", "feat"), P("dp", "feat"))
    in_line = mesh.shape["dp"] == 4 and mesh.shape["feat"] == 8
    return jax.shard_map(
        by_line if in_line else by_gather,
        mesh=mesh, in_specs=placed, out_specs=P("dp", "feat"), check_vma=False,
    )
```

```python
import functools
import math

import jax
import jax.numpy as jnp
from jax import lax
from jax.experimental import pallas as pl
from jax.experimental.pallas import tpu as pltpu
from jax.sharding import PartitionSpec as P

NORM = 128


def kernel_call(body, outs, smem=0, scratch=4, temps=(), sems=0):
    def call(*args):
        space = [pltpu.SMEM] * smem + [pltpu.VMEM] * (len(args) - smem)
        return pl.pallas_call(
            body,
            out_shape=[jax.ShapeDtypeStruct(s, t) for s, t in outs],
            in_specs=[pl.BlockSpec(memory_space=m) for m in space],
            out_specs=[pl.BlockSpec(memory_space=pl.ANY if sems else pltpu.VMEM) for _ in outs],
            scratch_shapes=[pltpu.VMEM(s, t) for s, t in temps]
            + ([pltpu.SemaphoreType.DMA((sems,))] if sems else []),
            compiler_params=pltpu.CompilerParams(vmem_limit_bytes=scratch * 1024 * 1024),
            cost_estimate=pl.CostEstimate(flops=0, bytes_accessed=0, transcendentals=0),
        )(*args)

    return call


def gram(left, right):
    return lax.dot_general(
        left, right, (((1,), (1,)), ((), ())), preferred_element_type=jnp.float32
    )


def dot_t(left, right):
    return lax.dot_general(
        left, right, (((0,), (0,)), ((), ())), preferred_element_type=jnp.float32
    )


def dot(left, right):
    return jnp.dot(left, right, preferred_element_type=jnp.float32)


def centered_into(out, block, mean, square):
    out[...] = (block[...].astype(jnp.float32) - mean).astype(jnp.bfloat16)
    wide = out[...].astype(jnp.float32)
    square[...] = jnp.sum(wide * wide, axis=0, keepdims=True)


def high_low(n, like):
    high = n.astype(jnp.bfloat16).astype(jnp.float32)
    lane = lax.broadcasted_iota(jnp.int32, like, 1)
    return jnp.where(lane == 0, high, jnp.where(lane == 1, n - high, 0.0))


def turn_into(turned, order, block):
    eighth = block.shape[0] // 8
    for k in range(8):
        start = pl.multiple_of(order[k] * eighth, eighth)
        turned[k * eighth:(k + 1) * eighth, :] = block[pl.ds(start, eighth), :]


def own_kernel(order, z, mean, own, turned, square, kept, sent):
    rows = z.shape[0]
    eighth, half = rows // 8, rows // 2
    centered_into(own, z, mean[...], square)
    turn_into(turned, order, own)
    inner = gram(turned[...], own[...])
    wide = turned[...].astype(jnp.float32)
    norm = jnp.sum(wide * wide, axis=1, keepdims=True)
    column = lax.broadcasted_iota(jnp.int32, (eighth, rows), 1)
    row = lax.broadcasted_iota(jnp.int32, (eighth, rows), 0)
    for k in range(8):
        here = slice(k * eighth, (k + 1) * eighth)
        off = jnp.where(column == row + order[k] * eighth, 0.0, inner[here])
        if k < 4:
            kept[here, :rows] = off
        else:
            sent[k * eighth - half:(k + 1) * eighth - half, :rows] = off.astype(jnp.bfloat16)
    lane = lax.broadcasted_iota(jnp.int32, (half, NORM), 1)
    kept[:, rows:] = jnp.where(lane == 0, norm[:half], 0.0)
    sent[:, rows:] = high_low(norm[half:], (half, NORM)).astype(jnp.bfloat16)


def split_sum(inner, kept, sent, here):
    half = kept.shape[0]
    kept[:, here] = inner[:half]
    sent[:, here] = inner[half:].astype(jnp.bfloat16)


def first_kernel(
    order, middle, turned, beside_in, opposite_in, mean,
    beside, beside_square, opposite, opposite_square, kept, sent, turned_beside,
):
    centered_into(beside, beside_in, mean[...], beside_square)

    @pl.when(middle[0] == 1)
    def _():
        centered_into(opposite, opposite_in, mean[...], opposite_square)
        turn_into(turned_beside, order, beside)
        split_sum(gram(turned_beside[...], opposite[...]), kept, sent, slice(None))

    @pl.when(middle[0] == 0)
    def _():
        split_sum(gram(turned[...], beside[...]), kept, sent, slice(None))


def early_kernel(middle, turned, beside, opposite, kept, sent):
    rows = beside.shape[0]

    @pl.when(middle[0] == 1)
    def _():
        split_sum(gram(turned[...], opposite[...]), kept, sent, slice(0, rows))
        split_sum(gram(turned[...], beside[...]), kept, sent, slice(rows, 2 * rows))


def late_kernel(middle, turned, sent_early, end_in, mean, end, square, kept, sent):
    rows = end.shape[0]

    @pl.when(middle[0] == 1)
    def _():
        sent[...] = sent_early[...]

    @pl.when(middle[0] == 0)
    def _():
        centered_into(end, end_in, mean[...], square)
        split_sum(gram(turned[...], end[...]), kept, sent, slice(0, rows))
        sent[:, rows:] = jnp.zeros_like(sent[:, rows:])


def stats_kernel(z, out):
    rows = z.shape[0]
    base = z[:16, :].astype(jnp.float32)[:1]
    apart = z[...].astype(jnp.float32) - base
    total = jnp.sum(apart, axis=0, keepdims=True)
    away = total / rows
    out[:1, :] = base + away
    out[1:, :] = jnp.sum(apart * apart, axis=0, keepdims=True) - total * away


def with_norm(x, last):
    if not last:
        return x
    tail = x[:, last:]
    split = high_low(jnp.sum(tail, axis=1, keepdims=True), tail.shape)
    return jnp.concatenate([x[:, :last], split], axis=1)


def add_kernel(last, kept, got, mine, *out):
    total = with_norm(kept[...] + got[...].astype(jnp.float32), last)
    quarter = mine.shape[0]
    mine[...] = total[:quarter]
    for k, ref in enumerate(out, 1):
        ref[...] = total[k * quarter:(k + 1) * quarter].astype(jnp.bfloat16)


def add_either_kernel(middle, kept_early, kept, got, mine, *out):
    quarter, rows = mine.shape[0], kept.shape[1]

    def put(total, here):
        mine[:, here] = total[:quarter]
        for k, ref in enumerate(out, 1):
            ref[:, here] = total[k * quarter:(k + 1) * quarter].astype(jnp.bfloat16)

    @pl.when(middle[0] == 1)
    def _():
        put(kept_early[...] + got[...].astype(jnp.float32), slice(None))

    @pl.when(middle[0] == 0)
    def _():
        put(kept[...] + got[:, :rows].astype(jnp.float32), slice(0, rows))
        put(jnp.zeros((4 * quarter, rows), jnp.float32), slice(rows, 2 * rows))


def total_kernel(last, mine, a, b, c, out):
    total = mine[...] + a[...].astype(jnp.float32)
    total = total + b[...].astype(jnp.float32) + c[...].astype(jnp.float32)
    out[...] = with_norm(total, last).astype(jnp.bfloat16)


def total_either_kernel(middle, first, mine, a, b, c, out):
    rows = first.shape[1]

    def put(here):
        total = mine[:, here] + a[:, here].astype(jnp.float32)
        total = total + b[:, here].astype(jnp.float32) + c[:, here].astype(jnp.float32)
        out[:, here] = total.astype(jnp.bfloat16)

    put(slice(0, rows))
    pl.when(middle[0] == 1)(lambda: put(slice(rows, 2 * rows)))

    @pl.when(middle[0] == 0)
    def _():
        out[:, rows:] = first[...]


def place_into(out, order, near, far):
    eighth = out.shape[0] // 8
    for k in range(4):
        here = slice(k * eighth, (k + 1) * eighth)
        out[pl.ds(pl.multiple_of(order[k] * eighth, eighth), eighth), :] = near[here, :]
        out[pl.ds(pl.multiple_of(order[4 + k] * eighth, eighth), eighth), :] = far[here, :]


def push_kernel(
    order, middle, near, far, beside, opposite, beside_square, opposite_square, out, over, inner
):
    width = beside.shape[1]

    @pl.when(middle[0] == 1)
    def _():
        place_into(inner, order, near, far)
        for k in range(2):
            here = slice(k * width // 2, (k + 1) * width // 2)
            outward = dot(inner[...], opposite[:, here])
            outward = outward - beside[:, here].astype(jnp.float32) * opposite_square[:, here]
            out[:, here] = outward.astype(jnp.bfloat16)
            across = dot_t(inner[...], beside[:, here])
            across = across - opposite[:, here].astype(jnp.float32) * beside_square[:, here]
            over[:, here] = across.astype(jnp.bfloat16)


def coefficient(total):
    return 2.0 * total / (25.0 * (total - 1)) / (total - 1)


def held_kernel(
    total, order, middle, near, far, own, z, other,
    own_square, beside_square, swapped_square, end_square, mean, spread, held, with_own,
):
    rows, width = own.shape
    place_into(with_own, order, near, far)
    norm = jnp.sum(with_own[:, rows:].astype(jnp.float32), axis=1, keepdims=True)
    for k in range(4):
        here = slice(k * width // 4, (k + 1) * width // 4)
        anchor = z[:, here].astype(jnp.float32)
        deviation = jnp.sqrt(spread[:, here] / (total - 1) + 0.0001)
        centered = anchor - mean[:, here]
        hinge = jnp.where(deviation < 1.0, centered / deviation, 0.0)
        plain = anchor - other[:, here].astype(jnp.float32) - total / (4.0 * (total - 1)) * hinge
        opposite = jnp.where(middle[0] == 1, swapped_square[:, here], end_square[:, here])
        square = own_square[:, here] + beside_square[:, here] + opposite
        product = dot(with_own[:, :rows], own[:, here])
        product = product + own[:, here].astype(jnp.float32) * (norm - square)
        held[:, here] = plain + coefficient(total) * product


def last_kernel(
    total, order, middle, near, far, beside, swapped, end, held, out, over, result, second, made, sem
):
    rows, width = beside.shape
    place_into(second, order, near, far)

    def put(opposite, arrived):
        for k in range(4):
            here = slice(k * width // 4, (k + 1) * width // 4)
            product = dot(second[:, rows:], beside[:, here])
            product = product + dot(second[:, :rows], opposite[:, here])
            product = product + arrived[:, here].astype(jnp.float32)
            made[:, here] = held[:, here] + coefficient(total) * product
            to_result(k).start()

    def to_result(k):
        here = slice(k * width // 4, (k + 1) * width // 4)
        return pltpu.make_async_copy(made.at[:, here], result.at[:, here], sem.at[k])

    pl.when(middle[0] == 1)(lambda: put(swapped, over))
    pl.when(middle[0] == 0)(lambda: put(end, out))
    for k in range(4):
        to_result(k).wait()


def to_partner(x, step):
    return lax.ppermute(x, "feat", [(i, i ^ step) for i in range(8)])


def halve(kept, sent, last=0):
    half, n = kept.shape
    part = (half // 4, n)
    return kernel_call(
        functools.partial(add_kernel, last), [(part, jnp.float32)] + [(part, jnp.bfloat16)] * 3
    )(kept, to_partner(sent, 1))


def scatter(mine, *out, last=0):
    got = [to_partner(x, 2 * k) for k, x in enumerate(out, 1)]
    return kernel_call(functools.partial(total_kernel, last), [(mine.shape, jnp.bfloat16)])(
        mine, *got
    )[0]


def pile_kernel(*refs):
    *pieces, out = refs
    rows = pieces[0].shape[0]
    for k, piece in enumerate(pieces):
        out[k * rows:(k + 1) * rows, :] = piece[...]


def gather_chips(x):
    pile = [((4 * x.shape[0], x.shape[1]), x.dtype)]
    return kernel_call(pile_kernel, pile)(x, *(to_partner(x, 2 * k) for k in (1, 2, 3)))[0]


def after(x, *others):
    return lax.optimization_barrier((x, *others))[0]


def by_line(z_anchor, z_other):
    rows, width = z_anchor.shape
    total = rows * 4
    plane = lax.axis_index("dp")
    middle = ((plane == 1) | (plane == 2)).astype(jnp.int32).reshape(1)
    order = lax.axis_index("feat") ^ jnp.array([0, 2, 4, 6, 1, 3, 5, 7], jnp.int32)
    across, outward = [(1, 2), (2, 1)], [(1, 0), (2, 3)]
    half = rows // 2
    flat, block = ((1, width), jnp.float32), ((rows, width), jnp.bfloat16)

    stats = kernel_call(stats_kernel, [((2, width), jnp.float32)], scratch=12)(z_anchor)[0]
    all_stats = [stats] + [
        lax.ppermute(stats, "dp", [(i, (i + k) % 4) for i in range(4)]) for k in (1, 2, 3)
    ]
    ahead = after(z_anchor, stats)
    beside_in = lax.ppermute(ahead, "dp", [(i, i ^ 1) for i in range(4)])
    swapped = lax.ppermute(ahead, "dp", across)
    mean = (all_stats[0][:1] + all_stats[1][:1] + all_stats[2][:1] + all_stats[3][:1]) / 4
    spread = 0.0
    for one in all_stats:
        shift = one[:1] - mean
        spread = spread + (one[1:] + rows * shift * shift)

    def summands(n):
        return [((half, n), jnp.float32), ((half, n), jnp.bfloat16)]

    own, turned, own_square, kept, sent = kernel_call(
        own_kernel, [block, block, flat, *summands(rows + NORM)], smem=1, scratch=12
    )(order, z_anchor, mean)
    near_own = scatter(*halve(kept, sent, rows), last=rows)
    near_own = jnp.concatenate([near_own] + [to_partner(near_own, 2 * k) for k in (1, 2, 3)])
    end = lax.ppermute(after(z_anchor, beside_in, swapped, near_own), "dp", [(0, 3), (3, 0)])

    beside, beside_square, swapped, swapped_square, kept, sent = kernel_call(
        first_kernel, [block, flat, block, flat, *summands(rows)],
        smem=2, scratch=12, temps=[block],
    )(order, middle, after(turned, near_own), beside_in, swapped, mean)
    first = scatter(*halve(kept, sent))
    kept_early, sent_early = kernel_call(
        early_kernel, summands(2 * rows), smem=1, scratch=12
    )(middle, after(turned, first), beside, swapped)
    near = after(gather_chips(first), sent_early)
    ready = kernel_call(
        push_kernel, [block, block], smem=2, scratch=12, temps=[((rows, rows), jnp.bfloat16)]
    )(order, middle, near, to_partner(near, 1), beside, swapped, beside_square, swapped_square)
    out, over = ready
    pushed = [
        lax.ppermute(out, "dp", outward), lax.ppermute(after(over, end), "dp", across)
    ]

    end, end_square, kept, sent = kernel_call(
        late_kernel, [block, flat, summands(rows)[0], summands(2 * rows)[1]], smem=1, scratch=12
    )(middle, after(turned, *ready), sent_early, end, mean)
    eighth = (rows // 8, 2 * rows)
    halved = kernel_call(
        add_either_kernel, [(eighth, jnp.float32)] + [(eighth, jnp.bfloat16)] * 3, smem=1
    )(middle, kept_early, kept, to_partner(sent, 1))
    result = ((rows, width), jnp.float32)
    held = kernel_call(
        functools.partial(held_kernel, total), [result],
        smem=2, scratch=12, temps=[((rows, rows + NORM), jnp.bfloat16)],
    )(
        order, middle, near_own, to_partner(near_own, 1), own, z_anchor, z_other,
        own_square, beside_square, swapped_square, after(end_square, halved[0]), mean, spread,
    )[0]
    got = [to_partner(x, 2 * k) for k, x in enumerate(halved[1:], 1)]
    second = kernel_call(total_either_kernel, [(eighth, jnp.bfloat16)], smem=1)(
        middle, first, halved[0], *got
    )[0]
    near = after(gather_chips(after(second, held)), pushed[0])
    return kernel_call(
        functools.partial(last_kernel, total), [result],
        smem=2, scratch=12, temps=[((rows, 2 * rows), jnp.bfloat16), result], sems=4,
    )(
        order, middle, near, to_partner(near, 1), beside, swapped, end, held, *pushed
    )[0]


def by_gather(z_anchor, z_other):
    rows_here, width = z_anchor.shape
    groups = lax.axis_size("dp")
    total = rows_here * groups
    mine = lax.axis_index("dp") * rows_here
    column = lax.all_gather(z_anchor, "dp", axis=0, tiled=True).astype(jnp.float32)
    mean = jnp.sum(column, axis=0) / total
    centered_all = column - mean
    variance = jnp.sum(centered_all * centered_all, axis=0) / (total - 1)
    rounded_all = centered_all.astype(jnp.bfloat16)
    widened = rounded_all.astype(jnp.float32)
    own_square = jnp.sum(widened * widened, axis=0)
    rounded = lax.dynamic_slice_in_dim(rounded_all, mine, rows_here, 0)
    inner = lax.psum(gram(rounded, rounded_all).astype(jnp.bfloat16), "feat")
    product = jnp.dot(inner, rounded_all, preferred_element_type=jnp.float32)
    product = product - rounded.astype(jnp.float32) * own_square
    return finish(z_anchor, z_other, mean, variance, total, product)


def finish(z_anchor, z_other, mean, variance, total, product):
    coef = 2.0 * total / (25.0 * (total - 1)) / (total - 1)
    anchor = z_anchor.astype(jnp.float32)
    centered = anchor - mean
    deviation = jnp.sqrt(variance + 0.0001)
    hinge = jnp.where(deviation < 1.0, centered / deviation, 0.0)
    factor = total / (4.0 * (total - 1))
    return anchor - z_other.astype(jnp.float32) - factor * hinge + coef * product


def solution(mesh):
    placed = (P("dp", "feat"), P("dp", "feat"))
    in_line = mesh.shape["dp"] == 4 and mesh.shape["feat"] == 8
    return jax.shard_map(
        by_line if in_line else by_gather,
        mesh=mesh, in_specs=placed, out_specs=P("dp", "feat"), check_vma=False,
    )
```

```python
import functools
import math

import jax
import jax.numpy as jnp
from jax import lax
from jax.experimental import pallas as pl
from jax.experimental.pallas import tpu as pltpu
from jax.sharding import PartitionSpec as P

NORM = 128


def kernel_call(body, outs, smem=0, scratch=4, temps=(), sems=0, out=pltpu.VMEM, outside=None):
    def call(*args):
        space = [pltpu.SMEM] * smem + [pltpu.VMEM] * (len(args) - smem)
        if outside is not None:
            space[outside] = pl.ANY
        return pl.pallas_call(
            body,
            out_shape=[jax.ShapeDtypeStruct(s, t) for s, t in outs],
            in_specs=[pl.BlockSpec(memory_space=m) for m in space],
            out_specs=[pl.BlockSpec(memory_space=out) for _ in outs],
            scratch_shapes=[pltpu.VMEM(s, t) for s, t in temps]
            + ([pltpu.SemaphoreType.DMA((sems,))] if sems else []),
            compiler_params=pltpu.CompilerParams(vmem_limit_bytes=scratch * 1024 * 1024),
            cost_estimate=pl.CostEstimate(flops=0, bytes_accessed=0, transcendentals=0),
        )(*args)

    return call


def gram(left, right):
    return lax.dot_general(
        left, right, (((1,), (1,)), ((), ())), preferred_element_type=jnp.float32
    )


def dot_t(left, right):
    return lax.dot_general(
        left, right, (((0,), (0,)), ((), ())), preferred_element_type=jnp.float32
    )


def dot(left, right):
    return jnp.dot(left, right, preferred_element_type=jnp.float32)


def centered_into(out, block, mean, square):
    out[...] = (block[...].astype(jnp.float32) - mean).astype(jnp.bfloat16)
    wide = out[...].astype(jnp.float32)
    square[...] = jnp.sum(wide * wide, axis=0, keepdims=True)


def pieces_in(source, landed, sem):
    rows = landed.shape[0] // 4
    return [
        pltpu.make_async_copy(
            source.at[k * rows:(k + 1) * rows], landed.at[k * rows:(k + 1) * rows], sem.at[k]
        )
        for k in range(4)
    ]


def centered_pieces(out, copies, landed, mean, square):
    rows, total = landed.shape[0] // 4, 0.0
    for k, copy in enumerate(copies):
        copy.wait()
        here = slice(k * rows, (k + 1) * rows)
        block = (landed[here, :].astype(jnp.float32) - mean).astype(jnp.bfloat16)
        out[here, :] = block
        wide = block.astype(jnp.float32)
        total = total + jnp.sum(wide * wide, axis=0, keepdims=True)
    square[...] = total


def high_low(n, like):
    high = n.astype(jnp.bfloat16).astype(jnp.float32)
    lane = lax.broadcasted_iota(jnp.int32, like, 1)
    return jnp.where(lane == 0, high, jnp.where(lane == 1, n - high, 0.0))


def turn_into(turned, order, block):
    eighth = block.shape[0] // 8
    for k in range(8):
        start = pl.multiple_of(order[k] * eighth, eighth)
        turned[k * eighth:(k + 1) * eighth, :] = block[pl.ds(start, eighth), :]


def own_kernel(order, z, mean, own, turned, square, kept, sent):
    rows = z.shape[0]
    eighth, half = rows // 8, rows // 2
    centered_into(own, z, mean[...], square)
    turn_into(turned, order, own)
    inner = gram(turned[...], own[...])
    wide = turned[...].astype(jnp.float32)
    norm = jnp.sum(wide * wide, axis=1, keepdims=True)
    column = lax.broadcasted_iota(jnp.int32, (eighth, rows), 1)
    row = lax.broadcasted_iota(jnp.int32, (eighth, rows), 0)
    for k in range(8):
        here = slice(k * eighth, (k + 1) * eighth)
        off = jnp.where(column == row + order[k] * eighth, 0.0, inner[here])
        if k < 4:
            kept[here, :rows] = off
        else:
            sent[k * eighth - half:(k + 1) * eighth - half, :rows] = off.astype(jnp.bfloat16)
    lane = lax.broadcasted_iota(jnp.int32, (half, NORM), 1)
    kept[:, rows:] = jnp.where(lane == 0, norm[:half], 0.0)
    sent[:, rows:] = high_low(norm[half:], (half, NORM)).astype(jnp.bfloat16)


def split_sum(inner, kept, sent, here):
    half = kept.shape[0]
    kept[:, here] = inner[:half]
    sent[:, here] = inner[half:].astype(jnp.bfloat16)


def first_kernel(
    order, middle, turned, beside_in, opposite_in, mean,
    beside, beside_square, opposite, opposite_square, kept, sent, turned_beside, landed, sem,
):
    copies = pieces_in(opposite_in, landed, sem)

    @pl.when(middle[0] == 1)
    def _():
        for copy in copies:
            copy.start()
        centered_into(beside, beside_in, mean[...], beside_square)
        turn_into(turned_beside, order, beside)
        centered_pieces(opposite, copies, landed, mean[...], opposite_square)
        split_sum(gram(turned_beside[...], opposite[...]), kept, sent, slice(None))

    @pl.when(middle[0] == 0)
    def _():
        centered_into(beside, beside_in, mean[...], beside_square)
        split_sum(gram(turned[...], beside[...]), kept, sent, slice(None))


def early_kernel(middle, turned, beside, opposite, kept, sent):
    rows = beside.shape[0]

    @pl.when(middle[0] == 1)
    def _():
        split_sum(gram(turned[...], opposite[...]), kept, sent, slice(0, rows))
        split_sum(gram(turned[...], beside[...]), kept, sent, slice(rows, 2 * rows))


def late_kernel(
    middle, turned, sent_early, end_in, mean, end, square, kept, sent, landed, sem
):
    rows = end.shape[0]

    @pl.when(middle[0] == 1)
    def _():
        sent[...] = sent_early[...]

    @pl.when(middle[0] == 0)
    def _():
        copies = pieces_in(end_in, landed, sem)
        for copy in copies:
            copy.start()
        centered_pieces(end, copies, landed, mean[...], square)
        split_sum(gram(turned[...], end[...]), kept, sent, slice(0, rows))
        sent[:, rows:] = jnp.zeros_like(sent[:, rows:])


def stats_kernel(z, out):
    rows = z.shape[0]
    base = z[:16, :].astype(jnp.float32)[:1]
    apart = z[...].astype(jnp.float32) - base
    total = jnp.sum(apart, axis=0, keepdims=True)
    away = total / rows
    out[:1, :] = base + away
    out[1:, :] = jnp.sum(apart * apart, axis=0, keepdims=True) - total * away


def with_norm(x, last):
    if not last:
        return x
    tail = x[:, last:]
    split = high_low(jnp.sum(tail, axis=1, keepdims=True), tail.shape)
    return jnp.concatenate([x[:, :last], split], axis=1)


def add_kernel(last, kept, got, mine, *out):
    total = with_norm(kept[...] + got[...].astype(jnp.float32), last)
    quarter = mine.shape[0]
    mine[...] = total[:quarter]
    for k, ref in enumerate(out, 1):
        ref[...] = total[k * quarter:(k + 1) * quarter].astype(jnp.bfloat16)


def add_either_kernel(middle, kept_early, kept, got, mine, *out):
    quarter, rows = mine.shape[0], kept.shape[1]

    def put(total, here):
        mine[:, here] = total[:quarter]
        for k, ref in enumerate(out, 1):
            ref[:, here] = total[k * quarter:(k + 1) * quarter].astype(jnp.bfloat16)

    @pl.when(middle[0] == 1)
    def _():
        put(kept_early[...] + got[...].astype(jnp.float32), slice(None))

    @pl.when(middle[0] == 0)
    def _():
        put(kept[...] + got[:, :rows].astype(jnp.float32), slice(0, rows))
        put(jnp.zeros((4 * quarter, rows), jnp.float32), slice(rows, 2 * rows))


def total_kernel(last, mine, a, b, c, out):
    total = mine[...] + a[...].astype(jnp.float32)
    total = total + b[...].astype(jnp.float32) + c[...].astype(jnp.float32)
    out[...] = with_norm(total, last).astype(jnp.bfloat16)


def total_either_kernel(middle, first, mine, a, b, c, out):
    rows = first.shape[1]

    def put(here):
        total = mine[:, here] + a[:, here].astype(jnp.float32)
        total = total + b[:, here].astype(jnp.float32) + c[:, here].astype(jnp.float32)
        out[:, here] = total.astype(jnp.bfloat16)

    put(slice(0, rows))
    pl.when(middle[0] == 1)(lambda: put(slice(rows, 2 * rows)))

    @pl.when(middle[0] == 0)
    def _():
        out[:, rows:] = first[...]


def place_into(out, order, near, far):
    eighth = out.shape[0] // 8
    for k in range(4):
        here = slice(k * eighth, (k + 1) * eighth)
        out[pl.ds(pl.multiple_of(order[k] * eighth, eighth), eighth), :] = near[here, :]
        out[pl.ds(pl.multiple_of(order[4 + k] * eighth, eighth), eighth), :] = far[here, :]


def push_kernel(
    order, middle, near, far, beside, opposite, beside_square, opposite_square, out, over, inner
):
    width = beside.shape[1]

    @pl.when(middle[0] == 1)
    def _():
        place_into(inner, order, near, far)
        for k in range(2):
            here = slice(k * width // 2, (k + 1) * width // 2)
            outward = dot(inner[...], opposite[:, here])
            outward = outward - beside[:, here].astype(jnp.float32) * opposite_square[:, here]
            out[:, here] = outward.astype(jnp.bfloat16)
            across = dot_t(inner[...], beside[:, here])
            across = across - opposite[:, here].astype(jnp.float32) * beside_square[:, here]
            over[:, here] = across.astype(jnp.bfloat16)


def coefficient(total):
    return 2.0 * total / (25.0 * (total - 1)) / (total - 1)


def held_kernel(
    total, order, middle, near, far, own, z, other,
    own_square, beside_square, swapped_square, end_square, mean, spread, held, with_own,
):
    rows, width = own.shape
    place_into(with_own, order, near, far)
    norm = jnp.sum(with_own[:, rows:].astype(jnp.float32), axis=1, keepdims=True)
    for k in range(4):
        here = slice(k * width // 4, (k + 1) * width // 4)
        anchor = z[:, here].astype(jnp.float32)
        deviation = jnp.sqrt(spread[:, here] / (total - 1) + 0.0001)
        centered = anchor - mean[:, here]
        hinge = jnp.where(deviation < 1.0, centered / deviation, 0.0)
        plain = anchor - other[:, here].astype(jnp.float32) - total / (4.0 * (total - 1)) * hinge
        opposite = jnp.where(middle[0] == 1, swapped_square[:, here], end_square[:, here])
        square = own_square[:, here] + beside_square[:, here] + opposite
        product = dot(with_own[:, :rows], own[:, here])
        product = product + own[:, here].astype(jnp.float32) * (norm - square)
        held[:, here] = plain + coefficient(total) * product


def last_kernel(
    total, order, middle, near, far, beside, swapped, end, held, out, over, result, second, made, sem
):
    rows, width = beside.shape
    place_into(second, order, near, far)

    def put(opposite, arrived):
        for k in range(4):
            here = slice(k * width // 4, (k + 1) * width // 4)
            product = dot(second[:, rows:], beside[:, here])
            product = product + dot(second[:, :rows], opposite[:, here])
            product = product + arrived[:, here].astype(jnp.float32)
            made[:, here] = held[:, here] + coefficient(total) * product
            to_result(k).start()

    def to_result(k):
        here = slice(k * width // 4, (k + 1) * width // 4)
        return pltpu.make_async_copy(made.at[:, here], result.at[:, here], sem.at[k])

    pl.when(middle[0] == 1)(lambda: put(swapped, over))
    pl.when(middle[0] == 0)(lambda: put(end, out))
    for k in range(4):
        to_result(k).wait()


def to_partner(x, step):
    return lax.ppermute(x, "feat", [(i, i ^ step) for i in range(8)])


def halve(kept, sent, last=0):
    half, n = kept.shape
    part = (half // 4, n)
    return kernel_call(
        functools.partial(add_kernel, last), [(part, jnp.float32)] + [(part, jnp.bfloat16)] * 3
    )(kept, to_partner(sent, 1))


def scatter(mine, *out, last=0):
    got = [to_partner(x, 2 * k) for k, x in enumerate(out, 1)]
    return kernel_call(functools.partial(total_kernel, last), [(mine.shape, jnp.bfloat16)])(
        mine, *got
    )[0]


def pile_kernel(*refs):
    *pieces, out = refs
    rows = pieces[0].shape[0]
    for k, piece in enumerate(pieces):
        out[k * rows:(k + 1) * rows, :] = piece[...]


def gather_chips(x):
    pile = [((4 * x.shape[0], x.shape[1]), x.dtype)]
    return kernel_call(pile_kernel, pile)(x, *(to_partner(x, 2 * k) for k in (1, 2, 3)))[0]


def after(x, *others):
    return lax.optimization_barrier((x, *others))[0]


def by_line(z_anchor, z_other):
    rows, width = z_anchor.shape
    total = rows * 4
    plane = lax.axis_index("dp")
    middle = ((plane == 1) | (plane == 2)).astype(jnp.int32).reshape(1)
    order = lax.axis_index("feat") ^ jnp.array([0, 2, 4, 6, 1, 3, 5, 7], jnp.int32)
    across, outward = [(1, 2), (2, 1)], [(1, 0), (2, 3)]
    half = rows // 2
    flat, block = ((1, width), jnp.float32), ((rows, width), jnp.bfloat16)

    stats = kernel_call(stats_kernel, [((2, width), jnp.float32)], scratch=12)(z_anchor)[0]
    all_stats = [stats] + [
        lax.ppermute(stats, "dp", [(i, (i + k) % 4) for i in range(4)]) for k in (1, 2, 3)
    ]
    ahead = after(z_anchor, stats)
    beside_in = lax.ppermute(ahead, "dp", [(i, i ^ 1) for i in range(4)])
    swapped = lax.ppermute(ahead, "dp", across)
    mean = (all_stats[0][:1] + all_stats[1][:1] + all_stats[2][:1] + all_stats[3][:1]) / 4
    spread = 0.0
    for one in all_stats:
        shift = one[:1] - mean
        spread = spread + (one[1:] + rows * shift * shift)

    def summands(n):
        return [((half, n), jnp.float32), ((half, n), jnp.bfloat16)]

    own, turned, own_square, kept, sent = kernel_call(
        own_kernel, [block, block, flat, *summands(rows + NORM)], smem=1, scratch=12
    )(order, z_anchor, mean)
    near_own = scatter(*halve(kept, sent, rows), last=rows)
    near_own = jnp.concatenate([near_own] + [to_partner(near_own, 2 * k) for k in (1, 2, 3)])
    end = lax.ppermute(after(z_anchor, beside_in, swapped, near_own), "dp", [(0, 3), (3, 0)])

    beside, beside_square, swapped, swapped_square, kept, sent = kernel_call(
        first_kernel, [block, flat, block, flat, *summands(rows)],
        smem=2, scratch=12, temps=[block, block], sems=4, outside=4,
    )(order, middle, after(turned, near_own), beside_in, swapped, mean)
    first = scatter(*halve(kept, sent))
    kept_early, sent_early = kernel_call(
        early_kernel, summands(2 * rows), smem=1, scratch=12
    )(middle, after(turned, first), beside, swapped)
    far_own = to_partner(near_own, 1)
    near = after(gather_chips(first), sent_early)
    ready = kernel_call(
        push_kernel, [block, block], smem=2, scratch=12, temps=[((rows, rows), jnp.bfloat16)]
    )(order, middle, near, after(to_partner(near, 1), far_own), beside, swapped, beside_square, swapped_square)
    out, over = ready
    pushed = [
        lax.ppermute(out, "dp", outward), lax.ppermute(after(over, end), "dp", across)
    ]

    end, end_square, kept, sent = kernel_call(
        late_kernel, [block, flat, summands(rows)[0], summands(2 * rows)[1]],
        smem=1, scratch=12, temps=[block], sems=4, outside=3,
    )(middle, after(turned, *ready), sent_early, end, mean)
    eighth = (rows // 8, 2 * rows)
    halved = kernel_call(
        add_either_kernel, [(eighth, jnp.float32)] + [(eighth, jnp.bfloat16)] * 3, smem=1
    )(middle, kept_early, kept, to_partner(sent, 1))
    result = ((rows, width), jnp.float32)
    held = kernel_call(
        functools.partial(held_kernel, total), [result],
        smem=2, scratch=12, temps=[((rows, rows + NORM), jnp.bfloat16)],
    )(
        order, middle, near_own, far_own, own, z_anchor, z_other,
        own_square, beside_square, swapped_square, after(end_square, halved[0]), mean, spread,
    )[0]
    got = [to_partner(x, 2 * k) for k, x in enumerate(halved[1:], 1)]
    second = kernel_call(total_either_kernel, [(eighth, jnp.bfloat16)], smem=1)(
        middle, first, halved[0], *got
    )[0]
    near = after(gather_chips(after(second, held)), pushed[0])
    return kernel_call(
        functools.partial(last_kernel, total), [result],
        smem=2, scratch=12, temps=[((rows, 2 * rows), jnp.bfloat16), result], sems=4, out=pl.ANY,
    )(
        order, middle, near, to_partner(near, 1), beside, swapped, end, held, *pushed
    )[0]


def by_gather(z_anchor, z_other):
    rows_here, width = z_anchor.shape
    groups = lax.axis_size("dp")
    total = rows_here * groups
    mine = lax.axis_index("dp") * rows_here
    column = lax.all_gather(z_anchor, "dp", axis=0, tiled=True).astype(jnp.float32)
    mean = jnp.sum(column, axis=0) / total
    centered_all = column - mean
    variance = jnp.sum(centered_all * centered_all, axis=0) / (total - 1)
    rounded_all = centered_all.astype(jnp.bfloat16)
    widened = rounded_all.astype(jnp.float32)
    own_square = jnp.sum(widened * widened, axis=0)
    rounded = lax.dynamic_slice_in_dim(rounded_all, mine, rows_here, 0)
    inner = lax.psum(gram(rounded, rounded_all).astype(jnp.bfloat16), "feat")
    product = jnp.dot(inner, rounded_all, preferred_element_type=jnp.float32)
    product = product - rounded.astype(jnp.float32) * own_square
    return finish(z_anchor, z_other, mean, variance, total, product)


def finish(z_anchor, z_other, mean, variance, total, product):
    coef = 2.0 * total / (25.0 * (total - 1)) / (total - 1)
    anchor = z_anchor.astype(jnp.float32)
    centered = anchor - mean
    deviation = jnp.sqrt(variance + 0.0001)
    hinge = jnp.where(deviation < 1.0, centered / deviation, 0.0)
    factor = total / (4.0 * (total - 1))
    return anchor - z_other.astype(jnp.float32) - factor * hinge + coef * product


def solution(mesh):
    placed = (P("dp", "feat"), P("dp", "feat"))
    in_line = mesh.shape["dp"] == 4 and mesh.shape["feat"] == 8
    return jax.shard_map(
        by_line if in_line else by_gather,
        mesh=mesh, in_specs=placed, out_specs=P("dp", "feat"), check_vma=False,
    )
```

```python
import functools
import math

import jax
import jax.numpy as jnp
from jax import lax
from jax.experimental import pallas as pl
from jax.experimental.pallas import tpu as pltpu
from jax.sharding import PartitionSpec as P

NORM = 128


def kernel_call(body, outs, smem=0, scratch=4, temps=(), sems=0):
    def call(*args):
        space = [pltpu.SMEM] * smem + [pltpu.VMEM] * (len(args) - smem)
        return pl.pallas_call(
            body,
            out_shape=[jax.ShapeDtypeStruct(s, t) for s, t in outs],
            in_specs=[pl.BlockSpec(memory_space=m) for m in space],
            out_specs=[pl.BlockSpec(memory_space=pl.ANY if sems else pltpu.VMEM) for _ in outs],
            scratch_shapes=[pltpu.VMEM(s, t) for s, t in temps]
            + ([pltpu.SemaphoreType.DMA((sems,))] if sems else []),
            compiler_params=pltpu.CompilerParams(vmem_limit_bytes=scratch * 1024 * 1024),
            cost_estimate=pl.CostEstimate(flops=0, bytes_accessed=0, transcendentals=0),
        )(*args)

    return call


def gram(left, right):
    return lax.dot_general(
        left, right, (((1,), (1,)), ((), ())), preferred_element_type=jnp.float32
    )


def dot_t(left, right):
    return lax.dot_general(
        left, right, (((0,), (0,)), ((), ())), preferred_element_type=jnp.float32
    )


def dot(left, right):
    return jnp.dot(left, right, preferred_element_type=jnp.float32)


def centered_into(out, block, mean, square):
    out[...] = (block[...].astype(jnp.float32) - mean).astype(jnp.bfloat16)
    wide = out[...].astype(jnp.float32)
    square[...] = jnp.sum(wide * wide, axis=0, keepdims=True)


def high_low(n, like):
    high = n.astype(jnp.bfloat16).astype(jnp.float32)
    lane = lax.broadcasted_iota(jnp.int32, like, 1)
    return jnp.where(lane == 0, high, jnp.where(lane == 1, n - high, 0.0))


def turn_into(turned, order, block):
    eighth = block.shape[0] // 8
    for k in range(8):
        start = pl.multiple_of(order[k] * eighth, eighth)
        turned[k * eighth:(k + 1) * eighth, :] = block[pl.ds(start, eighth), :]


def own_kernel(order, z, mean, own, turned, square, kept, sent):
    rows = z.shape[0]
    eighth, half = rows // 8, rows // 2
    centered_into(own, z, mean[...], square)
    turn_into(turned, order, own)
    inner = gram(turned[...], own[...])
    wide = turned[...].astype(jnp.float32)
    norm = jnp.sum(wide * wide, axis=1, keepdims=True)
    column = lax.broadcasted_iota(jnp.int32, (eighth, rows), 1)
    row = lax.broadcasted_iota(jnp.int32, (eighth, rows), 0)
    for k in range(8):
        here = slice(k * eighth, (k + 1) * eighth)
        off = jnp.where(column == row + order[k] * eighth, 0.0, inner[here])
        if k < 4:
            kept[here, :rows] = off
        else:
            sent[k * eighth - half:(k + 1) * eighth - half, :rows] = off.astype(jnp.bfloat16)
    lane = lax.broadcasted_iota(jnp.int32, (half, NORM), 1)
    kept[:, rows:] = jnp.where(lane == 0, norm[:half], 0.0)
    sent[:, rows:] = high_low(norm[half:], (half, NORM)).astype(jnp.bfloat16)


def split_sum(inner, kept, sent, here):
    half = kept.shape[0]
    kept[:, here] = inner[:half]
    sent[:, here] = inner[half:].astype(jnp.bfloat16)


def first_kernel(
    order, middle, turned, beside_in, opposite_in, mean,
    beside, beside_square, opposite, opposite_square, kept, sent, turned_beside,
):
    centered_into(beside, beside_in, mean[...], beside_square)

    @pl.when(middle[0] == 1)
    def _():
        centered_into(opposite, opposite_in, mean[...], opposite_square)
        turn_into(turned_beside, order, beside)
        split_sum(gram(turned_beside[...], opposite[...]), kept, sent, slice(None))

    @pl.when(middle[0] == 0)
    def _():
        split_sum(gram(turned[...], beside[...]), kept, sent, slice(None))


def early_kernel(middle, turned, beside, opposite, kept, sent):
    rows = beside.shape[0]

    @pl.when(middle[0] == 1)
    def _():
        split_sum(gram(turned[...], opposite[...]), kept, sent, slice(0, rows))
        split_sum(gram(turned[...], beside[...]), kept, sent, slice(rows, 2 * rows))


def late_kernel(middle, turned, sent_early, end_in, mean, end, square, kept, sent):
    rows = end.shape[0]

    @pl.when(middle[0] == 1)
    def _():
        sent[...] = sent_early[...]

    @pl.when(middle[0] == 0)
    def _():
        centered_into(end, end_in, mean[...], square)
        split_sum(gram(turned[...], end[...]), kept, sent, slice(0, rows))
        sent[:, rows:] = jnp.zeros_like(sent[:, rows:])


def stats_kernel(z, out):
    rows = z.shape[0]
    base = z[:16, :].astype(jnp.float32)[:1]
    apart = z[...].astype(jnp.float32) - base
    total = jnp.sum(apart, axis=0, keepdims=True)
    away = total / rows
    out[:1, :] = base + away
    out[1:, :] = jnp.sum(apart * apart, axis=0, keepdims=True) - total * away


def with_norm(x, last):
    if not last:
        return x
    tail = x[:, last:]
    split = high_low(jnp.sum(tail, axis=1, keepdims=True), tail.shape)
    return jnp.concatenate([x[:, :last], split], axis=1)


def add_kernel(last, kept, got, mine, *out):
    total = with_norm(kept[...] + got[...].astype(jnp.float32), last)
    quarter = mine.shape[0]
    mine[...] = total[:quarter]
    for k, ref in enumerate(out, 1):
        ref[...] = total[k * quarter:(k + 1) * quarter].astype(jnp.bfloat16)


def add_either_kernel(middle, kept_early, kept, got, mine, *out):
    quarter, rows = mine.shape[0], kept.shape[1]

    def put(total, here):
        mine[:, here] = total[:quarter]
        for k, ref in enumerate(out, 1):
            ref[:, here] = total[k * quarter:(k + 1) * quarter].astype(jnp.bfloat16)

    @pl.when(middle[0] == 1)
    def _():
        put(kept_early[...] + got[...].astype(jnp.float32), slice(None))

    @pl.when(middle[0] == 0)
    def _():
        put(kept[...] + got[:, :rows].astype(jnp.float32), slice(0, rows))
        put(jnp.zeros((4 * quarter, rows), jnp.float32), slice(rows, 2 * rows))


def total_kernel(last, mine, a, b, c, out):
    total = mine[...] + a[...].astype(jnp.float32)
    total = total + b[...].astype(jnp.float32) + c[...].astype(jnp.float32)
    out[...] = with_norm(total, last).astype(jnp.bfloat16)


def total_either_kernel(middle, first, mine, a, b, c, out):
    rows = first.shape[1]

    def put(here):
        total = mine[:, here] + a[:, here].astype(jnp.float32)
        total = total + b[:, here].astype(jnp.float32) + c[:, here].astype(jnp.float32)
        out[:, here] = total.astype(jnp.bfloat16)

    put(slice(0, rows))
    pl.when(middle[0] == 1)(lambda: put(slice(rows, 2 * rows)))

    @pl.when(middle[0] == 0)
    def _():
        out[:, rows:] = first[...]


def place_into(out, order, near, far):
    eighth = out.shape[0] // 8
    for k in range(4):
        here = slice(k * eighth, (k + 1) * eighth)
        out[pl.ds(pl.multiple_of(order[k] * eighth, eighth), eighth), :] = near[here, :]
        out[pl.ds(pl.multiple_of(order[4 + k] * eighth, eighth), eighth), :] = far[here, :]


def push_kernel(
    order, middle, near, far, beside, opposite, beside_square, opposite_square, out, over, inner
):
    width = beside.shape[1]

    @pl.when(middle[0] == 1)
    def _():
        place_into(inner, order, near, far)
        for k in range(2):
            here = slice(k * width // 2, (k + 1) * width // 2)
            outward = dot(inner[...], opposite[:, here])
            outward = outward - beside[:, here].astype(jnp.float32) * opposite_square[:, here]
            out[:, here] = outward.astype(jnp.bfloat16)
            across = dot_t(inner[...], beside[:, here])
            across = across - opposite[:, here].astype(jnp.float32) * beside_square[:, here]
            over[:, here] = across.astype(jnp.bfloat16)


def coefficient(total):
    return 2.0 * total / (25.0 * (total - 1)) / (total - 1)


def held_kernel(
    total, order, middle, near, far, own, z, other,
    own_square, beside_square, swapped_square, end_square, mean, spread, held, with_own,
):
    rows, width = own.shape
    place_into(with_own, order, near, far)
    norm = jnp.sum(with_own[:, rows:].astype(jnp.float32), axis=1, keepdims=True)
    for k in range(4):
        here = slice(k * width // 4, (k + 1) * width // 4)
        anchor = z[:, here].astype(jnp.float32)
        deviation = jnp.sqrt(spread[:, here] / (total - 1) + 0.0001)
        centered = anchor - mean[:, here]
        hinge = jnp.where(deviation < 1.0, centered / deviation, 0.0)
        plain = anchor - other[:, here].astype(jnp.float32) - total / (4.0 * (total - 1)) * hinge
        opposite = jnp.where(middle[0] == 1, swapped_square[:, here], end_square[:, here])
        square = own_square[:, here] + beside_square[:, here] + opposite
        product = dot(with_own[:, :rows], own[:, here])
        product = product + own[:, here].astype(jnp.float32) * (norm - square)
        held[:, here] = plain + coefficient(total) * product


def last_kernel(
    total, order, middle, near, far, beside, swapped, end, held, out, over, result, second, made, sem
):
    rows, width = beside.shape
    place_into(second, order, near, far)

    def put(opposite, arrived):
        for k in range(4):
            here = slice(k * width // 4, (k + 1) * width // 4)
            product = dot(second[:, rows:], beside[:, here])
            product = product + dot(second[:, :rows], opposite[:, here])
            product = product + arrived[:, here].astype(jnp.float32)
            made[:, here] = held[:, here] + coefficient(total) * product
            to_result(k).start()

    def to_result(k):
        here = slice(k * width // 4, (k + 1) * width // 4)
        return pltpu.make_async_copy(made.at[:, here], result.at[:, here], sem.at[k])

    pl.when(middle[0] == 1)(lambda: put(swapped, over))
    pl.when(middle[0] == 0)(lambda: put(end, out))
    for k in range(4):
        to_result(k).wait()


def to_partner(x, step):
    return lax.ppermute(x, "feat", [(i, i ^ step) for i in range(8)])


def halve(kept, sent, last=0):
    half, n = kept.shape
    part = (half // 4, n)
    return kernel_call(
        functools.partial(add_kernel, last), [(part, jnp.float32)] + [(part, jnp.bfloat16)] * 3
    )(kept, to_partner(sent, 1))


def scatter(mine, *out, last=0):
    got = [to_partner(x, 2 * k) for k, x in enumerate(out, 1)]
    return kernel_call(functools.partial(total_kernel, last), [(mine.shape, jnp.bfloat16)])(
        mine, *got
    )[0]


def pile_kernel(*refs):
    *pieces, out = refs
    rows = pieces[0].shape[0]
    for k, piece in enumerate(pieces):
        out[k * rows:(k + 1) * rows, :] = piece[...]


def gather_chips(x):
    pile = [((4 * x.shape[0], x.shape[1]), x.dtype)]
    return kernel_call(pile_kernel, pile)(x, *(to_partner(x, 2 * k) for k in (1, 2, 3)))[0]


def after(x, *others):
    return lax.optimization_barrier((x, *others))[0]


def by_line(z_anchor, z_other):
    rows, width = z_anchor.shape
    total = rows * 4
    plane = lax.axis_index("dp")
    middle = ((plane == 1) | (plane == 2)).astype(jnp.int32).reshape(1)
    order = lax.axis_index("feat") ^ jnp.array([0, 2, 4, 6, 1, 3, 5, 7], jnp.int32)
    across, outward = [(1, 2), (2, 1)], [(1, 0), (2, 3)]
    half = rows // 2
    flat, block = ((1, width), jnp.float32), ((rows, width), jnp.bfloat16)

    stats = kernel_call(stats_kernel, [((2, width), jnp.float32)], scratch=12)(z_anchor)[0]
    all_stats = [stats] + [
        lax.ppermute(stats, "dp", [(i, (i + k) % 4) for i in range(4)]) for k in (1, 2, 3)
    ]
    ahead = after(z_anchor, stats)
    beside_in = lax.ppermute(ahead, "dp", [(i, i ^ 1) for i in range(4)])
    swapped = lax.ppermute(ahead, "dp", across)
    mean = (all_stats[0][:1] + all_stats[1][:1] + all_stats[2][:1] + all_stats[3][:1]) / 4
    spread = 0.0
    for one in all_stats:
        shift = one[:1] - mean
        spread = spread + (one[1:] + rows * shift * shift)

    def summands(n):
        return [((half, n), jnp.float32), ((half, n), jnp.bfloat16)]

    own, turned, own_square, kept, sent = kernel_call(
        own_kernel, [block, block, flat, *summands(rows + NORM)], smem=1, scratch=12
    )(order, z_anchor, mean)
    near_own = scatter(*halve(kept, sent, rows), last=rows)
    near_own = jnp.concatenate([near_own] + [to_partner(near_own, 2 * k) for k in (1, 2, 3)])
    end = lax.ppermute(after(z_anchor, beside_in, swapped, near_own), "dp", [(0, 3), (3, 0)])

    beside, beside_square, swapped, swapped_square, kept, sent = kernel_call(
        first_kernel, [block, flat, block, flat, *summands(rows)],
        smem=2, scratch=12, temps=[block],
    )(order, middle, after(turned, near_own), beside_in, swapped, mean)
    first = scatter(*halve(kept, sent))
    kept_early, sent_early = kernel_call(
        early_kernel, summands(2 * rows), smem=1, scratch=12
    )(middle, after(turned, first), beside, swapped)
    near = after(gather_chips(first), sent_early)
    ready = kernel_call(
        push_kernel, [block, block], smem=2, scratch=12, temps=[((rows, rows), jnp.bfloat16)]
    )(order, middle, near, to_partner(near, 1), beside, swapped, beside_square, swapped_square)
    out, over = ready
    pushed = [
        lax.ppermute(out, "dp", outward), lax.ppermute(after(over, end), "dp", across)
    ]

    end, end_square, kept, sent = kernel_call(
        late_kernel, [block, flat, summands(rows)[0], summands(2 * rows)[1]], smem=1, scratch=12
    )(middle, after(turned, *ready), sent_early, end, mean)
    eighth = (rows // 8, 2 * rows)
    halved = kernel_call(
        add_either_kernel, [(eighth, jnp.float32)] + [(eighth, jnp.bfloat16)] * 3, smem=1
    )(middle, kept_early, kept, to_partner(sent, 1))
    result = ((rows, width), jnp.float32)
    held = kernel_call(
        functools.partial(held_kernel, total), [result],
        smem=2, scratch=12, temps=[((rows, rows + NORM), jnp.bfloat16)],
    )(
        order, middle, near_own, to_partner(near_own, 1), own, z_anchor, z_other,
        own_square, beside_square, swapped_square, after(end_square, halved[0]), mean, spread,
    )[0]
    got = [to_partner(x, 2 * k) for k, x in enumerate(halved[1:], 1)]
    second = kernel_call(total_either_kernel, [(eighth, jnp.bfloat16)], smem=1)(
        middle, first, halved[0], *got
    )[0]
    near = after(gather_chips(after(second, held)), pushed[1])
    return kernel_call(
        functools.partial(last_kernel, total), [result],
        smem=2, scratch=12, temps=[((rows, 2 * rows), jnp.bfloat16), result], sems=4,
    )(
        order, middle, near, to_partner(near, 1), beside, swapped, end, held, *pushed
    )[0]


def by_gather(z_anchor, z_other):
    rows_here, width = z_anchor.shape
    groups = lax.axis_size("dp")
    total = rows_here * groups
    mine = lax.axis_index("dp") * rows_here
    column = lax.all_gather(z_anchor, "dp", axis=0, tiled=True).astype(jnp.float32)
    mean = jnp.sum(column, axis=0) / total
    centered_all = column - mean
    variance = jnp.sum(centered_all * centered_all, axis=0) / (total - 1)
    rounded_all = centered_all.astype(jnp.bfloat16)
    widened = rounded_all.astype(jnp.float32)
    own_square = jnp.sum(widened * widened, axis=0)
    rounded = lax.dynamic_slice_in_dim(rounded_all, mine, rows_here, 0)
    inner = lax.psum(gram(rounded, rounded_all).astype(jnp.bfloat16), "feat")
    product = jnp.dot(inner, rounded_all, preferred_element_type=jnp.float32)
    product = product - rounded.astype(jnp.float32) * own_square
    return finish(z_anchor, z_other, mean, variance, total, product)


def finish(z_anchor, z_other, mean, variance, total, product):
    coef = 2.0 * total / (25.0 * (total - 1)) / (total - 1)
    anchor = z_anchor.astype(jnp.float32)
    centered = anchor - mean
    deviation = jnp.sqrt(variance + 0.0001)
    hinge = jnp.where(deviation < 1.0, centered / deviation, 0.0)
    factor = total / (4.0 * (total - 1))
    return anchor - z_other.astype(jnp.float32) - factor * hinge + coef * product


def solution(mesh):
    placed = (P("dp", "feat"), P("dp", "feat"))
    in_line = mesh.shape["dp"] == 4 and mesh.shape["feat"] == 8
    return jax.shard_map(
        by_line if in_line else by_gather,
        mesh=mesh, in_specs=placed, out_specs=P("dp", "feat"), check_vma=False,
    )
```

```python
import functools
import math

import jax
import jax.numpy as jnp
from jax import lax
from jax.experimental import pallas as pl
from jax.experimental.pallas import tpu as pltpu
from jax.sharding import PartitionSpec as P

NORM = 128


def kernel_call(body, outs, smem=0, scratch=4, temps=(), sems=0, out=pltpu.VMEM, outside=None):
    def call(*args):
        space = [pltpu.SMEM] * smem + [pltpu.VMEM] * (len(args) - smem)
        if outside is not None:
            space[outside] = pl.ANY
        return pl.pallas_call(
            body,
            out_shape=[jax.ShapeDtypeStruct(s, t) for s, t in outs],
            in_specs=[pl.BlockSpec(memory_space=m) for m in space],
            out_specs=[pl.BlockSpec(memory_space=out) for _ in outs],
            scratch_shapes=[pltpu.VMEM(s, t) for s, t in temps]
            + ([pltpu.SemaphoreType.DMA((sems,))] if sems else []),
            compiler_params=pltpu.CompilerParams(vmem_limit_bytes=scratch * 1024 * 1024),
            cost_estimate=pl.CostEstimate(flops=0, bytes_accessed=0, transcendentals=0),
        )(*args)

    return call


def gram(left, right):
    return lax.dot_general(
        left, right, (((1,), (1,)), ((), ())), preferred_element_type=jnp.float32
    )


def dot_t(left, right):
    return lax.dot_general(
        left, right, (((0,), (0,)), ((), ())), preferred_element_type=jnp.float32
    )


def dot(left, right):
    return jnp.dot(left, right, preferred_element_type=jnp.float32)


def centered_into(out, block, mean, square):
    out[...] = (block[...].astype(jnp.float32) - mean).astype(jnp.bfloat16)
    wide = out[...].astype(jnp.float32)
    square[...] = jnp.sum(wide * wide, axis=0, keepdims=True)


def pieces_in(source, landed, sem):
    rows = landed.shape[0] // 4
    return [
        pltpu.make_async_copy(
            source.at[k * rows:(k + 1) * rows], landed.at[k * rows:(k + 1) * rows], sem.at[k]
        )
        for k in range(4)
    ]


def centered_pieces(out, copies, landed, mean, square):
    rows, total = landed.shape[0] // 4, 0.0
    for k, copy in enumerate(copies):
        copy.wait()
        here = slice(k * rows, (k + 1) * rows)
        block = (landed[here, :].astype(jnp.float32) - mean).astype(jnp.bfloat16)
        out[here, :] = block
        wide = block.astype(jnp.float32)
        total = total + jnp.sum(wide * wide, axis=0, keepdims=True)
    square[...] = total


def high_low(n, like):
    high = n.astype(jnp.bfloat16).astype(jnp.float32)
    lane = lax.broadcasted_iota(jnp.int32, like, 1)
    return jnp.where(lane == 0, high, jnp.where(lane == 1, n - high, 0.0))


def turn_into(turned, order, block):
    eighth = block.shape[0] // 8
    for k in range(8):
        start = pl.multiple_of(order[k] * eighth, eighth)
        turned[k * eighth:(k + 1) * eighth, :] = block[pl.ds(start, eighth), :]


def own_kernel(order, z, mean, own, turned, square, kept, sent):
    rows = z.shape[0]
    eighth, half = rows // 8, rows // 2
    centered_into(own, z, mean[...], square)
    turn_into(turned, order, own)
    inner = gram(turned[...], own[...])
    wide = turned[...].astype(jnp.float32)
    norm = jnp.sum(wide * wide, axis=1, keepdims=True)
    column = lax.broadcasted_iota(jnp.int32, (eighth, rows), 1)
    row = lax.broadcasted_iota(jnp.int32, (eighth, rows), 0)
    for k in range(8):
        here = slice(k * eighth, (k + 1) * eighth)
        off = jnp.where(column == row + order[k] * eighth, 0.0, inner[here])
        if k < 4:
            kept[here, :rows] = off
        else:
            sent[k * eighth - half:(k + 1) * eighth - half, :rows] = off.astype(jnp.bfloat16)
    lane = lax.broadcasted_iota(jnp.int32, (half, NORM), 1)
    kept[:, rows:] = jnp.where(lane == 0, norm[:half], 0.0)
    sent[:, rows:] = high_low(norm[half:], (half, NORM)).astype(jnp.bfloat16)


def split_sum(inner, kept, sent, here):
    half = kept.shape[0]
    kept[:, here] = inner[:half]
    sent[:, here] = inner[half:].astype(jnp.bfloat16)


def first_kernel(
    order, middle, turned, beside_in, opposite_in, mean,
    beside, beside_square, opposite, opposite_square, kept, sent, turned_beside,
):
    centered_into(beside, beside_in, mean[...], beside_square)

    @pl.when(middle[0] == 1)
    def _():
        centered_into(opposite, opposite_in, mean[...], opposite_square)
        turn_into(turned_beside, order, beside)
        split_sum(gram(turned_beside[...], opposite[...]), kept, sent, slice(None))

    @pl.when(middle[0] == 0)
    def _():
        split_sum(gram(turned[...], beside[...]), kept, sent, slice(None))


def early_kernel(middle, turned, beside, opposite, kept, sent):
    rows = beside.shape[0]

    @pl.when(middle[0] == 1)
    def _():
        split_sum(gram(turned[...], opposite[...]), kept, sent, slice(0, rows))
        split_sum(gram(turned[...], beside[...]), kept, sent, slice(rows, 2 * rows))


def late_kernel(
    middle, turned, sent_early, end_in, mean, end, square, kept, sent, landed, sem
):
    rows = end.shape[0]

    @pl.when(middle[0] == 1)
    def _():
        sent[...] = sent_early[...]

    @pl.when(middle[0] == 0)
    def _():
        copies = pieces_in(end_in, landed, sem)
        for copy in copies:
            copy.start()
        centered_pieces(end, copies, landed, mean[...], square)
        split_sum(gram(turned[...], end[...]), kept, sent, slice(0, rows))
        sent[:, rows:] = jnp.zeros_like(sent[:, rows:])


def stats_kernel(z, out):
    rows = z.shape[0]
    base = z[:16, :].astype(jnp.float32)[:1]
    apart = z[...].astype(jnp.float32) - base
    total = jnp.sum(apart, axis=0, keepdims=True)
    away = total / rows
    out[:1, :] = base + away
    out[1:, :] = jnp.sum(apart * apart, axis=0, keepdims=True) - total * away


def with_norm(x, last):
    if not last:
        return x
    tail = x[:, last:]
    split = high_low(jnp.sum(tail, axis=1, keepdims=True), tail.shape)
    return jnp.concatenate([x[:, :last], split], axis=1)


def add_kernel(last, kept, got, mine, *out):
    total = with_norm(kept[...] + got[...].astype(jnp.float32), last)
    quarter = mine.shape[0]
    mine[...] = total[:quarter]
    for k, ref in enumerate(out, 1):
        ref[...] = total[k * quarter:(k + 1) * quarter].astype(jnp.bfloat16)


def add_either_kernel(middle, kept_early, kept, got, mine, *out):
    quarter, rows = mine.shape[0], kept.shape[1]

    def put(total, here):
        mine[:, here] = total[:quarter]
        for k, ref in enumerate(out, 1):
            ref[:, here] = total[k * quarter:(k + 1) * quarter].astype(jnp.bfloat16)

    @pl.when(middle[0] == 1)
    def _():
        put(kept_early[...] + got[...].astype(jnp.float32), slice(None))

    @pl.when(middle[0] == 0)
    def _():
        put(kept[...] + got[:, :rows].astype(jnp.float32), slice(0, rows))
        put(jnp.zeros((4 * quarter, rows), jnp.float32), slice(rows, 2 * rows))


def total_kernel(last, mine, a, b, c, out):
    total = mine[...] + a[...].astype(jnp.float32)
    total = total + b[...].astype(jnp.float32) + c[...].astype(jnp.float32)
    out[...] = with_norm(total, last).astype(jnp.bfloat16)


def total_either_kernel(middle, first, mine, a, b, c, out):
    rows = first.shape[1]

    def put(here):
        total = mine[:, here] + a[:, here].astype(jnp.float32)
        total = total + b[:, here].astype(jnp.float32) + c[:, here].astype(jnp.float32)
        out[:, here] = total.astype(jnp.bfloat16)

    put(slice(0, rows))
    pl.when(middle[0] == 1)(lambda: put(slice(rows, 2 * rows)))

    @pl.when(middle[0] == 0)
    def _():
        out[:, rows:] = first[...]


def place_into(out, order, near, far):
    eighth = out.shape[0] // 8
    for k in range(4):
        here = slice(k * eighth, (k + 1) * eighth)
        out[pl.ds(pl.multiple_of(order[k] * eighth, eighth), eighth), :] = near[here, :]
        out[pl.ds(pl.multiple_of(order[4 + k] * eighth, eighth), eighth), :] = far[here, :]


def push_kernel(
    order, middle, near, far, beside, opposite, beside_square, opposite_square, out, over, inner
):
    width = beside.shape[1]

    @pl.when(middle[0] == 1)
    def _():
        place_into(inner, order, near, far)
        for k in range(2):
            here = slice(k * width // 2, (k + 1) * width // 2)
            outward = dot(inner[...], opposite[:, here])
            outward = outward - beside[:, here].astype(jnp.float32) * opposite_square[:, here]
            out[:, here] = outward.astype(jnp.bfloat16)
            across = dot_t(inner[...], beside[:, here])
            across = across - opposite[:, here].astype(jnp.float32) * beside_square[:, here]
            over[:, here] = across.astype(jnp.bfloat16)


def coefficient(total):
    return 2.0 * total / (25.0 * (total - 1)) / (total - 1)


def held_kernel(
    total, order, middle, near, far, own, z, other,
    own_square, beside_square, swapped_square, end_square, mean, spread, held, with_own,
):
    rows, width = own.shape
    place_into(with_own, order, near, far)
    norm = jnp.sum(with_own[:, rows:].astype(jnp.float32), axis=1, keepdims=True)
    for k in range(4):
        here = slice(k * width // 4, (k + 1) * width // 4)
        anchor = z[:, here].astype(jnp.float32)
        deviation = jnp.sqrt(spread[:, here] / (total - 1) + 0.0001)
        centered = anchor - mean[:, here]
        hinge = jnp.where(deviation < 1.0, centered / deviation, 0.0)
        plain = anchor - other[:, here].astype(jnp.float32) - total / (4.0 * (total - 1)) * hinge
        opposite = jnp.where(middle[0] == 1, swapped_square[:, here], end_square[:, here])
        square = own_square[:, here] + beside_square[:, here] + opposite
        product = dot(with_own[:, :rows], own[:, here])
        product = product + own[:, here].astype(jnp.float32) * (norm - square)
        held[:, here] = plain + coefficient(total) * product


def last_kernel(
    total, order, middle, near, far, beside, swapped, end, held, out, over, result, second, made, sem
):
    rows, width = beside.shape
    place_into(second, order, near, far)

    def put(opposite, arrived):
        for k in range(4):
            here = slice(k * width // 4, (k + 1) * width // 4)
            product = dot(second[:, rows:], beside[:, here])
            product = product + dot(second[:, :rows], opposite[:, here])
            product = product + arrived[:, here].astype(jnp.float32)
            made[:, here] = held[:, here] + coefficient(total) * product
            to_result(k).start()

    def to_result(k):
        here = slice(k * width // 4, (k + 1) * width // 4)
        return pltpu.make_async_copy(made.at[:, here], result.at[:, here], sem.at[k])

    pl.when(middle[0] == 1)(lambda: put(swapped, over))
    pl.when(middle[0] == 0)(lambda: put(end, out))
    for k in range(4):
        to_result(k).wait()


def to_partner(x, step):
    return lax.ppermute(x, "feat", [(i, i ^ step) for i in range(8)])


def halve(kept, sent, last=0):
    half, n = kept.shape
    part = (half // 4, n)
    return kernel_call(
        functools.partial(add_kernel, last), [(part, jnp.float32)] + [(part, jnp.bfloat16)] * 3
    )(kept, to_partner(sent, 1))


def scatter(mine, *out, last=0):
    got = [to_partner(x, 2 * k) for k, x in enumerate(out, 1)]
    return kernel_call(functools.partial(total_kernel, last), [(mine.shape, jnp.bfloat16)])(
        mine, *got
    )[0]


def pile_kernel(*refs):
    *pieces, out = refs
    rows = pieces[0].shape[0]
    for k, piece in enumerate(pieces):
        out[k * rows:(k + 1) * rows, :] = piece[...]


def gather_chips(x):
    pile = [((4 * x.shape[0], x.shape[1]), x.dtype)]
    return kernel_call(pile_kernel, pile)(x, *(to_partner(x, 2 * k) for k in (1, 2, 3)))[0]


def after(x, *others):
    return lax.optimization_barrier((x, *others))[0]


def by_line(z_anchor, z_other):
    rows, width = z_anchor.shape
    total = rows * 4
    plane = lax.axis_index("dp")
    middle = ((plane == 1) | (plane == 2)).astype(jnp.int32).reshape(1)
    order = lax.axis_index("feat") ^ jnp.array([0, 2, 4, 6, 1, 3, 5, 7], jnp.int32)
    across, outward = [(1, 2), (2, 1)], [(1, 0), (2, 3)]
    half = rows // 2
    flat, block = ((1, width), jnp.float32), ((rows, width), jnp.bfloat16)

    stats = kernel_call(stats_kernel, [((2, width), jnp.float32)], scratch=12)(z_anchor)[0]
    all_stats = [stats] + [
        lax.ppermute(stats, "dp", [(i, (i + k) % 4) for i in range(4)]) for k in (1, 2, 3)
    ]
    ahead = after(z_anchor, stats)
    beside_in = lax.ppermute(ahead, "dp", [(i, i ^ 1) for i in range(4)])
    swapped = lax.ppermute(ahead, "dp", across)
    mean = (all_stats[0][:1] + all_stats[1][:1] + all_stats[2][:1] + all_stats[3][:1]) / 4
    spread = 0.0
    for one in all_stats:
        shift = one[:1] - mean
        spread = spread + (one[1:] + rows * shift * shift)

    def summands(n):
        return [((half, n), jnp.float32), ((half, n), jnp.bfloat16)]

    own, turned, own_square, kept, sent = kernel_call(
        own_kernel, [block, block, flat, *summands(rows + NORM)], smem=1, scratch=12
    )(order, z_anchor, mean)
    near_own = scatter(*halve(kept, sent, rows), last=rows)
    near_own = jnp.concatenate([near_own] + [to_partner(near_own, 2 * k) for k in (1, 2, 3)])
    end = lax.ppermute(after(z_anchor, beside_in, swapped, near_own), "dp", [(0, 3), (3, 0)])

    beside, beside_square, swapped, swapped_square, kept, sent = kernel_call(
        first_kernel, [block, flat, block, flat, *summands(rows)],
        smem=2, scratch=12, temps=[block],
    )(order, middle, after(turned, near_own), beside_in, swapped, mean)
    first = scatter(*halve(kept, sent))
    kept_early, sent_early = kernel_call(
        early_kernel, summands(2 * rows), smem=1, scratch=12
    )(middle, after(turned, first), beside, swapped)
    far_own = to_partner(near_own, 1)
    near = after(gather_chips(first), sent_early)
    ready = kernel_call(
        push_kernel, [block, block], smem=2, scratch=12, temps=[((rows, rows), jnp.bfloat16)]
    )(order, middle, near, to_partner(near, 1), beside, swapped, beside_square, swapped_square)
    out, over = ready
    pushed = [
        lax.ppermute(out, "dp", outward), lax.ppermute(after(over, end), "dp", across)
    ]

    end, end_square, kept, sent = kernel_call(
        late_kernel, [block, flat, summands(rows)[0], summands(2 * rows)[1]],
        smem=1, scratch=12, temps=[block], sems=4, outside=3,
    )(middle, after(turned, *ready), sent_early, end, mean)
    eighth = (rows // 8, 2 * rows)
    halved = kernel_call(
        add_either_kernel, [(eighth, jnp.float32)] + [(eighth, jnp.bfloat16)] * 3, smem=1
    )(middle, kept_early, kept, to_partner(sent, 1))
    result = ((rows, width), jnp.float32)
    held = kernel_call(
        functools.partial(held_kernel, total), [result],
        smem=2, scratch=12, temps=[((rows, rows + NORM), jnp.bfloat16)],
    )(
        order, middle, near_own, far_own, own, z_anchor, z_other,
        own_square, beside_square, swapped_square, after(end_square, halved[0]), mean, spread,
    )[0]
    got = [to_partner(x, 2 * k) for k, x in enumerate(halved[1:], 1)]
    second = kernel_call(total_either_kernel, [(eighth, jnp.bfloat16)], smem=1)(
        middle, first, halved[0], *got
    )[0]
    near = after(gather_chips(after(second, held)), pushed[0])
    return kernel_call(
        functools.partial(last_kernel, total), [result],
        smem=2, scratch=12, temps=[((rows, 2 * rows), jnp.bfloat16), result], sems=4, out=pl.ANY,
    )(
        order, middle, near, to_partner(near, 1), beside, swapped, end, held, *pushed
    )[0]


def by_gather(z_anchor, z_other):
    rows_here, width = z_anchor.shape
    groups = lax.axis_size("dp")
    total = rows_here * groups
    mine = lax.axis_index("dp") * rows_here
    column = lax.all_gather(z_anchor, "dp", axis=0, tiled=True).astype(jnp.float32)
    mean = jnp.sum(column, axis=0) / total
    centered_all = column - mean
    variance = jnp.sum(centered_all * centered_all, axis=0) / (total - 1)
    rounded_all = centered_all.astype(jnp.bfloat16)
    widened = rounded_all.astype(jnp.float32)
    own_square = jnp.sum(widened * widened, axis=0)
    rounded = lax.dynamic_slice_in_dim(rounded_all, mine, rows_here, 0)
    inner = lax.psum(gram(rounded, rounded_all).astype(jnp.bfloat16), "feat")
    product = jnp.dot(inner, rounded_all, preferred_element_type=jnp.float32)
    product = product - rounded.astype(jnp.float32) * own_square
    return finish(z_anchor, z_other, mean, variance, total, product)


def finish(z_anchor, z_other, mean, variance, total, product):
    coef = 2.0 * total / (25.0 * (total - 1)) / (total - 1)
    anchor = z_anchor.astype(jnp.float32)
    centered = anchor - mean
    deviation = jnp.sqrt(variance + 0.0001)
    hinge = jnp.where(deviation < 1.0, centered / deviation, 0.0)
    factor = total / (4.0 * (total - 1))
    return anchor - z_other.astype(jnp.float32) - factor * hinge + coef * product


def solution(mesh):
    placed = (P("dp", "feat"), P("dp", "feat"))
    in_line = mesh.shape["dp"] == 4 and mesh.shape["feat"] == 8
    return jax.shard_map(
        by_line if in_line else by_gather,
        mesh=mesh, in_specs=placed, out_specs=P("dp", "feat"), check_vma=False,
    )
```

```python
import functools
import math

import jax
import jax.numpy as jnp
from jax import lax
from jax.experimental import pallas as pl
from jax.experimental.pallas import tpu as pltpu
from jax.sharding import PartitionSpec as P

NORM = 128


def kernel_call(body, outs, smem=0, scratch=4, temps=(), sems=0, out=pltpu.VMEM, outside=None):
    def call(*args):
        space = [pltpu.SMEM] * smem + [pltpu.VMEM] * (len(args) - smem)
        if outside is not None:
            space[outside] = pl.ANY
        return pl.pallas_call(
            body,
            out_shape=[jax.ShapeDtypeStruct(s, t) for s, t in outs],
            in_specs=[pl.BlockSpec(memory_space=m) for m in space],
            out_specs=[pl.BlockSpec(memory_space=out) for _ in outs],
            scratch_shapes=[pltpu.VMEM(s, t) for s, t in temps]
            + ([pltpu.SemaphoreType.DMA((sems,))] if sems else []),
            compiler_params=pltpu.CompilerParams(vmem_limit_bytes=scratch * 1024 * 1024),
            cost_estimate=pl.CostEstimate(flops=0, bytes_accessed=0, transcendentals=0),
        )(*args)

    return call


def gram(left, right):
    return lax.dot_general(
        left, right, (((1,), (1,)), ((), ())), preferred_element_type=jnp.float32
    )


def dot_t(left, right):
    return lax.dot_general(
        left, right, (((0,), (0,)), ((), ())), preferred_element_type=jnp.float32
    )


def dot(left, right):
    return jnp.dot(left, right, preferred_element_type=jnp.float32)


def centered_into(out, block, mean, square):
    out[...] = (block[...].astype(jnp.float32) - mean).astype(jnp.bfloat16)
    wide = out[...].astype(jnp.float32)
    square[...] = jnp.sum(wide * wide, axis=0, keepdims=True)


def pieces_in(source, landed, sem):
    rows = landed.shape[0] // 4
    return [
        pltpu.make_async_copy(
            source.at[k * rows:(k + 1) * rows], landed.at[k * rows:(k + 1) * rows], sem.at[k]
        )
        for k in range(4)
    ]


def centered_pieces(out, copies, landed, mean, square):
    rows, total = landed.shape[0] // 4, 0.0
    for k, copy in enumerate(copies):
        copy.wait()
        here = slice(k * rows, (k + 1) * rows)
        block = (landed[here, :].astype(jnp.float32) - mean).astype(jnp.bfloat16)
        out[here, :] = block
        wide = block.astype(jnp.float32)
        total = total + jnp.sum(wide * wide, axis=0, keepdims=True)
    square[...] = total


def high_low(n, like):
    high = n.astype(jnp.bfloat16).astype(jnp.float32)
    lane = lax.broadcasted_iota(jnp.int32, like, 1)
    return jnp.where(lane == 0, high, jnp.where(lane == 1, n - high, 0.0))


def turn_into(turned, order, block):
    eighth = block.shape[0] // 8
    for k in range(8):
        start = pl.multiple_of(order[k] * eighth, eighth)
        turned[k * eighth:(k + 1) * eighth, :] = block[pl.ds(start, eighth), :]


def own_kernel(order, z, mean, own, turned, square, kept, sent):
    rows = z.shape[0]
    eighth, half = rows // 8, rows // 2
    centered_into(own, z, mean[...], square)
    turn_into(turned, order, own)
    inner = gram(turned[...], own[...])
    wide = turned[...].astype(jnp.float32)
    norm = jnp.sum(wide * wide, axis=1, keepdims=True)
    column = lax.broadcasted_iota(jnp.int32, (eighth, rows), 1)
    row = lax.broadcasted_iota(jnp.int32, (eighth, rows), 0)
    for k in range(8):
        here = slice(k * eighth, (k + 1) * eighth)
        off = jnp.where(column == row + order[k] * eighth, 0.0, inner[here])
        if k < 4:
            kept[here, :rows] = off
        else:
            sent[k * eighth - half:(k + 1) * eighth - half, :rows] = off.astype(jnp.bfloat16)
    lane = lax.broadcasted_iota(jnp.int32, (half, NORM), 1)
    kept[:, rows:] = jnp.where(lane == 0, norm[:half], 0.0)
    sent[:, rows:] = high_low(norm[half:], (half, NORM)).astype(jnp.bfloat16)


def split_sum(inner, kept, sent, here):
    half = kept.shape[0]
    kept[:, here] = inner[:half]
    sent[:, here] = inner[half:].astype(jnp.bfloat16)


def first_kernel(
    order, middle, turned, beside_in, opposite_in, mean,
    beside, beside_square, opposite, opposite_square, kept, sent, turned_beside,
):
    centered_into(beside, beside_in, mean[...], beside_square)

    @pl.when(middle[0] == 1)
    def _():
        centered_into(opposite, opposite_in, mean[...], opposite_square)
        turn_into(turned_beside, order, beside)
        split_sum(gram(turned_beside[...], opposite[...]), kept, sent, slice(None))

    @pl.when(middle[0] == 0)
    def _():
        split_sum(gram(turned[...], beside[...]), kept, sent, slice(None))


def early_kernel(middle, turned, beside, opposite, kept, sent):
    rows = beside.shape[0]

    @pl.when(middle[0] == 1)
    def _():
        split_sum(gram(turned[...], opposite[...]), kept, sent, slice(0, rows))
        split_sum(gram(turned[...], beside[...]), kept, sent, slice(rows, 2 * rows))


def late_kernel(
    middle, turned, sent_early, end_in, mean, end, square, kept, sent, landed, sem
):
    rows = end.shape[0]

    @pl.when(middle[0] == 1)
    def _():
        sent[...] = sent_early[...]

    @pl.when(middle[0] == 0)
    def _():
        copies = pieces_in(end_in, landed, sem)
        for copy in copies:
            copy.start()
        centered_pieces(end, copies, landed, mean[...], square)
        split_sum(gram(turned[...], end[...]), kept, sent, slice(0, rows))
        sent[:, rows:] = jnp.zeros_like(sent[:, rows:])


def stats_kernel(z, out):
    rows = z.shape[0]
    base = z[:16, :].astype(jnp.float32)[:1]
    apart = z[...].astype(jnp.float32) - base
    total = jnp.sum(apart, axis=0, keepdims=True)
    away = total / rows
    out[:1, :] = base + away
    out[1:, :] = jnp.sum(apart * apart, axis=0, keepdims=True) - total * away


def with_norm(x, last):
    if not last:
        return x
    tail = x[:, last:]
    split = high_low(jnp.sum(tail, axis=1, keepdims=True), tail.shape)
    return jnp.concatenate([x[:, :last], split], axis=1)


def add_kernel(last, kept, got, mine, *out):
    total = with_norm(kept[...] + got[...].astype(jnp.float32), last)
    quarter = mine.shape[0]
    mine[...] = total[:quarter]
    for k, ref in enumerate(out, 1):
        ref[...] = total[k * quarter:(k + 1) * quarter].astype(jnp.bfloat16)


def add_either_kernel(middle, kept_early, kept, got, mine, *out):
    quarter, rows = mine.shape[0], kept.shape[1]

    def put(total, here):
        mine[:, here] = total[:quarter]
        for k, ref in enumerate(out, 1):
            ref[:, here] = total[k * quarter:(k + 1) * quarter].astype(jnp.bfloat16)

    @pl.when(middle[0] == 1)
    def _():
        put(kept_early[...] + got[...].astype(jnp.float32), slice(None))

    @pl.when(middle[0] == 0)
    def _():
        put(kept[...] + got[:, :rows].astype(jnp.float32), slice(0, rows))
        put(jnp.zeros((4 * quarter, rows), jnp.float32), slice(rows, 2 * rows))


def total_kernel(last, mine, a, b, c, out):
    total = mine[...] + a[...].astype(jnp.float32)
    total = total + b[...].astype(jnp.float32) + c[...].astype(jnp.float32)
    out[...] = with_norm(total, last).astype(jnp.bfloat16)


def total_either_kernel(middle, first, mine, a, b, c, out):
    rows = first.shape[1]

    def put(here):
        total = mine[:, here] + a[:, here].astype(jnp.float32)
        total = total + b[:, here].astype(jnp.float32) + c[:, here].astype(jnp.float32)
        out[:, here] = total.astype(jnp.bfloat16)

    put(slice(0, rows))
    pl.when(middle[0] == 1)(lambda: put(slice(rows, 2 * rows)))

    @pl.when(middle[0] == 0)
    def _():
        out[:, rows:] = first[...]


def place_into(out, order, near, far):
    eighth = out.shape[0] // 8
    for k in range(4):
        here = slice(k * eighth, (k + 1) * eighth)
        out[pl.ds(pl.multiple_of(order[k] * eighth, eighth), eighth), :] = near[here, :]
        out[pl.ds(pl.multiple_of(order[4 + k] * eighth, eighth), eighth), :] = far[here, :]


def push_kernel(
    order, middle, near, far, beside, opposite, beside_square, opposite_square, out, over, inner
):
    width = beside.shape[1]

    @pl.when(middle[0] == 1)
    def _():
        place_into(inner, order, near, far)
        for k in range(2):
            here = slice(k * width // 2, (k + 1) * width // 2)
            outward = dot(inner[...], opposite[:, here])
            outward = outward - beside[:, here].astype(jnp.float32) * opposite_square[:, here]
            out[:, here] = outward.astype(jnp.bfloat16)
            across = dot_t(inner[...], beside[:, here])
            across = across - opposite[:, here].astype(jnp.float32) * beside_square[:, here]
            over[:, here] = across.astype(jnp.bfloat16)


def coefficient(total):
    return 2.0 * total / (25.0 * (total - 1)) / (total - 1)


def held_kernel(
    total, order, middle, near, far, own, z, other,
    own_square, beside_square, swapped_square, end_square, mean, spread, held, with_own,
):
    rows, width = own.shape
    place_into(with_own, order, near, far)
    norm = jnp.sum(with_own[:, rows:].astype(jnp.float32), axis=1, keepdims=True)
    for k in range(4):
        here = slice(k * width // 4, (k + 1) * width // 4)
        anchor = z[:, here].astype(jnp.float32)
        deviation = jnp.sqrt(spread[:, here] / (total - 1) + 0.0001)
        centered = anchor - mean[:, here]
        hinge = jnp.where(deviation < 1.0, centered / deviation, 0.0)
        plain = anchor - other[:, here].astype(jnp.float32) - total / (4.0 * (total - 1)) * hinge
        opposite = jnp.where(middle[0] == 1, swapped_square[:, here], end_square[:, here])
        square = own_square[:, here] + beside_square[:, here] + opposite
        product = dot(with_own[:, :rows], own[:, here])
        product = product + own[:, here].astype(jnp.float32) * (norm - square)
        held[:, here] = plain + coefficient(total) * product


def last_kernel(
    total, order, middle, near, far, beside, swapped, end, held, out, over, result, made, sem
):
    rows, width = beside.shape
    eighth = rows // 8

    def put(opposite, arrived):
        for k in range(4):
            here = slice(k * width // 4, (k + 1) * width // 4)
            for side, part in enumerate((near, far)):
                product = dot(part[:, rows:], beside[:, here])
                product = product + dot(part[:, :rows], opposite[:, here])
                for n in range(4):
                    start = pl.multiple_of(order[4 * side + n] * eighth, eighth)
                    to = pl.ds(start, eighth)
                    sums = product[n * eighth:(n + 1) * eighth] + arrived[to, here].astype(jnp.float32)
                    made[to, here] = held[to, here] + coefficient(total) * sums
            to_result(k).start()

    def to_result(k):
        here = slice(k * width // 4, (k + 1) * width // 4)
        return pltpu.make_async_copy(made.at[:, here], result.at[:, here], sem.at[k])

    pl.when(middle[0] == 1)(lambda: put(swapped, over))
    pl.when(middle[0] == 0)(lambda: put(end, out))
    for k in range(4):
        to_result(k).wait()


def to_partner(x, step):
    return lax.ppermute(x, "feat", [(i, i ^ step) for i in range(8)])


def halve(kept, sent, last=0):
    half, n = kept.shape
    part = (half // 4, n)
    return kernel_call(
        functools.partial(add_kernel, last), [(part, jnp.float32)] + [(part, jnp.bfloat16)] * 3
    )(kept, to_partner(sent, 1))


def scatter(mine, *out, last=0):
    got = [to_partner(x, 2 * k) for k, x in enumerate(out, 1)]
    return kernel_call(functools.partial(total_kernel, last), [(mine.shape, jnp.bfloat16)])(
        mine, *got
    )[0]


def pile_kernel(*refs):
    *pieces, out = refs
    rows = pieces[0].shape[0]
    for k, piece in enumerate(pieces):
        out[k * rows:(k + 1) * rows, :] = piece[...]


def gather_chips(x):
    pile = [((4 * x.shape[0], x.shape[1]), x.dtype)]
    return kernel_call(pile_kernel, pile)(x, *(to_partner(x, 2 * k) for k in (1, 2, 3)))[0]


def after(x, *others):
    return lax.optimization_barrier((x, *others))[0]


def by_line(z_anchor, z_other):
    rows, width = z_anchor.shape
    total = rows * 4
    plane = lax.axis_index("dp")
    middle = ((plane == 1) | (plane == 2)).astype(jnp.int32).reshape(1)
    order = lax.axis_index("feat") ^ jnp.array([0, 2, 4, 6, 1, 3, 5, 7], jnp.int32)
    across, outward = [(1, 2), (2, 1)], [(1, 0), (2, 3)]
    half = rows // 2
    flat, block = ((1, width), jnp.float32), ((rows, width), jnp.bfloat16)

    stats = kernel_call(stats_kernel, [((2, width), jnp.float32)], scratch=12)(z_anchor)[0]
    all_stats = [stats] + [
        lax.ppermute(stats, "dp", [(i, (i + k) % 4) for i in range(4)]) for k in (1, 2, 3)
    ]
    ahead = after(z_anchor, stats)
    beside_in = lax.ppermute(ahead, "dp", [(i, i ^ 1) for i in range(4)])
    swapped = lax.ppermute(ahead, "dp", across)
    mean = (all_stats[0][:1] + all_stats[1][:1] + all_stats[2][:1] + all_stats[3][:1]) / 4
    spread = 0.0
    for one in all_stats:
        shift = one[:1] - mean
        spread = spread + (one[1:] + rows * shift * shift)

    def summands(n):
        return [((half, n), jnp.float32), ((half, n), jnp.bfloat16)]

    own, turned, own_square, kept, sent = kernel_call(
        own_kernel, [block, block, flat, *summands(rows + NORM)], smem=1, scratch=12
    )(order, z_anchor, mean)
    near_own = scatter(*halve(kept, sent, rows), last=rows)
    near_own = jnp.concatenate([near_own] + [to_partner(near_own, 2 * k) for k in (1, 2, 3)])
    end = lax.ppermute(after(z_anchor, beside_in, swapped, near_own), "dp", [(0, 3), (3, 0)])

    beside, beside_square, swapped, swapped_square, kept, sent = kernel_call(
        first_kernel, [block, flat, block, flat, *summands(rows)],
        smem=2, scratch=12, temps=[block],
    )(order, middle, after(turned, near_own), beside_in, swapped, mean)
    first = scatter(*halve(kept, sent))
    kept_early, sent_early = kernel_call(
        early_kernel, summands(2 * rows), smem=1, scratch=12
    )(middle, after(turned, first), beside, swapped)
    far_own = to_partner(near_own, 1)
    near = after(gather_chips(first), sent_early)
    ready = kernel_call(
        push_kernel, [block, block], smem=2, scratch=12, temps=[((rows, rows), jnp.bfloat16)]
    )(order, middle, near, to_partner(near, 1), beside, swapped, beside_square, swapped_square)
    out, over = ready
    pushed = [
        lax.ppermute(out, "dp", outward), lax.ppermute(after(over, end), "dp", across)
    ]

    end, end_square, kept, sent = kernel_call(
        late_kernel, [block, flat, summands(rows)[0], summands(2 * rows)[1]],
        smem=1, scratch=12, temps=[block], sems=4, outside=3,
    )(middle, after(turned, *ready), sent_early, end, mean)
    eighth = (rows // 8, 2 * rows)
    halved = kernel_call(
        add_either_kernel, [(eighth, jnp.float32)] + [(eighth, jnp.bfloat16)] * 3, smem=1
    )(middle, kept_early, kept, to_partner(sent, 1))
    result = ((rows, width), jnp.float32)
    held = kernel_call(
        functools.partial(held_kernel, total), [result],
        smem=2, scratch=12, temps=[((rows, rows + NORM), jnp.bfloat16)],
    )(
        order, middle, near_own, far_own, own, z_anchor, z_other,
        own_square, beside_square, swapped_square, after(end_square, halved[0]), mean, spread,
    )[0]
    got = [to_partner(x, 2 * k) for k, x in enumerate(halved[1:], 1)]
    second = kernel_call(total_either_kernel, [(eighth, jnp.bfloat16)], smem=1)(
        middle, first, halved[0], *got
    )[0]
    near = after(gather_chips(after(second, held)), pushed[0])
    return kernel_call(
        functools.partial(last_kernel, total), [result],
        smem=2, scratch=12, temps=[result], sems=4, out=pl.ANY,
    )(
        order, middle, near, to_partner(near, 1), beside, swapped, end, held, *pushed
    )[0]


def by_gather(z_anchor, z_other):
    rows_here, width = z_anchor.shape
    groups = lax.axis_size("dp")
    total = rows_here * groups
    mine = lax.axis_index("dp") * rows_here
    column = lax.all_gather(z_anchor, "dp", axis=0, tiled=True).astype(jnp.float32)
    mean = jnp.sum(column, axis=0) / total
    centered_all = column - mean
    variance = jnp.sum(centered_all * centered_all, axis=0) / (total - 1)
    rounded_all = centered_all.astype(jnp.bfloat16)
    widened = rounded_all.astype(jnp.float32)
    own_square = jnp.sum(widened * widened, axis=0)
    rounded = lax.dynamic_slice_in_dim(rounded_all, mine, rows_here, 0)
    inner = lax.psum(gram(rounded, rounded_all).astype(jnp.bfloat16), "feat")
    product = jnp.dot(inner, rounded_all, preferred_element_type=jnp.float32)
    product = product - rounded.astype(jnp.float32) * own_square
    return finish(z_anchor, z_other, mean, variance, total, product)


def finish(z_anchor, z_other, mean, variance, total, product):
    coef = 2.0 * total / (25.0 * (total - 1)) / (total - 1)
    anchor = z_anchor.astype(jnp.float32)
    centered = anchor - mean
    deviation = jnp.sqrt(variance + 0.0001)
    hinge = jnp.where(deviation < 1.0, centered / deviation, 0.0)
    factor = total / (4.0 * (total - 1))
    return anchor - z_other.astype(jnp.float32) - factor * hinge + coef * product


def solution(mesh):
    placed = (P("dp", "feat"), P("dp", "feat"))
    in_line = mesh.shape["dp"] == 4 and mesh.shape["feat"] == 8
    return jax.shard_map(
        by_line if in_line else by_gather,
        mesh=mesh, in_specs=placed, out_specs=P("dp", "feat"), check_vma=False,
    )
```

```python
import functools
import math

import jax
import jax.numpy as jnp
from jax import lax
from jax.experimental import pallas as pl
from jax.experimental.pallas import tpu as pltpu
from jax.sharding import PartitionSpec as P

NORM = 128


def kernel_call(body, outs, smem=0, scratch=4, temps=(), sems=0, out=pltpu.VMEM, outside=None):
    def call(*args):
        space = [pltpu.SMEM] * smem + [pltpu.VMEM] * (len(args) - smem)
        if outside is not None:
            space[outside] = pl.ANY
        return pl.pallas_call(
            body,
            out_shape=[jax.ShapeDtypeStruct(s, t) for s, t in outs],
            in_specs=[pl.BlockSpec(memory_space=m) for m in space],
            out_specs=[pl.BlockSpec(memory_space=out) for _ in outs],
            scratch_shapes=[pltpu.VMEM(s, t) for s, t in temps]
            + ([pltpu.SemaphoreType.DMA((sems,))] if sems else []),
            compiler_params=pltpu.CompilerParams(vmem_limit_bytes=scratch * 1024 * 1024),
            cost_estimate=pl.CostEstimate(flops=0, bytes_accessed=0, transcendentals=0),
        )(*args)

    return call


def gram(left, right):
    return lax.dot_general(
        left, right, (((1,), (1,)), ((), ())), preferred_element_type=jnp.float32
    )


def dot_t(left, right):
    return lax.dot_general(
        left, right, (((0,), (0,)), ((), ())), preferred_element_type=jnp.float32
    )


def dot(left, right):
    return jnp.dot(left, right, preferred_element_type=jnp.float32)


def centered_into(out, block, mean, square):
    out[...] = (block[...].astype(jnp.float32) - mean).astype(jnp.bfloat16)
    wide = out[...].astype(jnp.float32)
    square[...] = jnp.sum(wide * wide, axis=0, keepdims=True)


def pieces_in(source, landed, sem):
    rows = landed.shape[0] // 4
    return [
        pltpu.make_async_copy(
            source.at[k * rows:(k + 1) * rows], landed.at[k * rows:(k + 1) * rows], sem.at[k]
        )
        for k in range(4)
    ]


def centered_pieces(out, copies, landed, mean, square):
    rows, total = landed.shape[0] // 4, 0.0
    for k, copy in enumerate(copies):
        copy.wait()
        here = slice(k * rows, (k + 1) * rows)
        block = (landed[here, :].astype(jnp.float32) - mean).astype(jnp.bfloat16)
        out[here, :] = block
        wide = block.astype(jnp.float32)
        total = total + jnp.sum(wide * wide, axis=0, keepdims=True)
    square[...] = total


def high_low(n, like):
    high = n.astype(jnp.bfloat16).astype(jnp.float32)
    lane = lax.broadcasted_iota(jnp.int32, like, 1)
    return jnp.where(lane == 0, high, jnp.where(lane == 1, n - high, 0.0))


def turn_into(turned, order, block):
    eighth = block.shape[0] // 8
    for k in range(8):
        start = pl.multiple_of(order[k] * eighth, eighth)
        turned[k * eighth:(k + 1) * eighth, :] = block[pl.ds(start, eighth), :]


def own_kernel(order, z, mean, own, turned, square, kept, sent):
    rows = z.shape[0]
    eighth, half = rows // 8, rows // 2
    centered_into(own, z, mean[...], square)
    turn_into(turned, order, own)
    inner = gram(turned[...], own[...])
    wide = turned[...].astype(jnp.float32)
    norm = jnp.sum(wide * wide, axis=1, keepdims=True)
    column = lax.broadcasted_iota(jnp.int32, (eighth, rows), 1)
    row = lax.broadcasted_iota(jnp.int32, (eighth, rows), 0)
    for k in range(8):
        here = slice(k * eighth, (k + 1) * eighth)
        off = jnp.where(column == row + order[k] * eighth, 0.0, inner[here])
        if k < 4:
            kept[here, :rows] = off
        else:
            sent[k * eighth - half:(k + 1) * eighth - half, :rows] = off.astype(jnp.bfloat16)
    lane = lax.broadcasted_iota(jnp.int32, (half, NORM), 1)
    kept[:, rows:] = jnp.where(lane == 0, norm[:half], 0.0)
    sent[:, rows:] = high_low(norm[half:], (half, NORM)).astype(jnp.bfloat16)


def split_sum(inner, kept, sent, here):
    half = kept.shape[0]
    kept[:, here] = inner[:half]
    sent[:, here] = inner[half:].astype(jnp.bfloat16)


def first_kernel(
    order, middle, turned, beside_in, opposite_in, mean,
    beside, beside_square, opposite, opposite_square, kept, sent, turned_beside,
):
    centered_into(beside, beside_in, mean[...], beside_square)

    @pl.when(middle[0] == 1)
    def _():
        centered_into(opposite, opposite_in, mean[...], opposite_square)
        turn_into(turned_beside, order, beside)
        split_sum(gram(turned_beside[...], opposite[...]), kept, sent, slice(None))

    @pl.when(middle[0] == 0)
    def _():
        split_sum(gram(turned[...], beside[...]), kept, sent, slice(None))


def early_kernel(middle, turned, beside, opposite, kept, sent):
    rows = beside.shape[0]

    @pl.when(middle[0] == 1)
    def _():
        split_sum(gram(turned[...], opposite[...]), kept, sent, slice(0, rows))
        split_sum(gram(turned[...], beside[...]), kept, sent, slice(rows, 2 * rows))


def late_kernel(
    middle, turned, sent_early, end_in, mean, end, square, kept, sent, landed, sem
):
    rows = end.shape[0]

    @pl.when(middle[0] == 1)
    def _():
        sent[...] = sent_early[...]

    @pl.when(middle[0] == 0)
    def _():
        copies = pieces_in(end_in, landed, sem)
        for copy in copies:
            copy.start()
        centered_pieces(end, copies, landed, mean[...], square)
        split_sum(gram(turned[...], end[...]), kept, sent, slice(0, rows))
        sent[:, rows:] = jnp.zeros_like(sent[:, rows:])


def stats_kernel(z, out, landed, sem):
    rows = landed.shape[0]
    copies = pieces_in(z, landed, sem)
    for copy in copies:
        copy.start()
    total, square = 0.0, 0.0
    for k, copy in enumerate(copies):
        copy.wait()
        if k == 0:
            base = landed[:16, :].astype(jnp.float32)[:1]
        piece = landed[k * rows // 4:(k + 1) * rows // 4, :]
        apart = piece.astype(jnp.float32) - base
        total = total + jnp.sum(apart, axis=0, keepdims=True)
        square = square + jnp.sum(apart * apart, axis=0, keepdims=True)
    away = total / rows
    out[:1, :] = base + away
    out[1:, :] = square - total * away


def with_norm(x, last):
    if not last:
        return x
    tail = x[:, last:]
    split = high_low(jnp.sum(tail, axis=1, keepdims=True), tail.shape)
    return jnp.concatenate([x[:, :last], split], axis=1)


def add_kernel(last, kept, got, mine, *out):
    total = with_norm(kept[...] + got[...].astype(jnp.float32), last)
    quarter = mine.shape[0]
    mine[...] = total[:quarter]
    for k, ref in enumerate(out, 1):
        ref[...] = total[k * quarter:(k + 1) * quarter].astype(jnp.bfloat16)


def add_either_kernel(middle, kept_early, kept, got, mine, *out):
    quarter, rows = mine.shape[0], kept.shape[1]

    def put(total, here):
        mine[:, here] = total[:quarter]
        for k, ref in enumerate(out, 1):
            ref[:, here] = total[k * quarter:(k + 1) * quarter].astype(jnp.bfloat16)

    @pl.when(middle[0] == 1)
    def _():
        put(kept_early[...] + got[...].astype(jnp.float32), slice(None))

    @pl.when(middle[0] == 0)
    def _():
        put(kept[...] + got[:, :rows].astype(jnp.float32), slice(0, rows))
        put(jnp.zeros((4 * quarter, rows), jnp.float32), slice(rows, 2 * rows))


def total_kernel(last, mine, a, b, c, out):
    total = mine[...] + a[...].astype(jnp.float32)
    total = total + b[...].astype(jnp.float32) + c[...].astype(jnp.float32)
    out[...] = with_norm(total, last).astype(jnp.bfloat16)


def total_either_kernel(middle, first, mine, a, b, c, out):
    rows = first.shape[1]

    def put(here):
        total = mine[:, here] + a[:, here].astype(jnp.float32)
        total = total + b[:, here].astype(jnp.float32) + c[:, here].astype(jnp.float32)
        out[:, here] = total.astype(jnp.bfloat16)

    put(slice(0, rows))
    pl.when(middle[0] == 1)(lambda: put(slice(rows, 2 * rows)))

    @pl.when(middle[0] == 0)
    def _():
        out[:, rows:] = first[...]


def place_into(out, order, near, far):
    eighth = out.shape[0] // 8
    for k in range(4):
        here = slice(k * eighth, (k + 1) * eighth)
        out[pl.ds(pl.multiple_of(order[k] * eighth, eighth), eighth), :] = near[here, :]
        out[pl.ds(pl.multiple_of(order[4 + k] * eighth, eighth), eighth), :] = far[here, :]


def push_kernel(
    order, middle, near, far, beside, opposite, beside_square, opposite_square, out, over, inner
):
    width = beside.shape[1]

    @pl.when(middle[0] == 1)
    def _():
        place_into(inner, order, near, far)
        for k in range(2):
            here = slice(k * width // 2, (k + 1) * width // 2)
            outward = dot(inner[...], opposite[:, here])
            outward = outward - beside[:, here].astype(jnp.float32) * opposite_square[:, here]
            out[:, here] = outward.astype(jnp.bfloat16)
            across = dot_t(inner[...], beside[:, here])
            across = across - opposite[:, here].astype(jnp.float32) * beside_square[:, here]
            over[:, here] = across.astype(jnp.bfloat16)


def coefficient(total):
    return 2.0 * total / (25.0 * (total - 1)) / (total - 1)


def held_kernel(
    total, order, middle, near, far, own, z, other,
    own_square, beside_square, swapped_square, end_square, mean, spread, held, with_own,
):
    rows, width = own.shape
    place_into(with_own, order, near, far)
    norm = jnp.sum(with_own[:, rows:].astype(jnp.float32), axis=1, keepdims=True)
    for k in range(4):
        here = slice(k * width // 4, (k + 1) * width // 4)
        anchor = z[:, here].astype(jnp.float32)
        deviation = jnp.sqrt(spread[:, here] / (total - 1) + 0.0001)
        centered = anchor - mean[:, here]
        hinge = jnp.where(deviation < 1.0, centered / deviation, 0.0)
        plain = anchor - other[:, here].astype(jnp.float32) - total / (4.0 * (total - 1)) * hinge
        opposite = jnp.where(middle[0] == 1, swapped_square[:, here], end_square[:, here])
        square = own_square[:, here] + beside_square[:, here] + opposite
        product = dot(with_own[:, :rows], own[:, here])
        product = product + own[:, here].astype(jnp.float32) * (norm - square)
        held[:, here] = plain + coefficient(total) * product


def last_kernel(
    total, order, middle, near, far, beside, swapped, end, held, out, over, result, second, made, sem
):
    rows, width = beside.shape
    place_into(second, order, near, far)

    def put(opposite, arrived):
        for k in range(4):
            here = slice(k * width // 4, (k + 1) * width // 4)
            product = dot(second[:, rows:], beside[:, here])
            product = product + dot(second[:, :rows], opposite[:, here])
            product = product + arrived[:, here].astype(jnp.float32)
            made[:, here] = held[:, here] + coefficient(total) * product
            to_result(k).start()

    def to_result(k):
        here = slice(k * width // 4, (k + 1) * width // 4)
        return pltpu.make_async_copy(made.at[:, here], result.at[:, here], sem.at[k])

    pl.when(middle[0] == 1)(lambda: put(swapped, over))
    pl.when(middle[0] == 0)(lambda: put(end, out))
    for k in range(4):
        to_result(k).wait()


def to_partner(x, step):
    return lax.ppermute(x, "feat", [(i, i ^ step) for i in range(8)])


def halve(kept, sent, last=0):
    half, n = kept.shape
    part = (half // 4, n)
    return kernel_call(
        functools.partial(add_kernel, last), [(part, jnp.float32)] + [(part, jnp.bfloat16)] * 3
    )(kept, to_partner(sent, 1))


def scatter(mine, *out, last=0):
    got = [to_partner(x, 2 * k) for k, x in enumerate(out, 1)]
    return kernel_call(functools.partial(total_kernel, last), [(mine.shape, jnp.bfloat16)])(
        mine, *got
    )[0]


def pile_kernel(*refs):
    *pieces, out = refs
    rows = pieces[0].shape[0]
    for k, piece in enumerate(pieces):
        out[k * rows:(k + 1) * rows, :] = piece[...]


def gather_chips(x):
    pile = [((4 * x.shape[0], x.shape[1]), x.dtype)]
    return kernel_call(pile_kernel, pile)(x, *(to_partner(x, 2 * k) for k in (1, 2, 3)))[0]


def after(x, *others):
    return lax.optimization_barrier((x, *others))[0]


def by_line(z_anchor, z_other):
    rows, width = z_anchor.shape
    total = rows * 4
    plane = lax.axis_index("dp")
    middle = ((plane == 1) | (plane == 2)).astype(jnp.int32).reshape(1)
    order = lax.axis_index("feat") ^ jnp.array([0, 2, 4, 6, 1, 3, 5, 7], jnp.int32)
    across, outward = [(1, 2), (2, 1)], [(1, 0), (2, 3)]
    half = rows // 2
    flat, block = ((1, width), jnp.float32), ((rows, width), jnp.bfloat16)

    stats = kernel_call(
        stats_kernel, [((2, width), jnp.float32)], scratch=12, temps=[block], sems=4, outside=0
    )(z_anchor)[0]
    all_stats = [stats] + [
        lax.ppermute(stats, "dp", [(i, (i + k) % 4) for i in range(4)]) for k in (1, 2, 3)
    ]
    ahead = after(z_anchor, stats)
    beside_in = lax.ppermute(ahead, "dp", [(i, i ^ 1) for i in range(4)])
    swapped = lax.ppermute(ahead, "dp", across)
    mean = (all_stats[0][:1] + all_stats[1][:1] + all_stats[2][:1] + all_stats[3][:1]) / 4
    spread = 0.0
    for one in all_stats:
        shift = one[:1] - mean
        spread = spread + (one[1:] + rows * shift * shift)

    def summands(n):
        return [((half, n), jnp.float32), ((half, n), jnp.bfloat16)]

    own, turned, own_square, kept, sent = kernel_call(
        own_kernel, [block, block, flat, *summands(rows + NORM)], smem=1, scratch=12
    )(order, z_anchor, mean)
    near_own = scatter(*halve(kept, sent, rows), last=rows)
    near_own = jnp.concatenate([near_own] + [to_partner(near_own, 2 * k) for k in (1, 2, 3)])
    end = lax.ppermute(after(z_anchor, beside_in, swapped, near_own), "dp", [(0, 3), (3, 0)])

    beside, beside_square, swapped, swapped_square, kept, sent = kernel_call(
        first_kernel, [block, flat, block, flat, *summands(rows)],
        smem=2, scratch=12, temps=[block],
    )(order, middle, after(turned, near_own), beside_in, swapped, mean)
    first = scatter(*halve(kept, sent))
    kept_early, sent_early = kernel_call(
        early_kernel, summands(2 * rows), smem=1, scratch=12
    )(middle, after(turned, first), beside, swapped)
    far_own = to_partner(near_own, 1)
    near = after(gather_chips(first), sent_early)
    ready = kernel_call(
        push_kernel, [block, block], smem=2, scratch=12, temps=[((rows, rows), jnp.bfloat16)]
    )(order, middle, near, to_partner(near, 1), beside, swapped, beside_square, swapped_square)
    out, over = ready
    pushed = [
        lax.ppermute(out, "dp", outward), lax.ppermute(after(over, end), "dp", across)
    ]

    end, end_square, kept, sent = kernel_call(
        late_kernel, [block, flat, summands(rows)[0], summands(2 * rows)[1]],
        smem=1, scratch=12, temps=[block], sems=4, outside=3,
    )(middle, after(turned, *ready), sent_early, end, mean)
    eighth = (rows // 8, 2 * rows)
    halved = kernel_call(
        add_either_kernel, [(eighth, jnp.float32)] + [(eighth, jnp.bfloat16)] * 3, smem=1
    )(middle, kept_early, kept, to_partner(sent, 1))
    result = ((rows, width), jnp.float32)
    held = kernel_call(
        functools.partial(held_kernel, total), [result],
        smem=2, scratch=12, temps=[((rows, rows + NORM), jnp.bfloat16)],
    )(
        order, middle, near_own, far_own, own, z_anchor, z_other,
        own_square, beside_square, swapped_square, after(end_square, halved[0]), mean, spread,
    )[0]
    got = [to_partner(x, 2 * k) for k, x in enumerate(halved[1:], 1)]
    second = kernel_call(total_either_kernel, [(eighth, jnp.bfloat16)], smem=1)(
        middle, first, halved[0], *got
    )[0]
    near = after(gather_chips(after(second, held)), pushed[0])
    return kernel_call(
        functools.partial(last_kernel, total), [result],
        smem=2, scratch=12, temps=[((rows, 2 * rows), jnp.bfloat16), result], sems=4, out=pl.ANY,
    )(
        order, middle, near, to_partner(near, 1), beside, swapped, end, held, *pushed
    )[0]


def by_gather(z_anchor, z_other):
    rows_here, width = z_anchor.shape
    groups = lax.axis_size("dp")
    total = rows_here * groups
    mine = lax.axis_index("dp") * rows_here
    column = lax.all_gather(z_anchor, "dp", axis=0, tiled=True).astype(jnp.float32)
    mean = jnp.sum(column, axis=0) / total
    centered_all = column - mean
    variance = jnp.sum(centered_all * centered_all, axis=0) / (total - 1)
    rounded_all = centered_all.astype(jnp.bfloat16)
    widened = rounded_all.astype(jnp.float32)
    own_square = jnp.sum(widened * widened, axis=0)
    rounded = lax.dynamic_slice_in_dim(rounded_all, mine, rows_here, 0)
    inner = lax.psum(gram(rounded, rounded_all).astype(jnp.bfloat16), "feat")
    product = jnp.dot(inner, rounded_all, preferred_element_type=jnp.float32)
    product = product - rounded.astype(jnp.float32) * own_square
    return finish(z_anchor, z_other, mean, variance, total, product)


def finish(z_anchor, z_other, mean, variance, total, product):
    coef = 2.0 * total / (25.0 * (total - 1)) / (total - 1)
    anchor = z_anchor.astype(jnp.float32)
    centered = anchor - mean
    deviation = jnp.sqrt(variance + 0.0001)
    hinge = jnp.where(deviation < 1.0, centered / deviation, 0.0)
    factor = total / (4.0 * (total - 1))
    return anchor - z_other.astype(jnp.float32) - factor * hinge + coef * product


def solution(mesh):
    placed = (P("dp", "feat"), P("dp", "feat"))
    in_line = mesh.shape["dp"] == 4 and mesh.shape["feat"] == 8
    return jax.shard_map(
        by_line if in_line else by_gather,
        mesh=mesh, in_specs=placed, out_specs=P("dp", "feat"), check_vma=False,
    )
```

```python
import functools
import math

import jax
import jax.numpy as jnp
from jax import lax
from jax.experimental import pallas as pl
from jax.experimental.pallas import tpu as pltpu
from jax.sharding import PartitionSpec as P

NORM = 128


def kernel_call(body, outs, smem=0, scratch=4, temps=(), sems=0, out=pltpu.VMEM, outside=None):
    def call(*args):
        space = [pltpu.SMEM] * smem + [pltpu.VMEM] * (len(args) - smem)
        if outside is not None:
            space[outside] = pl.ANY
        return pl.pallas_call(
            body,
            out_shape=[jax.ShapeDtypeStruct(s, t) for s, t in outs],
            in_specs=[pl.BlockSpec(memory_space=m) for m in space],
            out_specs=[pl.BlockSpec(memory_space=out) for _ in outs],
            scratch_shapes=[pltpu.VMEM(s, t) for s, t in temps]
            + ([pltpu.SemaphoreType.DMA((sems,))] if sems else []),
            compiler_params=pltpu.CompilerParams(vmem_limit_bytes=scratch * 1024 * 1024),
            cost_estimate=pl.CostEstimate(flops=0, bytes_accessed=0, transcendentals=0),
        )(*args)

    return call


def gram(left, right):
    return lax.dot_general(
        left, right, (((1,), (1,)), ((), ())), preferred_element_type=jnp.float32
    )


def dot_t(left, right):
    return lax.dot_general(
        left, right, (((0,), (0,)), ((), ())), preferred_element_type=jnp.float32
    )


def dot(left, right):
    return jnp.dot(left, right, preferred_element_type=jnp.float32)


def centered_into(out, block, mean, square):
    out[...] = (block[...].astype(jnp.float32) - mean).astype(jnp.bfloat16)
    wide = out[...].astype(jnp.float32)
    square[...] = jnp.sum(wide * wide, axis=0, keepdims=True)


def pieces_in(source, landed, sem):
    rows = landed.shape[0] // 4
    return [
        pltpu.make_async_copy(
            source.at[k * rows:(k + 1) * rows], landed.at[k * rows:(k + 1) * rows], sem.at[k]
        )
        for k in range(4)
    ]


def centered_pieces(out, copies, landed, mean, square):
    rows, total = landed.shape[0] // 4, 0.0
    for k, copy in enumerate(copies):
        copy.wait()
        here = slice(k * rows, (k + 1) * rows)
        block = (landed[here, :].astype(jnp.float32) - mean).astype(jnp.bfloat16)
        out[here, :] = block
        wide = block.astype(jnp.float32)
        total = total + jnp.sum(wide * wide, axis=0, keepdims=True)
    square[...] = total


def high_low(n, like):
    high = n.astype(jnp.bfloat16).astype(jnp.float32)
    lane = lax.broadcasted_iota(jnp.int32, like, 1)
    return jnp.where(lane == 0, high, jnp.where(lane == 1, n - high, 0.0))


def turn_into(turned, order, block):
    eighth = block.shape[0] // 8
    for k in range(8):
        start = pl.multiple_of(order[k] * eighth, eighth)
        turned[k * eighth:(k + 1) * eighth, :] = block[pl.ds(start, eighth), :]


def own_kernel(order, z, mean, own, turned, square, kept, sent):
    rows = z.shape[0]
    eighth, half = rows // 8, rows // 2
    centered_into(own, z, mean[...], square)
    turn_into(turned, order, own)
    inner = gram(turned[...], own[...])
    wide = turned[...].astype(jnp.float32)
    norm = jnp.sum(wide * wide, axis=1, keepdims=True)
    column = lax.broadcasted_iota(jnp.int32, (eighth, rows), 1)
    row = lax.broadcasted_iota(jnp.int32, (eighth, rows), 0)
    for k in range(8):
        here = slice(k * eighth, (k + 1) * eighth)
        off = jnp.where(column == row + order[k] * eighth, 0.0, inner[here])
        if k < 4:
            kept[here, :rows] = off
        else:
            sent[k * eighth - half:(k + 1) * eighth - half, :rows] = off.astype(jnp.bfloat16)
    lane = lax.broadcasted_iota(jnp.int32, (half, NORM), 1)
    kept[:, rows:] = jnp.where(lane == 0, norm[:half], 0.0)
    sent[:, rows:] = high_low(norm[half:], (half, NORM)).astype(jnp.bfloat16)


def split_sum(inner, kept, sent, here):
    half = kept.shape[0]
    kept[:, here] = inner[:half]
    sent[:, here] = inner[half:].astype(jnp.bfloat16)


def first_kernel(
    order, middle, turned, beside_in, opposite_in, mean,
    beside, beside_square, opposite, opposite_square, kept, sent, turned_beside,
):
    centered_into(beside, beside_in, mean[...], beside_square)

    @pl.when(middle[0] == 1)
    def _():
        centered_into(opposite, opposite_in, mean[...], opposite_square)
        turn_into(turned_beside, order, beside)
        split_sum(gram(turned_beside[...], opposite[...]), kept, sent, slice(None))

    @pl.when(middle[0] == 0)
    def _():
        split_sum(gram(turned[...], beside[...]), kept, sent, slice(None))


def early_kernel(middle, turned, beside, opposite, kept, sent):
    rows = beside.shape[0]

    @pl.when(middle[0] == 1)
    def _():
        split_sum(gram(turned[...], opposite[...]), kept, sent, slice(0, rows))
        split_sum(gram(turned[...], beside[...]), kept, sent, slice(rows, 2 * rows))


def late_kernel(
    middle, turned, sent_early, end_in, mean, end, square, kept, sent, landed, sem
):
    rows = end.shape[0]

    @pl.when(middle[0] == 1)
    def _():
        sent[...] = sent_early[...]

    @pl.when(middle[0] == 0)
    def _():
        copies = pieces_in(end_in, landed, sem)
        for copy in copies:
            copy.start()
        centered_pieces(end, copies, landed, mean[...], square)
        split_sum(gram(turned[...], end[...]), kept, sent, slice(0, rows))
        sent[:, rows:] = jnp.zeros_like(sent[:, rows:])


def stats_kernel(z, out, landed, sem):
    rows = landed.shape[0]
    copies = pieces_in(z, landed, sem)
    for copy in copies:
        copy.start()
    total, square = 0.0, 0.0
    for k, copy in enumerate(copies):
        copy.wait()
        if k == 0:
            base = landed[:16, :].astype(jnp.float32)[:1]
        piece = landed[k * rows // 4:(k + 1) * rows // 4, :]
        apart = piece.astype(jnp.float32) - base
        total = total + jnp.sum(apart, axis=0, keepdims=True)
        square = square + jnp.sum(apart * apart, axis=0, keepdims=True)
    away = total / rows
    out[:1, :] = base + away
    out[1:, :] = square - total * away


def with_norm(x, last):
    if not last:
        return x
    tail = x[:, last:]
    split = high_low(jnp.sum(tail, axis=1, keepdims=True), tail.shape)
    return jnp.concatenate([x[:, :last], split], axis=1)


def add_kernel(last, kept, got, mine, *out):
    total = with_norm(kept[...] + got[...].astype(jnp.float32), last)
    quarter = mine.shape[0]
    mine[...] = total[:quarter]
    for k, ref in enumerate(out, 1):
        ref[...] = total[k * quarter:(k + 1) * quarter].astype(jnp.bfloat16)


def add_either_kernel(middle, kept_early, kept, got, mine, *out):
    quarter, rows = mine.shape[0], kept.shape[1]

    def put(total, here):
        mine[:, here] = total[:quarter]
        for k, ref in enumerate(out, 1):
            ref[:, here] = total[k * quarter:(k + 1) * quarter].astype(jnp.bfloat16)

    @pl.when(middle[0] == 1)
    def _():
        put(kept_early[...] + got[...].astype(jnp.float32), slice(None))

    @pl.when(middle[0] == 0)
    def _():
        put(kept[...] + got[:, :rows].astype(jnp.float32), slice(0, rows))
        put(jnp.zeros((4 * quarter, rows), jnp.float32), slice(rows, 2 * rows))


def total_kernel(last, mine, a, b, c, out):
    total = mine[...] + a[...].astype(jnp.float32)
    total = total + b[...].astype(jnp.float32) + c[...].astype(jnp.float32)
    out[...] = with_norm(total, last).astype(jnp.bfloat16)


def total_either_kernel(middle, first, mine, a, b, c, out):
    rows = first.shape[1]

    def put(here):
        total = mine[:, here] + a[:, here].astype(jnp.float32)
        total = total + b[:, here].astype(jnp.float32) + c[:, here].astype(jnp.float32)
        out[:, here] = total.astype(jnp.bfloat16)

    put(slice(0, rows))
    pl.when(middle[0] == 1)(lambda: put(slice(rows, 2 * rows)))

    @pl.when(middle[0] == 0)
    def _():
        out[:, rows:] = first[...]


def place_into(out, order, near, far):
    eighth = out.shape[0] // 8
    for k in range(4):
        here = slice(k * eighth, (k + 1) * eighth)
        out[pl.ds(pl.multiple_of(order[k] * eighth, eighth), eighth), :] = near[here, :]
        out[pl.ds(pl.multiple_of(order[4 + k] * eighth, eighth), eighth), :] = far[here, :]


def push_kernel(
    order, middle, near, far, beside, opposite, beside_square, opposite_square, out, over, inner
):
    width = beside.shape[1]

    @pl.when(middle[0] == 1)
    def _():
        place_into(inner, order, near, far)
        for k in range(2):
            here = slice(k * width // 2, (k + 1) * width // 2)
            outward = dot(inner[...], opposite[:, here])
            outward = outward - beside[:, here].astype(jnp.float32) * opposite_square[:, here]
            out[:, here] = outward.astype(jnp.bfloat16)
            across = dot_t(inner[...], beside[:, here])
            across = across - opposite[:, here].astype(jnp.float32) * beside_square[:, here]
            over[:, here] = across.astype(jnp.bfloat16)


def coefficient(total):
    return 2.0 * total / (25.0 * (total - 1)) / (total - 1)


def held_kernel(
    total, order, middle, near, far, own, z, other,
    own_square, beside_square, swapped_square, end_square, mean, spread, held, with_own,
):
    rows, width = own.shape
    place_into(with_own, order, near, far)
    norm = jnp.sum(with_own[:, rows:].astype(jnp.float32), axis=1, keepdims=True)
    for k in range(4):
        here = slice(k * width // 4, (k + 1) * width // 4)
        anchor = z[:, here].astype(jnp.float32)
        deviation = jnp.sqrt(spread[:, here] / (total - 1) + 0.0001)
        centered = anchor - mean[:, here]
        hinge = jnp.where(deviation < 1.0, centered / deviation, 0.0)
        plain = anchor - other[:, here].astype(jnp.float32) - total / (4.0 * (total - 1)) * hinge
        opposite = jnp.where(middle[0] == 1, swapped_square[:, here], end_square[:, here])
        square = own_square[:, here] + beside_square[:, here] + opposite
        product = dot(with_own[:, :rows], own[:, here])
        product = product + own[:, here].astype(jnp.float32) * (norm - square)
        held[:, here] = plain + coefficient(total) * product


def last_kernel(
    total, order, middle, near, far, beside, swapped, end, held, out, over, result, second, made, sem
):
    rows, width = beside.shape
    place_into(second, order, near, far)

    def put(opposite, arrived):
        for k in range(4):
            here = slice(k * width // 4, (k + 1) * width // 4)
            product = dot(second[:, rows:], beside[:, here])
            product = product + dot(second[:, :rows], opposite[:, here])
            product = product + arrived[:, here].astype(jnp.float32)
            made[:, here] = held[:, here] + coefficient(total) * product
            to_result(k).start()

    def to_result(k):
        here = slice(k * width // 4, (k + 1) * width // 4)
        return pltpu.make_async_copy(made.at[:, here], result.at[:, here], sem.at[k])

    pl.when(middle[0] == 1)(lambda: put(swapped, over))
    pl.when(middle[0] == 0)(lambda: put(end, out))
    for k in range(4):
        to_result(k).wait()


def to_partner(x, step):
    return lax.ppermute(x, "feat", [(i, i ^ step) for i in range(8)])


def halve(kept, sent, last=0):
    half, n = kept.shape
    part = (half // 4, n)
    return kernel_call(
        functools.partial(add_kernel, last), [(part, jnp.float32)] + [(part, jnp.bfloat16)] * 3
    )(kept, to_partner(sent, 1))


def scatter(mine, *out, last=0):
    got = [to_partner(x, 2 * k) for k, x in enumerate(out, 1)]
    return kernel_call(functools.partial(total_kernel, last), [(mine.shape, jnp.bfloat16)])(
        mine, *got
    )[0]


def pile_kernel(*refs):
    *pieces, out = refs
    rows = pieces[0].shape[0]
    for k, piece in enumerate(pieces):
        out[k * rows:(k + 1) * rows, :] = piece[...]


def gather_chips(x):
    pile = [((4 * x.shape[0], x.shape[1]), x.dtype)]
    return kernel_call(pile_kernel, pile)(x, *(to_partner(x, 2 * k) for k in (1, 2, 3)))[0]


def after(x, *others):
    return lax.optimization_barrier((x, *others))[0]


def by_line(z_anchor, z_other):
    rows, width = z_anchor.shape
    total = rows * 4
    plane = lax.axis_index("dp")
    middle = ((plane == 1) | (plane == 2)).astype(jnp.int32).reshape(1)
    order = lax.axis_index("feat") ^ jnp.array([0, 2, 4, 6, 1, 3, 5, 7], jnp.int32)
    across, outward = [(1, 2), (2, 1)], [(1, 0), (2, 3)]
    half = rows // 2
    flat, block = ((1, width), jnp.float32), ((rows, width), jnp.bfloat16)

    stats = kernel_call(
        stats_kernel, [((2, width), jnp.float32)], scratch=8, temps=[block], sems=4, outside=0
    )(z_anchor)[0]
    all_stats = [stats] + [
        lax.ppermute(stats, "dp", [(i, (i + k) % 4) for i in range(4)]) for k in (1, 2, 3)
    ]
    ahead = after(z_anchor, stats)
    beside_in = lax.ppermute(ahead, "dp", [(i, i ^ 1) for i in range(4)])
    swapped = lax.ppermute(ahead, "dp", across)
    mean = (all_stats[0][:1] + all_stats[1][:1] + all_stats[2][:1] + all_stats[3][:1]) / 4
    spread = 0.0
    for one in all_stats:
        shift = one[:1] - mean
        spread = spread + (one[1:] + rows * shift * shift)

    def summands(n):
        return [((half, n), jnp.float32), ((half, n), jnp.bfloat16)]

    own, turned, own_square, kept, sent = kernel_call(
        own_kernel, [block, block, flat, *summands(rows + NORM)], smem=1, scratch=8
    )(order, z_anchor, mean)
    near_own = scatter(*halve(kept, sent, rows), last=rows)
    near_own = jnp.concatenate([near_own] + [to_partner(near_own, 2 * k) for k in (1, 2, 3)])
    end = lax.ppermute(after(z_anchor, beside_in, swapped, near_own), "dp", [(0, 3), (3, 0)])

    beside, beside_square, swapped, swapped_square, kept, sent = kernel_call(
        first_kernel, [block, flat, block, flat, *summands(rows)],
        smem=2, scratch=8, temps=[block],
    )(order, middle, after(turned, near_own), beside_in, swapped, mean)
    first = scatter(*halve(kept, sent))
    kept_early, sent_early = kernel_call(
        early_kernel, summands(2 * rows), smem=1, scratch=8
    )(middle, after(turned, first), beside, swapped)
    far_own = to_partner(near_own, 1)
    near = after(gather_chips(first), sent_early)
    ready = kernel_call(
        push_kernel, [block, block], smem=2, scratch=8, temps=[((rows, rows), jnp.bfloat16)]
    )(order, middle, near, to_partner(near, 1), beside, swapped, beside_square, swapped_square)
    out, over = ready
    pushed = [
        lax.ppermute(out, "dp", outward), lax.ppermute(after(over, end), "dp", across)
    ]

    end, end_square, kept, sent = kernel_call(
        late_kernel, [block, flat, summands(rows)[0], summands(2 * rows)[1]],
        smem=1, scratch=8, temps=[block], sems=4, outside=3,
    )(middle, after(turned, *ready), sent_early, end, mean)
    eighth = (rows // 8, 2 * rows)
    halved = kernel_call(
        add_either_kernel, [(eighth, jnp.float32)] + [(eighth, jnp.bfloat16)] * 3, smem=1
    )(middle, kept_early, kept, to_partner(sent, 1))
    result = ((rows, width), jnp.float32)
    held = kernel_call(
        functools.partial(held_kernel, total), [result],
        smem=2, scratch=8, temps=[((rows, rows + NORM), jnp.bfloat16)],
    )(
        order, middle, near_own, far_own, own, z_anchor, z_other,
        own_square, beside_square, swapped_square, after(end_square, halved[0]), mean, spread,
    )[0]
    got = [to_partner(x, 2 * k) for k, x in enumerate(halved[1:], 1)]
    second = kernel_call(total_either_kernel, [(eighth, jnp.bfloat16)], smem=1)(
        middle, first, halved[0], *got
    )[0]
    near = after(gather_chips(after(second, held)), pushed[0])
    return kernel_call(
        functools.partial(last_kernel, total), [result],
        smem=2, scratch=8, temps=[((rows, 2 * rows), jnp.bfloat16), result], sems=4, out=pl.ANY,
    )(
        order, middle, near, to_partner(near, 1), beside, swapped, end, held, *pushed
    )[0]


def by_gather(z_anchor, z_other):
    rows_here, width = z_anchor.shape
    groups = lax.axis_size("dp")
    total = rows_here * groups
    mine = lax.axis_index("dp") * rows_here
    column = lax.all_gather(z_anchor, "dp", axis=0, tiled=True).astype(jnp.float32)
    mean = jnp.sum(column, axis=0) / total
    centered_all = column - mean
    variance = jnp.sum(centered_all * centered_all, axis=0) / (total - 1)
    rounded_all = centered_all.astype(jnp.bfloat16)
    widened = rounded_all.astype(jnp.float32)
    own_square = jnp.sum(widened * widened, axis=0)
    rounded = lax.dynamic_slice_in_dim(rounded_all, mine, rows_here, 0)
    inner = lax.psum(gram(rounded, rounded_all).astype(jnp.bfloat16), "feat")
    product = jnp.dot(inner, rounded_all, preferred_element_type=jnp.float32)
    product = product - rounded.astype(jnp.float32) * own_square
    return finish(z_anchor, z_other, mean, variance, total, product)


def finish(z_anchor, z_other, mean, variance, total, product):
    coef = 2.0 * total / (25.0 * (total - 1)) / (total - 1)
    anchor = z_anchor.astype(jnp.float32)
    centered = anchor - mean
    deviation = jnp.sqrt(variance + 0.0001)
    hinge = jnp.where(deviation < 1.0, centered / deviation, 0.0)
    factor = total / (4.0 * (total - 1))
    return anchor - z_other.astype(jnp.float32) - factor * hinge + coef * product


def solution(mesh):
    placed = (P("dp", "feat"), P("dp", "feat"))
    in_line = mesh.shape["dp"] == 4 and mesh.shape["feat"] == 8
    return jax.shard_map(
        by_line if in_line else by_gather,
        mesh=mesh, in_specs=placed, out_specs=P("dp", "feat"), check_vma=False,
    )
```
